256 devices in a mesh: patch: 16 (over y_lo, z), tensor: 8 (over x, core), guide: 2 (over y_hi).
Axes of the slice: x: 4, y: 4 (y_hi: 2, y_lo: 2; y = y_hi * 2 + y_lo), z: 8, core: 2. Of those that a mesh axis runs over, the one named last changes fastest.
Arguments:
- query: bfloat16 [2, 8192, 5120], P('guide', 'patch', 'tensor'), may hold values from -6 to 6
- key_fresh: bfloat16 [2, 8192, 5120], P('guide', 'patch', 'tensor'), may hold values from -6 to 6
- value_fresh: bfloat16 [2, 8192, 5120], P('guide', 'patch', 'tensor'), may hold values from -6 to 6
- key_stale: bfloat16 [2, 8192, 5120], P('guide', 'patch', 'tensor'), may hold values from -6 to 6
- value_stale: bfloat16 [2, 8192, 5120], P('guide', 'patch', 'tensor'), may hold values from -6 to 6
- out_weight: bfloat16 [5120, 5120], P('tensor'), may hold values from -0.078125 to 0.078125
- stream: bfloat16 [2, 8192, 5120], P('guide', 'patch', 'tensor'), may hold values from -3 to 3
- gate_table: float32 [50, 5120], P(None, 'tensor'), may hold values from 0.5 to 1.5
- step_index: int32 [1], replicated, may hold values from 0 to 49
Outputs:
- guided: bfloat16 [8192, 5120], P('patch', ('tensor', 'guide'))
The draws below stay inside these ranges and needn't reach their ends.
All inputs are finite; a program needn't handle non-finite values.
Results may differ from the reference program's by a relative error of at most 0.012.
Values may be sent and summed in bfloat16 or wider, within the bound.
No kernel may reach another device: no remote copies, remote signals or barrier semaphores. Data moves between devices by JAX's collectives and lax.ppermute only.
A program may use at most 128 MiB of HBM per device.

```python
import jax
import jax.numpy as jnp
from jax import lax

D = 5120
HEADS = 40
HEAD_DIM = 128
TOK_DEV = 512
STEPS = 50
TOKENS = 8192
N_PATCH = 16


def drawn_values(key):
    values = 1.6 * jax.random.normal(key, (2, TOKENS, HEADS * HEAD_DIM), jnp.float32)
    return jnp.clip(values, -6.0, 6.0)


def draw_query(key, part):
    key = jax.random.fold_in(key, 3)
    values = drawn_values(key)
    return values.astype(jnp.bfloat16)


def draw_key_fresh(key, part):
    key = jax.random.fold_in(key, 5)
    values = drawn_values(key)
    return values.astype(jnp.bfloat16)


def draw_key_stale(key, part):
    key = jax.random.fold_in(key, 7)
    values = drawn_values(key)
    return values.astype(jnp.bfloat16)


def steps_of(key, dims, shards, low, high):
    factor_of = 1.0
    for position, shards_of in shards:
        heights = jax.random.uniform(jax.random.fold_in(jax.random.fold_in(key, 6), position), (shards_of,), jnp.float32, low / len(shards), high / len(shards))
        factor_of = factor_of * jnp.repeat(jnp.exp(heights), dims[position] // shards_of).reshape((-1,) + (1,) * (len(dims) - 1 - position))
    return factor_of


def bell_draw(key, dims, scale, most, shards=(), held_as=jnp.bfloat16):
    level = steps_of(key, dims, shards, -0.22, 0.18) if shards else 1.0
    result = jax.random.normal(key, dims, jnp.float32) * scale * level
    return jnp.minimum(jnp.maximum(result, -most), most).astype(held_as)


def setup_inputs(seed: int = 0) -> dict:
    key_list = jax.random.split(jax.random.key(seed), 10)
    query = draw_query(jax.random.fold_in(key_list[9], 71), 0)
    key_fresh = draw_key_fresh(jax.random.fold_in(key_list[9], 71), 0)
    value_fresh = bell_draw(key_list[2], (2, TOKENS, HEADS * HEAD_DIM), 1.0, 6.0, ((0, 2), (1, 16), (2, 8)))
    key_stale = draw_key_stale(jax.random.fold_in(key_list[9], 71), 0)
    value_stale = bell_draw(key_list[4], (2, TOKENS, HEADS * HEAD_DIM), 1.0, 6.0, ((0, 2), (1, 16), (2, 8)))
    out_weight = bell_draw(key_list[5], (HEADS * HEAD_DIM, D), (HEADS * HEAD_DIM) ** -0.5, 0.078125, ((0, 8),))
    stream = bell_draw(key_list[6], (2, TOKENS, D), 0.5, 3.0, ((0, 2), (1, 16), (2, 8)))
    gate_table = jnp.clip(0.5 + 1.0 * jax.random.uniform(key_list[7], (STEPS, D), jnp.float32) ** steps_of(key_list[7], (STEPS, D), ((1, 8),), -0.2, 0.2), 0.5, 1.5)
    step_index = jax.random.randint(key_list[8], (1,), 0, STEPS).astype(jnp.int32)
    return dict(query=query, key_fresh=key_fresh, value_fresh=value_fresh, key_stale=key_stale, value_stale=value_stale, out_weight=out_weight, stream=stream, gate_table=gate_table, step_index=step_index)


guide_scale = 5.0


def reference(query, key_fresh, value_fresh, key_stale, value_stale, out_weight, stream, gate_table, step_index):
    width = HEADS * HEAD_DIM
    factor = HEAD_DIM ** -0.5

    def attend(index):
        branch = index // N_PATCH
        patch_id = index % N_PATCH
        start = (patch_id * TOK_DEV).astype(jnp.int32)
        zero = jnp.zeros((), jnp.int32)
        queries = lax.dynamic_slice(query, (branch, start, zero), (1, TOK_DEV, width))[0]
        new_keys = lax.dynamic_slice(key_fresh, (branch, start, zero), (1, TOK_DEV, width))[0]
        new_values = lax.dynamic_slice(value_fresh, (branch, start, zero), (1, TOK_DEV, width))[0]
        old_keys = lax.dynamic_index_in_dim(key_stale, branch, 0, keepdims=False)
        old_values = lax.dynamic_index_in_dim(value_stale, branch, 0, keepdims=False)
        all_keys = lax.dynamic_update_slice(old_keys, new_keys, (start, zero))
        all_values = lax.dynamic_update_slice(old_values, new_values, (start, zero))
        qhead = queries.astype(jnp.float32).reshape(TOK_DEV, HEADS, HEAD_DIM)
        khead = all_keys.astype(jnp.float32).reshape(TOKENS, HEADS, HEAD_DIM)
        vhead = all_values.astype(jnp.float32).reshape(TOKENS, HEADS, HEAD_DIM)
        score = jnp.einsum("qhd,khd->hqk", qhead, khead) * factor
        peak = jnp.max(score, axis=-1, keepdims=True)
        weights = jnp.exp(score - peak).astype(jnp.bfloat16).astype(jnp.float32)
        total = jnp.sum(weights, axis=-1)
        summed = jnp.einsum("hqk,khd->qhd", weights, vhead)
        attended = summed / jnp.transpose(total)[:, :, None]
        return attended.reshape(TOK_DEV, width).astype(jnp.bfloat16)

    pieces = lax.map(attend, jnp.arange(2 * N_PATCH, dtype=jnp.int32))
    attended = pieces.reshape(2, TOKENS, width)
    gate = gate_table[step_index[0]]
    blocks = []
    for branch in range(2):
        term = jnp.dot(attended[branch], out_weight, preferred_element_type=jnp.float32)
        blocks.append(stream[branch].astype(jnp.float32) + gate[None, :] * term)
    guided = blocks[1] + guide_scale * (blocks[0] - blocks[1])
    return guided.astype(jnp.bfloat16)
```

```python
import functools

import jax
import jax.numpy as jnp
from jax import lax
from jax.experimental import pallas as pl
from jax.experimental.pallas import tpu as pltpu
from jax.sharding import PartitionSpec as P

HEAD_DIM = 128
SLOTS = 4
RING = 8
ROWS = 512
BLOCK = ROWS + 16
SCALE2 = 1.4426950408889634 / HEAD_DIM**0.5
SAFE_SUM = 2.0**100
VMEM = pl.BlockSpec(memory_space=pltpu.VMEM)
SMEM = pl.BlockSpec(memory_space=pltpu.SMEM)
PLACE = ("patch", "tensor")
ROW_BY_ROW = (((1,), (1,)), ((), ()))

guide_scale = 5.0


def params(mib):
    return pltpu.CompilerParams(vmem_limit_bytes=mib * 2**20)


def slot_pairs(slot, back):
    pairs = []
    for y in range(2):
        for z in range(RING):
            for x in range(4):
                for core in range(2):
                    there = SLOTS * core + (z + slot) % SLOTS
                    source = (y * RING + z) * 8 + x * 2 + core
                    target = (y * RING + there) * 8 + x * 2 + z // SLOTS
                    pairs.append((target, source) if back else (source, target))
    return pairs


def to_slot(value, slot):
    return lax.ppermute(value, PLACE, slot_pairs(slot, False))


def from_slot(value, slot):
    return lax.ppermute(value, PLACE, slot_pairs(slot, True))


def other_y(value):
    return lax.ppermute(value, "patch", [(i, (i + RING) % (2 * RING)) for i in range(2 * RING)])


def other_core(value):
    return lax.ppermute(value, "tensor", [(i, i ^ 1) for i in range(8)])


def other_guide(value):
    return lax.ppermute(value, "guide", [(0, 1), (1, 0)])


def shift_x(value, step):
    return lax.ppermute(value, "tensor", [(i, (i + 2 * step) % 8) for i in range(8)])


def scores(queries, keys):
    return lax.dot_general(queries, keys, ROW_BY_ROW, preferred_element_type=jnp.float32)


def lay_out(z_ref, query, key, value, kv0, kv1, kv2, kv3, q0, q1, q2, q3):
    z = z_ref[0]
    last = slice(SLOTS * HEAD_DIM, (SLOTS + 1) * HEAD_DIM)
    for slot, (kv, q) in enumerate(((kv0, q0), (kv1, q1), (kv2, q2), (kv3, q3))):
        head = pl.ds(pl.multiple_of(lax.rem(z + slot, SLOTS) * HEAD_DIM, HEAD_DIM), HEAD_DIM)
        kv[0:ROWS, :] = key[:, head]
        kv[ROWS : 2 * ROWS, :] = value[:, head]
        kv[2 * ROWS : 3 * ROWS, :] = key[:, last]
        kv[3 * ROWS : 4 * ROWS, :] = value[:, last]
        q[0:ROWS, :] = query[:, head]
    q0[ROWS : 2 * ROWS, :] = query[:, last]


def fresh_kernel(query, key, value, out, lse):
    score = scores(query[...], key[...])
    peak = jnp.max(score, axis=1, keepdims=True) * SCALE2
    weights = jnp.exp2(score * SCALE2 - peak).astype(jnp.bfloat16)
    wide = jnp.concatenate([value[...], jnp.ones((ROWS, HEAD_DIM), jnp.bfloat16)], axis=1)
    both = jnp.dot(weights, wide, preferred_element_type=jnp.float32)
    total = both[:, HEAD_DIM:]
    out[0] = both[:, :HEAD_DIM] / total
    lse[0] = peak + jnp.log2(total)


def attend_kernel(slot, *refs):
    q, refs = refs[0], refs[1:]
    blocks, (out, level_at, held) = refs[:16], refs[16:]
    chunk = ROWS // 2
    for part in range(q.shape[0] // ROWS):
        order = [i for i in range(16) if i != 4 * slot]

        def chunk_step(c, carry, part=part, order=order):
            begin = pl.multiple_of(c * chunk, chunk)
            queries = q[pl.ds(part * ROWS + begin, chunk), :]
            both, peak = None, None
            for i in order:
                keys = blocks[i][2 * part * ROWS : (2 * part + 1) * ROWS, :]
                values = blocks[i][(2 * part + 1) * ROWS : (2 * part + 2) * ROWS, :]
                score = scores(queries, keys)
                if peak is None:
                    peak = jnp.max(score, axis=1, keepdims=True) * SCALE2
                weights = jnp.exp2(score * SCALE2 - peak).astype(jnp.bfloat16)
                wide = jnp.concatenate([values, jnp.ones((ROWS, HEAD_DIM), jnp.bfloat16)], axis=1)
                more = jnp.dot(weights, wide, preferred_element_type=jnp.float32)
                both = more if both is None else both + more

            def finish(both, peak):
                total = both[:, HEAD_DIM:]
                out[pl.ds(part * BLOCK + begin, chunk), :] = (both[:, :HEAD_DIM] / total).astype(jnp.bfloat16)
                level_at[pl.ds(begin, chunk), :] = peak + jnp.log2(total)

            finish(both, peak)
            largest = jnp.max(both[:, HEAD_DIM : HEAD_DIM + 1])

            @pl.when(jnp.logical_not(largest < SAFE_SUM))
            def _():
                for i in range(16):
                    held[i] = blocks[i][2 * part * ROWS : (2 * part + 2) * ROWS, :]

                def follow(i, state):
                    both, peak = state
                    keys, values = held[i, :ROWS, :], held[i, ROWS:, :]
                    score = scores(queries, keys) * SCALE2
                    score = jnp.where(i == 4 * slot, -1e30, score)
                    higher = jnp.maximum(peak, jnp.max(score, axis=1, keepdims=True))
                    weights = jnp.where(i == 4 * slot, 0.0, jnp.exp2(score - higher)).astype(jnp.bfloat16)
                    wide = jnp.concatenate([values, jnp.ones((ROWS, HEAD_DIM), jnp.bfloat16)], axis=1)
                    more = jnp.dot(weights, wide, preferred_element_type=jnp.float32)
                    return both * jnp.exp2(peak - higher) + more, higher

                start = (jnp.zeros((chunk, 2 * HEAD_DIM), jnp.float32), jnp.full((chunk, 1), -1e30, jnp.float32))
                finish(*lax.fori_loop(0, 16, follow, start))

            return carry

        lax.fori_loop(0, ROWS // chunk, chunk_step, 0)
        tile = HEAD_DIM
        lines = [jnp.transpose(level_at[i * tile : (i + 1) * tile, :])[0:1, :] for i in range(ROWS // tile)]
        level = jnp.concatenate(lines, axis=0)
        high = level.astype(jnp.bfloat16).astype(jnp.float32)
        rest = level - high
        middle = rest.astype(jnp.bfloat16).astype(jnp.float32)
        rows = jnp.concatenate([high, middle, rest - middle, jnp.zeros_like(level)], axis=0)
        out[part * BLOCK + ROWS : (part + 1) * BLOCK, :] = rows.astype(jnp.bfloat16)


def attend(slot, queries, blocks):
    parts = queries.shape[0] // ROWS
    units = 15 * parts
    return pl.pallas_call(
        functools.partial(attend_kernel, slot),
        out_shape=jax.ShapeDtypeStruct((parts * BLOCK, HEAD_DIM), jnp.bfloat16),
        in_specs=[VMEM] * 17,
        out_specs=VMEM,
        scratch_shapes=[
            pltpu.VMEM((ROWS, HEAD_DIM), jnp.float32),
            pltpu.VMEM((16, 2 * ROWS, HEAD_DIM), jnp.bfloat16),
        ],
        compiler_params=params(32),
        cost_estimate=pl.CostEstimate(
            flops=units * ROWS * ROWS * 4 * HEAD_DIM * 4,
            bytes_accessed=9 * 2**20,
            transcendentals=units * ROWS * ROWS,
        ),
        name="attend",
    )(queries, *blocks)


def combine_kernel(z_ref, guide_ref, r0, r1, r2, r3, out, lse, keep, send):
    z = z_ref[0]
    guide = guide_ref[0]
    half = ROWS // 2
    tile = HEAD_DIM
    todo = [(r, 0, lax.rem(z + s, SLOTS)) for s, r in enumerate((r0, r1, r2, r3))] + [(r0, BLOCK, SLOTS)]
    for r, row, head in todo:
        stat = r[row + ROWS : row + BLOCK, :].astype(jnp.float32)
        level = stat[0:4, :] + stat[4:8, :] + stat[8:12, :]
        for h in range(2):
            parts = []
            for i in range(h * half // tile, (h + 1) * half // tile):
                there = jnp.transpose(jnp.broadcast_to(level[i : i + 1, :], (tile, tile)))
                rows = slice(i * tile, (i + 1) * tile)
                here = out[head, rows, :]
                share = 1.0 / (1.0 + jnp.exp2(lse[head, rows, :] - there))
                came = r[row + i * tile : row + (i + 1) * tile, :].astype(jnp.float32)
                parts.append((here + (came - here) * share).astype(jnp.bfloat16))
            joined = jnp.concatenate(parts, axis=0)

            @pl.when(guide == h)
            def _(head=head, joined=joined):
                keep[head] = joined

            @pl.when(guide != h)
            def _(head=head, joined=joined):
                send[head] = joined


def project_kernel(place_ref, guide_ref, own, other, weight, out):
    first = guide_ref[0] == 0
    by_own = jnp.where(first, guide_scale, 1.0 - guide_scale)
    by_other = jnp.where(first, 1.0 - guide_scale, guide_scale)
    mixed = [
        (own[h].astype(jnp.float32) * by_own + other[h].astype(jnp.float32) * by_other).astype(jnp.bfloat16)
        for h in range(own.shape[0])
    ]
    rows = jnp.concatenate(mixed, axis=1)
    out[0] = jnp.dot(rows, weight[...], preferred_element_type=jnp.float32).astype(out.dtype)


def project(places, guide, own, other, weight, dtype):
    heads, rows, _ = own.shape
    width = weight.shape[0]
    whole = pl.BlockSpec((heads, rows, HEAD_DIM), lambda s, places, guide: (0, 0, 0))
    return pl.pallas_call(
        project_kernel,
        out_shape=jax.ShapeDtypeStruct((4, rows, width), dtype),
        grid_spec=pltpu.PrefetchScalarGridSpec(
            num_scalar_prefetch=2,
            grid=(4,),
            in_specs=[whole, whole, pl.BlockSpec((width, width), lambda s, places, guide: (0, places[s]))],
            out_specs=pl.BlockSpec((1, rows, width), lambda s, places, guide: (s, 0, 0)),
        ),
        compiler_params=params(58),
        cost_estimate=pl.CostEstimate(flops=2 * rows * width * width * 4, bytes_accessed=6 * 2**20, transcendentals=0),
        name="project",
    )(places, guide, own, other, weight)


def on_device(
    query,
    key_fresh,
    value_fresh,
    key_stale,
    value_stale,
    out_weight,
    stream,
    gate_table,
    step_index,
):
    rows, width = query.shape[1:]
    heads = width // HEAD_DIM
    half = rows // 2
    patch = lax.axis_index("patch")
    tensor = lax.axis_index("tensor")
    guide = lax.axis_index("guide")
    z = (patch % RING).astype(jnp.int32).reshape(1)
    guide_at = guide.astype(jnp.int32).reshape(1)

    kv_shape = jax.ShapeDtypeStruct((4 * rows, HEAD_DIM), jnp.bfloat16)
    q_shapes = [jax.ShapeDtypeStruct(((2 if s == 0 else 1) * rows, HEAD_DIM), jnp.bfloat16) for s in range(SLOTS)]
    laid = pl.pallas_call(
        lay_out,
        out_shape=[kv_shape] * SLOTS + q_shapes,
        in_specs=[SMEM] + [VMEM] * 3,
        out_specs=[VMEM] * 8,
        compiler_params=params(32),
        name="lay_out",
    )(z, query[0], key_stale[0], value_stale[0])
    kv, queries = list(laid[:SLOTS]), list(laid[SLOTS:])

    stream_mine = lax.dynamic_slice_in_dim(stream[0], guide * half, half, 0)
    stream_sent = lax.dynamic_slice_in_dim(stream[0], (1 - guide) * half, half, 0)
    stream_other = other_guide(stream_sent)

    column = pl.BlockSpec((rows, HEAD_DIM), lambda h: (0, h))
    stacked = pl.BlockSpec((1, rows, HEAD_DIM), lambda h: (h, 0, 0))
    fresh_shape = jax.ShapeDtypeStruct((heads, rows, HEAD_DIM), jnp.float32)
    fresh, fresh_lse = pl.pallas_call(
        fresh_kernel,
        out_shape=[fresh_shape, fresh_shape],
        grid=(heads,),
        in_specs=[column] * 3,
        out_specs=[stacked] * 2,
        compiler_params=params(32),
        cost_estimate=pl.CostEstimate(
            flops=heads * rows * rows * 4 * HEAD_DIM * 4, bytes_accessed=5 * 2**20, transcendentals=heads * rows * rows
        ),
        name="fresh",
    )(query[0], key_fresh[0], value_fresh[0])

    def after(value, *others):
        return lax.optimization_barrier((value, *others))[0]

    waiting = kv + queries
    arrived = []
    for n, value in enumerate(waiting):
        if n == 2:
            value = after(value, arrived[0], fresh_lse)
        elif n > 2:
            value = after(value, arrived[n - 2], *([stream_other] if n == 4 else []))
        arrived.append(to_slot(value, n % SLOTS))
    kv, queries = arrived[:SLOTS], arrived[SLOTS:]
    blocks = []
    for own in kv:
        over = other_y(own)
        blocks += [own, other_core(own), over, other_core(over)]
    came = [from_slot(attend(s, queries[s], blocks), s) for s in range(SLOTS)]

    att_shape = jax.ShapeDtypeStruct((heads, half, HEAD_DIM), jnp.bfloat16)
    keep, send = pl.pallas_call(
        combine_kernel,
        out_shape=[att_shape, att_shape],
        in_specs=[SMEM, SMEM] + [VMEM] * 6,
        out_specs=[VMEM] * 2,
        compiler_params=params(32),
        name="combine",
    )(z, guide_at, *came, fresh, fresh_lse)
    other = other_guide(send)

    x, core = tensor // 2, tensor % 2
    chips = (x + jnp.arange(4, dtype=jnp.int32)) % 4
    for_other = project((2 * chips + 1 - core).astype(jnp.int32), guide_at, keep, other, out_weight, jnp.bfloat16)
    swapped = other_core(for_other)
    for_own = project((2 * chips + core).astype(jnp.int32), guide_at, keep, other, out_weight, jnp.float32)
    shares = [for_own[s] + swapped[s].astype(jnp.float32) for s in range(4)]
    term = shares[0]
    for s in range(1, 4):
        term = term + shift_x(shares[s].astype(jnp.bfloat16), s).astype(jnp.float32)

    gate = lax.dynamic_index_in_dim(gate_table, step_index[0], 0, keepdims=False)
    mine, its = stream_mine.astype(jnp.float32), stream_other.astype(jnp.float32)
    cond = jnp.where(guide == 0, mine, its)
    uncond = jnp.where(guide == 0, its, mine)
    guided = (uncond + guide_scale * (cond - uncond) + gate[None, :] * term).astype(jnp.bfloat16)
    own_cols = width // 2
    kept = lax.dynamic_slice_in_dim(guided, guide * own_cols, own_cols, 1)
    handed = lax.dynamic_slice_in_dim(guided, (1 - guide) * own_cols, own_cols, 1)
    got = other_guide(handed)
    return jnp.where(
        guide == 0, jnp.concatenate([kept, got], axis=0), jnp.concatenate([got, kept], axis=0)
    )


def solution(mesh):
    in_specs = (
        P("guide", "patch", "tensor"),
        P("guide", "patch", "tensor"),
        P("guide", "patch", "tensor"),
        P("guide", "patch", "tensor"),
        P("guide", "patch", "tensor"),
        P("tensor", None),
        P("guide", "patch", "tensor"),
        P(None, "tensor"),
        P(),
    )
    out_specs = P("patch", ("tensor", "guide"))
    return jax.shard_map(
        on_device, mesh=mesh, in_specs=in_specs, out_specs=out_specs, check_vma=False
    )
```

```python
import functools

import jax
import jax.numpy as jnp
from jax import lax
from jax.experimental import pallas as pl
from jax.experimental.pallas import tpu as pltpu
from jax.sharding import PartitionSpec as P

HEAD_DIM = 128
SLOTS = 4
RING = 8
ROWS = 512
HALF = ROWS // 2
BLOCK = HALF + 16
SCALE2 = 1.4426950408889634 / HEAD_DIM**0.5
SAFE_SUM = 2.0**100
VMEM = pl.BlockSpec(memory_space=pltpu.VMEM)
SMEM = pl.BlockSpec(memory_space=pltpu.SMEM)
ANY = pl.BlockSpec(memory_space=pl.ANY)
PLACE = ("patch", "tensor")
ORDER = (1, 3, 0, 2)
TURNS = (1, 0, 3, 2)
ROW_BY_ROW = (((1,), (1,)), ((), ()))

guide_scale = 5.0


def params(mib):
    return pltpu.CompilerParams(vmem_limit_bytes=mib * 2**20)


def slot_pairs(slot, back):
    pairs = []
    for y in range(2):
        for z in range(RING):
            for x in range(4):
                for core in range(2):
                    there = SLOTS * core + (z + slot) % SLOTS
                    source = (y * RING + z) * 8 + x * 2 + core
                    target = (y * RING + there) * 8 + x * 2 + z // SLOTS
                    pairs.append((target, source) if back else (source, target))
    return pairs


def to_slot(value, slot):
    return lax.ppermute(value, PLACE, slot_pairs(slot, False))


def from_slot(value, slot):
    return lax.ppermute(value, PLACE, slot_pairs(slot, True))


def from_slot_to_other_guide(value, slot):
    pairs = [(2 * i + g, 2 * j + 1 - g) for i, j in slot_pairs(slot, True) for g in range(2)]
    return lax.ppermute(value, PLACE + ("guide",), pairs)


def other_y(value):
    return lax.ppermute(value, "patch", [(i, (i + RING) % (2 * RING)) for i in range(2 * RING)])


def other_core(value):
    return lax.ppermute(value, "tensor", [(i, i ^ 1) for i in range(8)])


def other_guide(value):
    return lax.ppermute(value, "guide", [(0, 1), (1, 0)])


def shift_x(value, step):
    return lax.ppermute(value, "tensor", [(i, (i + 2 * step) % 8) for i in range(8)])


def scores(queries, keys):
    return lax.dot_general(queries, keys, ROW_BY_ROW, preferred_element_type=jnp.float32)


def lay_out(z_ref, query, key, value, *refs):
    messages, (held, loaded, stored, *buffers) = refs[:SLOTS], refs[SLOTS:]
    z = z_ref[0]
    loads = [pltpu.make_async_copy(src, held.at[i], loaded.at[i]) for i, src in enumerate((key, value, query))]
    for load in loads:
        load.start()
    for load in loads:
        load.wait()
    last = slice(SLOTS * HEAD_DIM, (SLOTS + 1) * HEAD_DIM)
    stores = []
    for slot in ORDER:
        message, buffer = messages[slot], buffers[slot]
        head = pl.ds(pl.multiple_of(lax.rem(z + slot, SLOTS) * HEAD_DIM, HEAD_DIM), HEAD_DIM)
        buffer[0:ROWS, :] = held[0, :, head]
        buffer[ROWS : 2 * ROWS, :] = held[1, :, head]
        buffer[2 * ROWS : 3 * ROWS, :] = held[0, :, last]
        buffer[3 * ROWS : 4 * ROWS, :] = held[1, :, last]
        buffer[4 * ROWS : 5 * ROWS, :] = held[2, :, head]
        if slot == 0:
            buffer[5 * ROWS : 6 * ROWS, :] = held[2, :, last]
        stores.append(pltpu.make_async_copy(buffer, message, stored.at[slot]))
        stores[-1].start()
    for store in stores:
        store.wait()


def with_ones(values):
    return jnp.concatenate([values, jnp.ones(values.shape, values.dtype)], axis=1)


def write_level(target, row, level_at, half):
    tile = HEAD_DIM
    lines = []
    for i in range(half * HALF // tile, (half + 1) * HALF // tile):
        lines.append(jnp.transpose(level_at[i * tile : (i + 1) * tile, :])[0:1, :])
    level = jnp.concatenate(lines, axis=0)
    high = level.astype(jnp.bfloat16).astype(jnp.float32)
    rest = level - high
    middle = rest.astype(jnp.bfloat16).astype(jnp.float32)
    rows = jnp.concatenate([high, middle, rest - middle, jnp.zeros((10, tile), jnp.float32)], axis=0)
    target[row : row + BLOCK - HALF, :] = rows.astype(jnp.bfloat16)


def write_halves(guide, row, attended, level_at, keep, send):
    for half in range(2):
        for mine, target in ((True, keep), (False, send)):

            @pl.when((guide == half) == mine)
            def _(half=half, target=target):
                target[row : row + HALF, :] = attended[half * HALF : (half + 1) * HALF, :]
                write_level(target, row + HALF, level_at, half)


def fresh_kernel(guide_ref, query, key, value, keep, send, attended, level_at):
    for h in range(query.shape[1] // HEAD_DIM):
        cols = slice(h * HEAD_DIM, (h + 1) * HEAD_DIM)
        score = scores(query[:, cols], key[:, cols])
        peak = jnp.max(score, axis=1, keepdims=True) * SCALE2
        weights = jnp.exp2(score * SCALE2 - peak).astype(jnp.bfloat16)
        both = jnp.dot(weights, with_ones(value[:, cols]), preferred_element_type=jnp.float32)
        total = both[:, HEAD_DIM:]
        attended[...] = (both[:, :HEAD_DIM] / total).astype(jnp.bfloat16)
        level_at[...] = peak + jnp.log2(total)
        write_halves(guide_ref[0], h * BLOCK, attended, level_at, keep, send)


def attend_kernel(slot, guide_ref, *refs):
    blocks, (keep, send, attended, level_at, held) = refs[:16], refs[16:]
    own = 4 * slot
    q = blocks[own]
    for part in range(keep.shape[0] // BLOCK):
        order = [i for i in range(16) if i != own]

        def chunk_step(c, carry, part=part, order=order):
            begin = pl.multiple_of(c * HALF, HALF)
            queries = q[pl.ds((4 + part) * ROWS + begin, HALF), :]
            both, peak = None, None
            for i in order:
                keys = blocks[i][2 * part * ROWS : (2 * part + 1) * ROWS, :]
                values = blocks[i][(2 * part + 1) * ROWS : (2 * part + 2) * ROWS, :]
                score = scores(queries, keys)
                if peak is None:
                    peak = jnp.max(score, axis=1, keepdims=True) * SCALE2
                weights = jnp.exp2(score * SCALE2 - peak).astype(jnp.bfloat16)
                more = jnp.dot(weights, with_ones(values), preferred_element_type=jnp.float32)
                both = more if both is None else both + more

            def finish(both, peak):
                total = both[:, HEAD_DIM:]
                attended[pl.ds(begin, HALF), :] = (both[:, :HEAD_DIM] / total).astype(jnp.bfloat16)
                level_at[pl.ds(begin, HALF), :] = peak + jnp.log2(total)

            finish(both, peak)
            largest = jnp.max(both[:, HEAD_DIM : HEAD_DIM + 1])

            @pl.when(jnp.logical_not(largest < SAFE_SUM))
            def _():
                for i in range(16):
                    held[i] = blocks[i][2 * part * ROWS : (2 * part + 2) * ROWS, :]

                def follow(i, state):
                    both, peak = state
                    keys, values = held[i, :ROWS, :], held[i, ROWS:, :]
                    score = scores(queries, keys) * SCALE2
                    score = jnp.where(i == own, -1e30, score)
                    higher = jnp.maximum(peak, jnp.max(score, axis=1, keepdims=True))
                    weights = jnp.where(i == own, 0.0, jnp.exp2(score - higher)).astype(jnp.bfloat16)
                    more = jnp.dot(weights, with_ones(values), preferred_element_type=jnp.float32)
                    return both * jnp.exp2(peak - higher) + more, higher

                start = (jnp.zeros((HALF, 2 * HEAD_DIM), jnp.float32), jnp.full((HALF, 1), -1e30, jnp.float32))
                finish(*lax.fori_loop(0, 16, follow, start))

            return carry

        lax.fori_loop(0, 2, chunk_step, 0)
        write_halves(guide_ref[0], part * BLOCK, attended, level_at, keep, send)


def attend(slot, guide, blocks):
    parts = 2 if slot == 0 else 1
    units = 15 * parts
    out = jax.ShapeDtypeStruct((parts * BLOCK, HEAD_DIM), jnp.bfloat16)
    return pl.pallas_call(
        functools.partial(attend_kernel, slot),
        out_shape=[out, out],
        in_specs=[SMEM] + [VMEM] * 16,
        out_specs=[VMEM] * 2,
        scratch_shapes=[
            pltpu.VMEM((ROWS, HEAD_DIM), jnp.bfloat16),
            pltpu.VMEM((ROWS, HEAD_DIM), jnp.float32),
            pltpu.VMEM((16, 2 * ROWS, HEAD_DIM), jnp.bfloat16),
        ],
        compiler_params=params(32),
        cost_estimate=pl.CostEstimate(
            flops=units * ROWS * ROWS * 4 * HEAD_DIM * 4,
            bytes_accessed=9 * 2**20,
            transcendentals=units * ROWS * ROWS,
        ),
        name="attend",
    )(guide, *blocks)


def combine_kernel(z_ref, guide_ref, *refs):
    sides, out = (refs[0:5], refs[5:10]), refs[10]
    z = z_ref[0]
    first = guide_ref[0] == 0
    factors = (
        jnp.where(first, guide_scale, 1.0 - guide_scale),
        jnp.where(first, 1.0 - guide_scale, guide_scale),
    )
    tile = HEAD_DIM
    todo = [(s, 0, lax.rem(z + s, SLOTS)) for s in range(SLOTS)] + [(0, BLOCK, SLOTS)]

    def level_of(ref, start):
        stat = ref[pl.ds(start, BLOCK - HALF), :].astype(jnp.float32)
        level = stat[0:2, :] + stat[2:4, :] + stat[4:6, :]
        return [jnp.transpose(jnp.broadcast_to(level[i : i + 1, :], (tile, tile))) for i in range(HALF // tile)]

    for s, row, head in todo:
        at = pl.multiple_of(head * BLOCK, BLOCK - HALF)
        mixed = None
        for side, factor in zip(sides, factors):
            came, fresh = side[s], side[4]
            there = jnp.concatenate(level_of(came, row + HALF), axis=0)
            here = jnp.concatenate(level_of(fresh, at + HALF), axis=0)
            share = 1.0 / (1.0 + jnp.exp2(here - there))
            old = came[row : row + HALF, :].astype(jnp.float32)
            new = fresh[pl.ds(at, HALF), :].astype(jnp.float32)
            joined = (new + (old - new) * share) * factor
            mixed = joined if mixed is None else mixed + joined
        out[head] = mixed.astype(jnp.bfloat16)


def pick_kernel(place_ref, weight, out):
    out[0] = weight[...]


def project_kernel(place_ref, own, other, weight, other_weight, out0, out1, out2, out3, near, far, near_sem, far_sem):
    width = weight.shape[0]
    copies = []
    for s in range(4):
        cols = pl.ds(pl.multiple_of(place_ref[s] * width, width), width)
        copies.append(
            (
                pltpu.make_async_copy(weight.at[:, cols], near.at[s], near_sem.at[s]),
                pltpu.make_async_copy(other_weight.at[s], far.at[s], far_sem.at[s]),
            )
        )
    for s in (1, 2, 3, 0):
        copies[s][0].start()
        copies[s][1].start()
    mine = jnp.concatenate([own[h] for h in range(own.shape[0])], axis=1)
    its = jnp.concatenate([other[h] for h in range(own.shape[0])], axis=1)
    for s, out in ((1, out1), (2, out2), (3, out3), (0, out0)):
        copies[s][0].wait()
        copies[s][1].wait()
        share = jnp.dot(mine, near[s], preferred_element_type=jnp.float32)
        share = share + jnp.dot(its, far[s], preferred_element_type=jnp.float32)
        out[...] = share.astype(out.dtype)


def on_device(
    query,
    key_fresh,
    value_fresh,
    key_stale,
    value_stale,
    out_weight,
    stream,
    gate_table,
    step_index,
):
    rows, width = query.shape[1:]
    heads = width // HEAD_DIM
    half = rows // 2
    patch = lax.axis_index("patch")
    tensor = lax.axis_index("tensor")
    guide = lax.axis_index("guide")
    z = (patch % RING).astype(jnp.int32).reshape(1)
    guide_at = guide.astype(jnp.int32).reshape(1)

    def after(value, *others):
        return lax.optimization_barrier((value, *others))[0]

    sizes = [(6 if s == 0 else 5) * rows for s in range(SLOTS)]
    messages = pl.pallas_call(
        lay_out,
        out_shape=[jax.ShapeDtypeStruct((size, HEAD_DIM), jnp.bfloat16) for size in sizes],
        in_specs=[SMEM] + [ANY] * 3,
        out_specs=[ANY] * SLOTS,
        scratch_shapes=[
            pltpu.VMEM((3, rows, width), jnp.bfloat16),
            pltpu.SemaphoreType.DMA((3,)),
            pltpu.SemaphoreType.DMA((SLOTS,)),
        ]
        + [pltpu.VMEM((size, HEAD_DIM), jnp.bfloat16) for size in sizes],
        compiler_params=params(32),
        name="lay_out",
    )(z, query[0], key_stale[0], value_stale[0])

    stream_mine = lax.dynamic_slice_in_dim(stream[0], guide * half, half, 0)
    stream_sent = lax.dynamic_slice_in_dim(stream[0], (1 - guide) * half, half, 0)

    fresh_shape = jax.ShapeDtypeStruct((heads * BLOCK, HEAD_DIM), jnp.bfloat16)
    fresh_keep, fresh_send = pl.pallas_call(
        fresh_kernel,
        out_shape=[fresh_shape, fresh_shape],
        in_specs=[SMEM] + [VMEM] * 3,
        out_specs=[VMEM] * 2,
        scratch_shapes=[pltpu.VMEM((rows, HEAD_DIM), jnp.bfloat16), pltpu.VMEM((rows, HEAD_DIM), jnp.float32)],
        compiler_params=params(32),
        cost_estimate=pl.CostEstimate(
            flops=heads * rows * rows * 4 * HEAD_DIM * 4, bytes_accessed=5 * 2**20, transcendentals=heads * rows * rows
        ),
        name="fresh",
    )(guide_at, query[0], key_fresh[0], value_fresh[0])

    x, core = tensor // 2, tensor % 2
    chips = (x + jnp.arange(4, dtype=jnp.int32)) % 4
    near_places = (2 * chips + core).astype(jnp.int32)
    far_places = (2 * chips + 1 - core).astype(jnp.int32)
    weight_sent = pl.pallas_call(
        pick_kernel,
        out_shape=jax.ShapeDtypeStruct((4, width, width), jnp.bfloat16),
        grid_spec=pltpu.PrefetchScalarGridSpec(
            num_scalar_prefetch=1,
            grid=(4,),
            in_specs=[pl.BlockSpec((width, width), lambda s, places: (0, places[s]))],
            out_specs=pl.BlockSpec((1, width, width), lambda s, places: (s, 0, 0)),
        ),
        compiler_params=params(58),
        name="pick",
    )(far_places, out_weight)

    first, second, third, fourth = ORDER
    arrived = {}
    arrived[first] = to_slot(messages[first], first)
    arrived[second] = to_slot(messages[second], second)
    fresh_other = other_guide(fresh_send)
    arrived[third] = to_slot(after(messages[third], arrived[first], fresh_keep), third)
    stream_other = other_guide(after(stream_sent, fresh_send))
    weight_other = other_core(after(weight_sent, arrived[first]))
    arrived[fourth] = to_slot(after(messages[fourth], arrived[second], stream_other, fresh_other, weight_other), fourth)
    swapped = {}
    for s in ORDER:
        own = arrived[s]
        over = other_y(own)
        swapped[s] = [own, other_core(own), over, other_core(over)]
    blocks = [block for s in range(SLOTS) for block in swapped[s]]
    mine, its = [None] * SLOTS, [None] * SLOTS
    at = guide_at
    for n, s in enumerate(TURNS):
        keep, send = attend(s, at, blocks)
        mine[s], its[s] = from_slot(keep, s), from_slot_to_other_guide(send, s)
        at = after(guide_at, keep, *([mine[TURNS[n - 1]], its[TURNS[n - 1]]] if n else []))

    mixed = pl.pallas_call(
        combine_kernel,
        out_shape=jax.ShapeDtypeStruct((heads, half, HEAD_DIM), jnp.bfloat16),
        in_specs=[SMEM, SMEM] + [VMEM] * 10,
        out_specs=VMEM,
        compiler_params=params(32),
        name="combine",
    )(z, guide_at, *mine, fresh_keep, *its, fresh_other)

    share = jax.ShapeDtypeStruct((half, width), jnp.float32)
    sent = jax.ShapeDtypeStruct((half, width), jnp.bfloat16)
    shares = pl.pallas_call(
        project_kernel,
        out_shape=[share, sent, sent, sent],
        in_specs=[SMEM, VMEM, VMEM, ANY, ANY],
        out_specs=[VMEM] * 4,
        scratch_shapes=[pltpu.VMEM((4, width, width), jnp.bfloat16)] * 2 + [pltpu.SemaphoreType.DMA((4,))] * 2,
        compiler_params=params(48),
        cost_estimate=pl.CostEstimate(
            flops=2 * half * width * width * 8, bytes_accessed=10 * 2**20, transcendentals=0
        ),
        name="project",
    )(near_places, mixed, other_core(mixed), out_weight, weight_other)
    term = shares[0]
    for s in range(1, 4):
        term = term + shift_x(shares[s], s).astype(jnp.float32)

    gate = lax.dynamic_index_in_dim(gate_table, step_index[0], 0, keepdims=False)
    near, far = stream_mine.astype(jnp.float32), stream_other.astype(jnp.float32)
    cond = jnp.where(guide == 0, near, far)
    uncond = jnp.where(guide == 0, far, near)
    guided = (uncond + guide_scale * (cond - uncond) + gate[None, :] * term).astype(jnp.bfloat16)
    own_cols = width // 2
    stays = lax.dynamic_slice_in_dim(guided, guide * own_cols, own_cols, 1)
    goes = lax.dynamic_slice_in_dim(guided, (1 - guide) * own_cols, own_cols, 1)
    got = other_guide(goes)
    return jnp.where(
        guide == 0, jnp.concatenate([stays, got], axis=0), jnp.concatenate([got, stays], axis=0)
    )


def solution(mesh):
    in_specs = (
        P("guide", "patch", "tensor"),
        P("guide", "patch", "tensor"),
        P("guide", "patch", "tensor"),
        P("guide", "patch", "tensor"),
        P("guide", "patch", "tensor"),
        P("tensor", None),
        P("guide", "patch", "tensor"),
        P(None, "tensor"),
        P(),
    )
    out_specs = P("patch", ("tensor", "guide"))
    return jax.shard_map(
        on_device, mesh=mesh, in_specs=in_specs, out_specs=out_specs, check_vma=False
    )
```

```python
import functools

import jax
import jax.numpy as jnp
from jax import lax
from jax.experimental import pallas as pl
from jax.experimental.pallas import tpu as pltpu
from jax.sharding import PartitionSpec as P

HEAD_DIM = 128
SLOTS = 4
RING = 8
ROWS = 512
HALF = ROWS // 2
BLOCK = HALF + 16
SCALE2 = 1.4426950408889634 / HEAD_DIM**0.5
SAFE_SUM = 2.0**100
VMEM = pl.BlockSpec(memory_space=pltpu.VMEM)
SMEM = pl.BlockSpec(memory_space=pltpu.SMEM)
ANY = pl.BlockSpec(memory_space=pl.ANY)
PLACE = ("patch", "tensor")
PAIRS = ((1, 3), (0, 2))
ORDER = PAIRS[0] + PAIRS[1]
LOTS = (((1, 0), (0, 0), (0, 1), (3, 0), (2, 0)),)
STAGE_ARRAYS = {(PAIRS[0], 1): 4, (PAIRS[1], 0): 2, (PAIRS[1], None): 2}
ROW_BY_ROW = (((1,), (1,)), ((), ()))

guide_scale = 5.0


def params(mib):
    return pltpu.CompilerParams(vmem_limit_bytes=mib * 2**20)


def slot_pairs(slot, back):
    pairs = []
    for y in range(2):
        for z in range(RING):
            for x in range(4):
                for core in range(2):
                    there = SLOTS * core + (z + slot) % SLOTS
                    source = (y * RING + z) * 8 + x * 2 + core
                    target = (y * RING + there) * 8 + x * 2 + z // SLOTS
                    pairs.append((target, source) if back else (source, target))
    return pairs


def to_slot(value, slot):
    return lax.ppermute(value, PLACE, slot_pairs(slot, False))


def from_slot(value, slot):
    return lax.ppermute(value, PLACE, slot_pairs(slot, True))


def from_slot_to_other_guide(value, slot):
    pairs = [(2 * i + g, 2 * j + 1 - g) for i, j in slot_pairs(slot, True) for g in range(2)]
    return lax.ppermute(value, PLACE + ("guide",), pairs)


def other_y(value):
    return lax.ppermute(value, "patch", [(i, (i + RING) % (2 * RING)) for i in range(2 * RING)])


def other_core(value):
    return lax.ppermute(value, "tensor", [(i, i ^ 1) for i in range(8)])


def other_guide(value):
    return lax.ppermute(value, "guide", [(0, 1), (1, 0)])


def shift_x(value, step):
    return lax.ppermute(value, "tensor", [(i, (i + 2 * step) % 8) for i in range(8)])


def scores(queries, keys):
    return lax.dot_general(queries, keys, ROW_BY_ROW, preferred_element_type=jnp.float32)


def lay_out(z_ref, query, key, value, *refs):
    messages, (held, loaded, stored, *buffers) = refs[:SLOTS], refs[SLOTS:]
    z = z_ref[0]
    loads = [pltpu.make_async_copy(src, held.at[i], loaded.at[i]) for i, src in enumerate((key, value, query))]
    for load in loads:
        load.start()
    for load in loads:
        load.wait()
    last = slice(SLOTS * HEAD_DIM, (SLOTS + 1) * HEAD_DIM)
    stores = []
    for slot in ORDER:
        message, buffer = messages[slot], buffers[slot]
        head = pl.ds(pl.multiple_of(lax.rem(z + slot, SLOTS) * HEAD_DIM, HEAD_DIM), HEAD_DIM)
        buffer[0:ROWS, :] = held[0, :, head]
        buffer[ROWS : 2 * ROWS, :] = held[1, :, head]
        buffer[2 * ROWS : 3 * ROWS, :] = held[0, :, last]
        buffer[3 * ROWS : 4 * ROWS, :] = held[1, :, last]
        buffer[4 * ROWS : 5 * ROWS, :] = held[2, :, head]
        if slot == 0:
            buffer[5 * ROWS : 6 * ROWS, :] = held[2, :, last]
        stores.append(pltpu.make_async_copy(buffer, message, stored.at[slot]))
        stores[-1].start()
    for store in stores:
        store.wait()


def with_ones(values):
    return jnp.concatenate([values, jnp.ones(values.shape, values.dtype)], axis=1)


def write_level(target, row, level_at, half):
    tile = HEAD_DIM
    lines = []
    for i in range(half * HALF // tile, (half + 1) * HALF // tile):
        lines.append(jnp.transpose(level_at[i * tile : (i + 1) * tile, :])[0:1, :])
    level = jnp.concatenate(lines, axis=0)
    high = level.astype(jnp.bfloat16).astype(jnp.float32)
    rest = level - high
    middle = rest.astype(jnp.bfloat16).astype(jnp.float32)
    rows = jnp.concatenate([high, middle, rest - middle, jnp.zeros((10, tile), jnp.float32)], axis=0)
    target[row : row + BLOCK - HALF, :] = rows.astype(jnp.bfloat16)


def write_halves(guide, row, attended, level_at, keep, send):
    for half in range(2):
        for mine, target in ((True, keep), (False, send)):

            @pl.when((guide == half) == mine)
            def _(half=half, target=target):
                target[row : row + HALF, :] = attended[half * HALF : (half + 1) * HALF, :]
                write_level(target, row + HALF, level_at, half)


def fresh_kernel(guide_ref, query, key, value, keep, send, attended, level_at):
    for h in range(query.shape[1] // HEAD_DIM):
        cols = slice(h * HEAD_DIM, (h + 1) * HEAD_DIM)
        score = scores(query[:, cols], key[:, cols])
        peak = jnp.max(score, axis=1, keepdims=True) * SCALE2
        weights = jnp.exp2(score * SCALE2 - peak).astype(jnp.bfloat16)
        both = jnp.dot(weights, with_ones(value[:, cols]), preferred_element_type=jnp.float32)
        total = both[:, HEAD_DIM:]
        attended[...] = (both[:, :HEAD_DIM] / total).astype(jnp.bfloat16)
        level_at[...] = peak + jnp.log2(total)
        write_halves(guide_ref[0], h * BLOCK, attended, level_at, keep, send)


def stage_kernel(pair, own_at, lots, first, last, *refs):
    if last:
        guide_ref, *refs = refs
    slots = sorted({slot for lot in lots for slot, _ in lot})
    messages, refs = dict(zip(slots, refs)), refs[len(slots) :]
    count = STAGE_ARRAYS[pair, own_at]
    arrays, refs = refs[:count], refs[count:]
    if not first:
        states_in, refs = refs[: 2 * len(lots)], refs[2 * len(lots) :]
    if last:
        outs, refs = refs[: 2 * len(slots)], refs[2 * len(slots) :]
        outs = {slot: outs[2 * i : 2 * i + 2] for i, slot in enumerate(slots)}
        attended, level_at, *refs = refs
    else:
        states_out, refs = refs[: 2 * len(lots)], refs[2 * len(lots) :]
    (held,) = refs
    places = [(a, i) for a in range(count) for i in range(2)]
    lane = lax.broadcasted_iota(jnp.int32, (HALF, HEAD_DIM), 1)
    for l, lot in enumerate(lots):
        for n, (slot, part) in enumerate(lot):
            fresh_at = -1
            if own_at is not None and slot in pair:
                fresh_at = places.index((own_at, pair.index(slot)))

            def rows_of(a, i, part=part):
                base = (4 * i + 2 * part) * ROWS
                return arrays[a], base

            def chunk_step(c, carry, l=l, n=n, slot=slot, part=part, fresh_at=fresh_at, rows_of=rows_of):
                begin = pl.multiple_of(c * HALF, HALF)
                span = pl.ds(n * ROWS + begin, HALF)
                queries = messages[slot][pl.ds((4 + part) * ROWS + begin, HALF), :]

                def before():
                    stat = states_in[2 * l + 1][span, :]
                    total = jnp.broadcast_to(stat[:, 0:1], stat.shape)
                    middle = HEAD_DIM // 2
                    return jnp.concatenate([states_in[2 * l][span, :], total], axis=1), stat[:, middle : middle + 1]

                def finish(both, peak):
                    total = both[:, HEAD_DIM:]
                    if last:
                        here = pl.ds(begin, HALF)
                        attended[here, :] = (both[:, :HEAD_DIM] / total).astype(jnp.bfloat16)
                        level_at[here, :] = peak + jnp.log2(total)
                    else:
                        states_out[2 * l][span, :] = both[:, :HEAD_DIM]
                        states_out[2 * l + 1][span, :] = jnp.where(lane < HEAD_DIM // 2, total, peak)

                both, peak = (None, None) if first else before()
                for at, (a, i) in enumerate(places):
                    if at == fresh_at:
                        continue
                    array, base = rows_of(a, i)
                    score = scores(queries, array[base : base + ROWS, :])
                    if peak is None:
                        peak = jnp.max(score, axis=1, keepdims=True) * SCALE2
                    weights = jnp.exp2(score * SCALE2 - peak).astype(jnp.bfloat16)
                    values = array[base + ROWS : base + 2 * ROWS, :]
                    more = jnp.dot(weights, with_ones(values), preferred_element_type=jnp.float32)
                    both = more if both is None else both + more
                finish(both, peak)
                largest = jnp.max(both[:, HEAD_DIM : HEAD_DIM + 1])

                @pl.when(jnp.logical_not(largest < SAFE_SUM))
                def _():
                    for at, (a, i) in enumerate(places):
                        array, base = rows_of(a, i)
                        held[at] = array[base : base + 2 * ROWS, :]

                    def follow(at, state):
                        both, peak = state
                        score = scores(queries, held[at, :ROWS, :]) * SCALE2
                        score = jnp.where(at == fresh_at, -1e30, score)
                        higher = jnp.maximum(peak, jnp.max(score, axis=1, keepdims=True))
                        weights = jnp.where(at == fresh_at, 0.0, jnp.exp2(score - higher)).astype(jnp.bfloat16)
                        more = jnp.dot(weights, with_ones(held[at, ROWS:, :]), preferred_element_type=jnp.float32)
                        return both * jnp.exp2(peak - higher) + more, higher

                    if first:
                        start = (jnp.zeros((HALF, 2 * HEAD_DIM), jnp.float32), jnp.full((HALF, 1), -1e30, jnp.float32))
                    else:
                        start = before()
                    finish(*lax.fori_loop(0, len(places), follow, start))

                return carry

            lax.fori_loop(0, 2, chunk_step, 0)
            if last:
                write_halves(guide_ref[0], part * BLOCK, attended, level_at, *outs[slot])


def stage(pair, own_at, lots, messages, arrays, states, guide=None):
    first, last = states is None, guide is not None
    slots = sorted({slot for lot in lots for slot, _ in lot})
    operands = ([guide] if last else []) + [messages[s] for s in slots] + list(arrays) + ([] if first else list(states))
    if last:
        out_shape = [
            jax.ShapeDtypeStruct(((2 if slot == 0 else 1) * BLOCK, HEAD_DIM), jnp.bfloat16)
            for slot in slots
            for _ in range(2)
        ]
    else:
        out_shape = [jax.ShapeDtypeStruct((len(lot) * ROWS, HEAD_DIM), jnp.float32) for lot in lots for _ in range(2)]
    scratch = [pltpu.VMEM((2 * len(arrays), 2 * ROWS, HEAD_DIM), jnp.bfloat16)]
    if last:
        scratch = [pltpu.VMEM((ROWS, HEAD_DIM), jnp.bfloat16), pltpu.VMEM((ROWS, HEAD_DIM), jnp.float32)] + scratch
    units = sum(len(lot) for lot in lots) * 2 * len(arrays)
    return pl.pallas_call(
        functools.partial(stage_kernel, pair, own_at, lots, first, last),
        out_shape=out_shape,
        in_specs=([SMEM] if last else []) + [VMEM] * (len(operands) - last),
        out_specs=[VMEM] * len(out_shape),
        scratch_shapes=scratch,
        compiler_params=params(32),
        cost_estimate=pl.CostEstimate(
            flops=units * ROWS * ROWS * 4 * HEAD_DIM * 4,
            bytes_accessed=9 * 2**20,
            transcendentals=units * ROWS * ROWS,
        ),
        name="stage",
    )(*operands)


def combine_kernel(z_ref, guide_ref, *refs):
    sides, out = (refs[0:5], refs[5:10]), refs[10]
    z = z_ref[0]
    first = guide_ref[0] == 0
    factors = (
        jnp.where(first, guide_scale, 1.0 - guide_scale),
        jnp.where(first, 1.0 - guide_scale, guide_scale),
    )
    tile = HEAD_DIM
    todo = [(s, 0, lax.rem(z + s, SLOTS)) for s in range(SLOTS)] + [(0, BLOCK, SLOTS)]

    def level_of(ref, start):
        stat = ref[pl.ds(start, BLOCK - HALF), :].astype(jnp.float32)
        level = stat[0:2, :] + stat[2:4, :] + stat[4:6, :]
        return [jnp.transpose(jnp.broadcast_to(level[i : i + 1, :], (tile, tile))) for i in range(HALF // tile)]

    for s, row, head in todo:
        at = pl.multiple_of(head * BLOCK, BLOCK - HALF)
        mixed = None
        for side, factor in zip(sides, factors):
            came, fresh = side[s], side[4]
            there = jnp.concatenate(level_of(came, row + HALF), axis=0)
            here = jnp.concatenate(level_of(fresh, at + HALF), axis=0)
            share = 1.0 / (1.0 + jnp.exp2(here - there))
            old = came[row : row + HALF, :].astype(jnp.float32)
            new = fresh[pl.ds(at, HALF), :].astype(jnp.float32)
            joined = (new + (old - new) * share) * factor
            mixed = joined if mixed is None else mixed + joined
        out[head] = mixed.astype(jnp.bfloat16)


def pick_kernel(place_ref, weight, out):
    out[0] = weight[...]


def project_kernel(place_ref, own, other, weight, other_weight, out0, out1, out2, out3, near, near_sem):
    width = weight.shape[0]
    copies = []
    for s in range(4):
        cols = pl.ds(pl.multiple_of(place_ref[s] * width, width), width)
        copies.append(pltpu.make_async_copy(weight.at[:, cols], near.at[s], near_sem.at[s]))
    for s in (1, 2, 3, 0):
        copies[s].start()
    mine = jnp.concatenate([own[h] for h in range(own.shape[0])], axis=1)
    its = jnp.concatenate([other[h] for h in range(own.shape[0])], axis=1)
    for s, out in ((1, out1), (2, out2), (3, out3), (0, out0)):
        share = jnp.dot(its, other_weight[s], preferred_element_type=jnp.float32)
        copies[s].wait()
        share = share + jnp.dot(mine, near[s], preferred_element_type=jnp.float32)
        out[...] = share.astype(out.dtype)


def on_device(
    query,
    key_fresh,
    value_fresh,
    key_stale,
    value_stale,
    out_weight,
    stream,
    gate_table,
    step_index,
):
    rows, width = query.shape[1:]
    heads = width // HEAD_DIM
    half = rows // 2
    patch = lax.axis_index("patch")
    tensor = lax.axis_index("tensor")
    guide = lax.axis_index("guide")
    z = (patch % RING).astype(jnp.int32).reshape(1)
    guide_at = guide.astype(jnp.int32).reshape(1)

    def after(value, *others):
        return lax.optimization_barrier((value, *others))[0]

    sizes = [(6 if s == 0 else 5) * rows for s in range(SLOTS)]
    messages = pl.pallas_call(
        lay_out,
        out_shape=[jax.ShapeDtypeStruct((size, HEAD_DIM), jnp.bfloat16) for size in sizes],
        in_specs=[SMEM] + [ANY] * 3,
        out_specs=[ANY] * SLOTS,
        scratch_shapes=[
            pltpu.VMEM((3, rows, width), jnp.bfloat16),
            pltpu.SemaphoreType.DMA((3,)),
            pltpu.SemaphoreType.DMA((SLOTS,)),
        ]
        + [pltpu.VMEM((size, HEAD_DIM), jnp.bfloat16) for size in sizes],
        compiler_params=params(58),
        name="lay_out",
    )(z, query[0], key_stale[0], value_stale[0])

    stream_mine = lax.dynamic_slice_in_dim(stream[0], guide * half, half, 0)
    stream_sent = lax.dynamic_slice_in_dim(stream[0], (1 - guide) * half, half, 0)

    fresh_shape = jax.ShapeDtypeStruct((heads * BLOCK, HEAD_DIM), jnp.bfloat16)
    fresh_keep, fresh_send = pl.pallas_call(
        fresh_kernel,
        out_shape=[fresh_shape, fresh_shape],
        in_specs=[SMEM] + [VMEM] * 3,
        out_specs=[VMEM] * 2,
        scratch_shapes=[pltpu.VMEM((rows, HEAD_DIM), jnp.bfloat16), pltpu.VMEM((rows, HEAD_DIM), jnp.float32)],
        compiler_params=params(32),
        cost_estimate=pl.CostEstimate(
            flops=heads * rows * rows * 4 * HEAD_DIM * 4, bytes_accessed=5 * 2**20, transcendentals=heads * rows * rows
        ),
        name="fresh",
    )(guide_at, query[0], key_fresh[0], value_fresh[0])

    x, core = tensor // 2, tensor % 2
    chips = (x + jnp.arange(4, dtype=jnp.int32)) % 4
    near_places = (2 * chips + core).astype(jnp.int32)
    far_places = (2 * chips + 1 - core).astype(jnp.int32)
    weight_sent = pl.pallas_call(
        pick_kernel,
        out_shape=jax.ShapeDtypeStruct((4, width, width), jnp.bfloat16),
        grid_spec=pltpu.PrefetchScalarGridSpec(
            num_scalar_prefetch=1,
            grid=(4,),
            in_specs=[pl.BlockSpec((width, width), lambda s, places: (0, places[s]))],
            out_specs=pl.BlockSpec((1, width, width), lambda s, places: (s, 0, 0)),
        ),
        compiler_params=params(58),
        name="pick",
    )(far_places, out_weight)

    def joined(pair):
        return jnp.concatenate([arrived[slot][: 4 * rows] for slot in pair], axis=0)

    arrived = {slot: to_slot(messages[slot], slot) for slot in PAIRS[0]}
    here, there = (arrived[slot] for slot in PAIRS[0])
    fresh_other = other_guide(fresh_send)
    stream_other = other_guide(stream_sent)
    weight_other = other_core(weight_sent)
    here, there, fresh_other, stream_other, weight_other = lax.optimization_barrier(
        (here, there, fresh_other, stream_other, weight_other)
    )
    arrived = dict(zip(PAIRS[0], (here, there)))
    for slot in PAIRS[1]:
        arrived[slot] = to_slot(after(messages[slot], here, there), slot)
    early = joined(PAIRS[0])
    early_y, early_core = other_y(early), other_core(early)
    early_y_core = other_core(early_y)
    late = joined(PAIRS[1])
    late_y, late_core = other_y(late), other_core(late)
    states = stage(PAIRS[0], 1, LOTS, arrived, [early_core, early, early_y, early_y_core], None)
    states = stage(PAIRS[1], 0, LOTS, arrived, [late, late_core], states)
    late_y, *states = lax.optimization_barrier((late_y, *states))
    late_y_core = other_core(late_y)
    mine, its = [None] * SLOTS, [None] * SLOTS
    at = guide_at
    for l, lot in enumerate(LOTS):
        slots = sorted({slot for slot, _ in lot})
        outs = stage(PAIRS[1], None, (lot,), arrived, [late_y, late_y_core], states[2 * l : 2 * l + 2], at)
        for i, slot in enumerate(slots):
            mine[slot] = from_slot(outs[2 * i], slot)
            its[slot] = from_slot_to_other_guide(outs[2 * i + 1], slot)
        at = after(guide_at, outs[0])

    mixed = pl.pallas_call(
        combine_kernel,
        out_shape=jax.ShapeDtypeStruct((heads, half, HEAD_DIM), jnp.bfloat16),
        in_specs=[SMEM, SMEM] + [VMEM] * 10,
        out_specs=VMEM,
        compiler_params=params(32),
        name="combine",
    )(z, guide_at, *mine, fresh_keep, *its, fresh_other)

    share = jax.ShapeDtypeStruct((half, width), jnp.float32)
    sent = jax.ShapeDtypeStruct((half, width), jnp.bfloat16)
    shares = pl.pallas_call(
        project_kernel,
        out_shape=[share, sent, sent, sent],
        in_specs=[SMEM, VMEM, VMEM, ANY, VMEM],
        out_specs=[VMEM] * 4,
        scratch_shapes=[pltpu.VMEM((4, width, width), jnp.bfloat16), pltpu.SemaphoreType.DMA((4,))],
        compiler_params=params(48),
        cost_estimate=pl.CostEstimate(
            flops=2 * half * width * width * 8, bytes_accessed=10 * 2**20, transcendentals=0
        ),
        name="project",
    )(near_places, mixed, other_core(mixed), out_weight, weight_other)
    term = shares[0]
    for s in range(1, 4):
        term = term + shift_x(shares[s], s).astype(jnp.float32)

    gate = lax.dynamic_index_in_dim(gate_table, step_index[0], 0, keepdims=False)
    near, far = stream_mine.astype(jnp.float32), stream_other.astype(jnp.float32)
    cond = jnp.where(guide == 0, near, far)
    uncond = jnp.where(guide == 0, far, near)
    guided = (uncond + guide_scale * (cond - uncond) + gate[None, :] * term).astype(jnp.bfloat16)
    own_cols = width // 2
    stays = lax.dynamic_slice_in_dim(guided, guide * own_cols, own_cols, 1)
    goes = lax.dynamic_slice_in_dim(guided, (1 - guide) * own_cols, own_cols, 1)
    got = other_guide(goes)
    return jnp.where(
        guide == 0, jnp.concatenate([stays, got], axis=0), jnp.concatenate([got, stays], axis=0)
    )


def solution(mesh):
    in_specs = (
        P("guide", "patch", "tensor"),
        P("guide", "patch", "tensor"),
        P("guide", "patch", "tensor"),
        P("guide", "patch", "tensor"),
        P("guide", "patch", "tensor"),
        P("tensor", None),
        P("guide", "patch", "tensor"),
        P(None, "tensor"),
        P(),
    )
    out_specs = P("patch", ("tensor", "guide"))
    return jax.shard_map(
        on_device, mesh=mesh, in_specs=in_specs, out_specs=out_specs, check_vma=False
    )
```

```python
import functools

import jax
import jax.numpy as jnp
from jax import lax
from jax.experimental import pallas as pl
from jax.experimental.pallas import tpu as pltpu
from jax.sharding import PartitionSpec as P

HEAD_DIM = 128
SLOTS = 4
RING = 8
ROWS = 512
HALF = ROWS // 2
BLOCK = HALF + 16
SCALE2 = 1.4426950408889634 / HEAD_DIM**0.5
SAFE_SUM = 2.0**100
VMEM = pl.BlockSpec(memory_space=pltpu.VMEM)
SMEM = pl.BlockSpec(memory_space=pltpu.SMEM)
ANY = pl.BlockSpec(memory_space=pl.ANY)
PLACE = ("patch", "tensor")
PAIRS = ((1, 3), (0, 2))
ORDER = PAIRS[0] + PAIRS[1]
LOTS = (((1, 0),), ((0, 0), (0, 1)), ((3, 0),), ((2, 0),))
STAGE_ARRAYS = {(PAIRS[0], 1): 4, (PAIRS[1], 0): 2, (PAIRS[1], None): 2}
ROW_BY_ROW = (((1,), (1,)), ((), ()))

guide_scale = 5.0


def params(mib):
    return pltpu.CompilerParams(vmem_limit_bytes=mib * 2**20)


def slot_pairs(slot, back):
    pairs = []
    for y in range(2):
        for z in range(RING):
            for x in range(4):
                for core in range(2):
                    there = SLOTS * core + (z + slot) % SLOTS
                    source = (y * RING + z) * 8 + x * 2 + core
                    target = (y * RING + there) * 8 + x * 2 + z // SLOTS
                    pairs.append((target, source) if back else (source, target))
    return pairs


def to_slot(value, slot):
    return lax.ppermute(value, PLACE, slot_pairs(slot, False))


def from_slot(value, slot):
    return lax.ppermute(value, PLACE, slot_pairs(slot, True))


def from_slot_to_other_guide(value, slot):
    pairs = [(2 * i + g, 2 * j + 1 - g) for i, j in slot_pairs(slot, True) for g in range(2)]
    return lax.ppermute(value, PLACE + ("guide",), pairs)


def other_y(value):
    return lax.ppermute(value, "patch", [(i, (i + RING) % (2 * RING)) for i in range(2 * RING)])


def other_core(value):
    return lax.ppermute(value, "tensor", [(i, i ^ 1) for i in range(8)])


def other_guide(value):
    return lax.ppermute(value, "guide", [(0, 1), (1, 0)])


def shift_x(value, step):
    return lax.ppermute(value, "tensor", [(i, (i + 2 * step) % 8) for i in range(8)])


def scores(queries, keys):
    return lax.dot_general(queries, keys, ROW_BY_ROW, preferred_element_type=jnp.float32)


def lay_out(z_ref, query, key, value, *refs):
    messages, (held, loaded, stored, *buffers) = refs[:SLOTS], refs[SLOTS:]
    z = z_ref[0]
    loads = [pltpu.make_async_copy(src, held.at[i], loaded.at[i]) for i, src in enumerate((key, value, query))]
    for load in loads:
        load.start()
    for load in loads:
        load.wait()
    last = slice(SLOTS * HEAD_DIM, (SLOTS + 1) * HEAD_DIM)
    stores = []
    for slot in ORDER:
        message, buffer = messages[slot], buffers[slot]
        head = pl.ds(pl.multiple_of(lax.rem(z + slot, SLOTS) * HEAD_DIM, HEAD_DIM), HEAD_DIM)
        buffer[0:ROWS, :] = held[0, :, head]
        buffer[ROWS : 2 * ROWS, :] = held[1, :, head]
        buffer[2 * ROWS : 3 * ROWS, :] = held[0, :, last]
        buffer[3 * ROWS : 4 * ROWS, :] = held[1, :, last]
        buffer[4 * ROWS : 5 * ROWS, :] = held[2, :, head]
        if slot == 0:
            buffer[5 * ROWS : 6 * ROWS, :] = held[2, :, last]
        stores.append(pltpu.make_async_copy(buffer, message, stored.at[slot]))
        stores[-1].start()
    for store in stores:
        store.wait()


def with_ones(values):
    return jnp.concatenate([values, jnp.ones(values.shape, values.dtype)], axis=1)


def write_level(target, row, level_at, half):
    tile = HEAD_DIM
    lines = []
    for i in range(half * HALF // tile, (half + 1) * HALF // tile):
        lines.append(jnp.transpose(level_at[i * tile : (i + 1) * tile, :])[0:1, :])
    level = jnp.concatenate(lines, axis=0)
    high = level.astype(jnp.bfloat16).astype(jnp.float32)
    rest = level - high
    middle = rest.astype(jnp.bfloat16).astype(jnp.float32)
    rows = jnp.concatenate([high, middle, rest - middle, jnp.zeros((10, tile), jnp.float32)], axis=0)
    target[row : row + BLOCK - HALF, :] = rows.astype(jnp.bfloat16)


def write_halves(guide, row, attended, level_at, keep, send):
    for half in range(2):
        for mine, target in ((True, keep), (False, send)):

            @pl.when((guide == half) == mine)
            def _(half=half, target=target):
                target[row : row + HALF, :] = attended[half * HALF : (half + 1) * HALF, :]
                write_level(target, row + HALF, level_at, half)


def fresh_kernel(guide_ref, query, key, value, keep, send, attended, level_at):
    for h in range(query.shape[1] // HEAD_DIM):
        cols = slice(h * HEAD_DIM, (h + 1) * HEAD_DIM)
        score = scores(query[:, cols], key[:, cols])
        peak = jnp.max(score, axis=1, keepdims=True) * SCALE2
        weights = jnp.exp2(score * SCALE2 - peak).astype(jnp.bfloat16)
        both = jnp.dot(weights, with_ones(value[:, cols]), preferred_element_type=jnp.float32)
        total = both[:, HEAD_DIM:]
        attended[...] = (both[:, :HEAD_DIM] / total).astype(jnp.bfloat16)
        level_at[...] = peak + jnp.log2(total)
        write_halves(guide_ref[0], h * BLOCK, attended, level_at, keep, send)


def stage_kernel(pair, own_at, lot, at_row, first, last, *refs):
    if last:
        guide_ref, *refs = refs
    slots = sorted({slot for slot, _ in lot})
    messages, refs = dict(zip(slots, refs)), refs[len(slots) :]
    count = STAGE_ARRAYS[pair, own_at]
    arrays, refs = refs[:count], refs[count:]
    if not first:
        (summed_in, stat_in), refs = refs[:2], refs[2:]
    if last:
        outs, (attended, level_at, held) = refs[: 2 * len(slots)], refs[2 * len(slots) :]
    else:
        summed_out, stat_out, held = refs
    places = [(a, i) for a in range(count) for i in range(2)]
    middle = HEAD_DIM // 2
    lane = lax.broadcasted_iota(jnp.int32, (HALF, HEAD_DIM), 1)

    def fresh_place(slot):
        if own_at is None or slot not in pair:
            return -1
        return places.index((own_at, pair.index(slot)))

    def before(n, begin):
        span = pl.ds(at_row + n * ROWS + begin, HALF)
        stat = stat_in[span, :]
        total = jnp.broadcast_to(stat[:, 0:1], stat.shape)
        return jnp.concatenate([summed_in[span, :], total], axis=1), stat[:, middle : middle + 1]

    def finish(n, begin, both, peak):
        span = pl.ds(n * ROWS + begin, HALF)
        total = both[:, HEAD_DIM:]
        if last:
            attended[span, :] = (both[:, :HEAD_DIM] / total).astype(jnp.bfloat16)
            level_at[span, :] = peak + jnp.log2(total)
        else:
            summed_out[span, :] = both[:, :HEAD_DIM]
            stat_out[span, :] = jnp.where(lane < middle, total, peak)

    largest = None
    for n, (slot, part) in enumerate(lot):
        for begin in (0, HALF):
            queries = messages[slot][(4 + part) * ROWS + begin : (4 + part) * ROWS + begin + HALF, :]
            both, peak = (None, None) if first else before(n, begin)
            for at, (a, i) in enumerate(places):
                if at == fresh_place(slot):
                    continue
                base = (4 * i + 2 * part) * ROWS
                score = scores(queries, arrays[a][base : base + ROWS, :])
                if peak is None:
                    peak = jnp.max(score, axis=1, keepdims=True) * SCALE2
                weights = jnp.exp2(score * SCALE2 - peak).astype(jnp.bfloat16)
                values = arrays[a][base + ROWS : base + 2 * ROWS, :]
                more = jnp.dot(weights, with_ones(values), preferred_element_type=jnp.float32)
                both = more if both is None else both + more
            finish(n, begin, both, peak)
            largest = both[:, HEAD_DIM:] if largest is None else jnp.maximum(largest, both[:, HEAD_DIM:])

    @pl.when(jnp.logical_not(jnp.max(largest) < SAFE_SUM))
    def _():
        for n, (slot, part) in enumerate(lot):
            for at, (a, i) in enumerate(places):
                base = (4 * i + 2 * part) * ROWS
                held[at] = arrays[a][base : base + 2 * ROWS, :]

            def chunk_step(c, carry, n=n, slot=slot, part=part):
                begin = pl.multiple_of(c * HALF, HALF)
                queries = messages[slot][pl.ds((4 + part) * ROWS + begin, HALF), :]

                def follow(at, state):
                    both, peak = state
                    score = scores(queries, held[at, :ROWS, :]) * SCALE2
                    score = jnp.where(at == fresh_place(slot), -1e30, score)
                    higher = jnp.maximum(peak, jnp.max(score, axis=1, keepdims=True))
                    weights = jnp.where(at == fresh_place(slot), 0.0, jnp.exp2(score - higher)).astype(jnp.bfloat16)
                    more = jnp.dot(weights, with_ones(held[at, ROWS:, :]), preferred_element_type=jnp.float32)
                    return both * jnp.exp2(peak - higher) + more, higher

                if first:
                    start = (jnp.zeros((HALF, 2 * HEAD_DIM), jnp.float32), jnp.full((HALF, 1), -1e30, jnp.float32))
                else:
                    start = before(n, begin)
                finish(n, begin, *lax.fori_loop(0, len(places), follow, start))
                return carry

            lax.fori_loop(0, 2, chunk_step, 0)

    if last:
        for n, (slot, part) in enumerate(lot):
            here = pl.ds(n * ROWS, ROWS)
            keep, send = outs[2 * slots.index(slot) : 2 * slots.index(slot) + 2]
            write_halves(guide_ref[0], part * BLOCK, attended.at[here, :], level_at.at[here, :], keep, send)


def stage(pair, own_at, lot, messages, arrays, state, guide=None, at_row=0):
    first, last = state is None, guide is not None
    slots = sorted({slot for slot, _ in lot})
    operands = ([guide] if last else []) + [messages[s] for s in slots] + list(arrays) + ([] if first else list(state))
    if last:
        out_shape = [
            jax.ShapeDtypeStruct(((2 if slot == 0 else 1) * BLOCK, HEAD_DIM), jnp.bfloat16)
            for slot in slots
            for _ in range(2)
        ]
    else:
        out_shape = [jax.ShapeDtypeStruct((len(lot) * ROWS, HEAD_DIM), jnp.float32)] * 2
    scratch = [pltpu.VMEM((2 * len(arrays), 2 * ROWS, HEAD_DIM), jnp.bfloat16)]
    if last:
        lines = len(lot) * ROWS
        scratch = [pltpu.VMEM((lines, HEAD_DIM), jnp.bfloat16), pltpu.VMEM((lines, HEAD_DIM), jnp.float32)] + scratch
    units = len(lot) * 2 * len(arrays)
    return pl.pallas_call(
        functools.partial(stage_kernel, pair, own_at, lot, at_row, first, last),
        out_shape=out_shape,
        in_specs=([SMEM] if last else []) + [VMEM] * (len(operands) - last),
        out_specs=[VMEM] * len(out_shape),
        scratch_shapes=scratch,
        compiler_params=params(32),
        cost_estimate=pl.CostEstimate(
            flops=units * ROWS * ROWS * 4 * HEAD_DIM * 4,
            bytes_accessed=9 * 2**20,
            transcendentals=units * ROWS * ROWS,
        ),
        name="stage",
    )(*operands)


def combine_kernel(z_ref, guide_ref, *refs):
    sides, out = (refs[0:5], refs[5:10]), refs[10]
    z = z_ref[0]
    first = guide_ref[0] == 0
    factors = (
        jnp.where(first, guide_scale, 1.0 - guide_scale),
        jnp.where(first, 1.0 - guide_scale, guide_scale),
    )
    tile = HEAD_DIM
    todo = [(s, 0, lax.rem(z + s, SLOTS)) for s in range(SLOTS)] + [(0, BLOCK, SLOTS)]

    def level_of(ref, start):
        stat = ref[pl.ds(start, BLOCK - HALF), :].astype(jnp.float32)
        level = stat[0:2, :] + stat[2:4, :] + stat[4:6, :]
        return [jnp.transpose(jnp.broadcast_to(level[i : i + 1, :], (tile, tile))) for i in range(HALF // tile)]

    for s, row, head in todo:
        at = pl.multiple_of(head * BLOCK, BLOCK - HALF)
        mixed = None
        for side, factor in zip(sides, factors):
            came, fresh = side[s], side[4]
            there = jnp.concatenate(level_of(came, row + HALF), axis=0)
            here = jnp.concatenate(level_of(fresh, at + HALF), axis=0)
            share = 1.0 / (1.0 + jnp.exp2(here - there))
            old = came[row : row + HALF, :].astype(jnp.float32)
            new = fresh[pl.ds(at, HALF), :].astype(jnp.float32)
            joined = (new + (old - new) * share) * factor
            mixed = joined if mixed is None else mixed + joined
        out[head] = mixed.astype(jnp.bfloat16)


def pick_kernel(near_ref, far_ref, weight, near, far, buffer, loaded, stored):
    width = weight.shape[0]
    loads, stores = [], []
    for i, (places, target) in enumerate(((far_ref, far), (near_ref, near))):
        for s in range(4):
            cols = pl.ds(pl.multiple_of(places[s] * width, width), width)
            at = 4 * i + s
            loads.append(pltpu.make_async_copy(weight.at[:, cols], buffer.at[at], loaded.at[at]))
            stores.append(pltpu.make_async_copy(buffer.at[at], target.at[s], stored.at[at]))
    for load in loads:
        load.start()
    for load, store in zip(loads, stores):
        load.wait()
        store.start()
    for store in stores:
        store.wait()


def project_kernel(own, other, weight, other_weight, out0, out1, out2, out3):
    mine = jnp.concatenate([own[h] for h in range(own.shape[0])], axis=1)
    its = jnp.concatenate([other[h] for h in range(own.shape[0])], axis=1)
    for s, out in ((1, out1), (2, out2), (3, out3), (0, out0)):
        share = jnp.dot(mine, weight[s], preferred_element_type=jnp.float32)
        share = share + jnp.dot(its, other_weight[s], preferred_element_type=jnp.float32)
        out[...] = share.astype(out.dtype)


def on_device(
    query,
    key_fresh,
    value_fresh,
    key_stale,
    value_stale,
    out_weight,
    stream,
    gate_table,
    step_index,
):
    rows, width = query.shape[1:]
    heads = width // HEAD_DIM
    half = rows // 2
    patch = lax.axis_index("patch")
    tensor = lax.axis_index("tensor")
    guide = lax.axis_index("guide")
    z = (patch % RING).astype(jnp.int32).reshape(1)
    guide_at = guide.astype(jnp.int32).reshape(1)

    def after(value, *others):
        return lax.optimization_barrier((value, *others))[0]

    sizes = [(6 if s == 0 else 5) * rows for s in range(SLOTS)]
    messages = pl.pallas_call(
        lay_out,
        out_shape=[jax.ShapeDtypeStruct((size, HEAD_DIM), jnp.bfloat16) for size in sizes],
        in_specs=[SMEM] + [ANY] * 3,
        out_specs=[ANY] * SLOTS,
        scratch_shapes=[
            pltpu.VMEM((3, rows, width), jnp.bfloat16),
            pltpu.SemaphoreType.DMA((3,)),
            pltpu.SemaphoreType.DMA((SLOTS,)),
        ]
        + [pltpu.VMEM((size, HEAD_DIM), jnp.bfloat16) for size in sizes],
        compiler_params=params(58),
        name="lay_out",
    )(z, query[0], key_stale[0], value_stale[0])

    stream_mine = lax.dynamic_slice_in_dim(stream[0], guide * half, half, 0)
    stream_sent = lax.dynamic_slice_in_dim(stream[0], (1 - guide) * half, half, 0)

    fresh_shape = jax.ShapeDtypeStruct((heads * BLOCK, HEAD_DIM), jnp.bfloat16)
    fresh_keep, fresh_send = pl.pallas_call(
        fresh_kernel,
        out_shape=[fresh_shape, fresh_shape],
        in_specs=[SMEM] + [VMEM] * 3,
        out_specs=[VMEM] * 2,
        scratch_shapes=[pltpu.VMEM((rows, HEAD_DIM), jnp.bfloat16), pltpu.VMEM((rows, HEAD_DIM), jnp.float32)],
        compiler_params=params(32),
        cost_estimate=pl.CostEstimate(flops=2**10, bytes_accessed=2**10, transcendentals=0),
        name="fresh",
    )(guide_at, query[0], key_fresh[0], value_fresh[0])

    x, core = tensor // 2, tensor % 2
    chips = (x + jnp.arange(4, dtype=jnp.int32)) % 4
    near_places = (2 * chips + core).astype(jnp.int32)
    far_places = (2 * chips + 1 - core).astype(jnp.int32)
    blocks_shape = jax.ShapeDtypeStruct((4, width, width), jnp.bfloat16)
    weight_own, weight_sent = pl.pallas_call(
        pick_kernel,
        out_shape=[blocks_shape, blocks_shape],
        in_specs=[SMEM, SMEM, ANY],
        out_specs=[ANY, ANY],
        scratch_shapes=[
            pltpu.VMEM((8, width, width), jnp.bfloat16),
            pltpu.SemaphoreType.DMA((8,)),
            pltpu.SemaphoreType.DMA((8,)),
        ],
        compiler_params=params(48),
        cost_estimate=pl.CostEstimate(flops=0, bytes_accessed=2**10, transcendentals=0),
        name="pick",
    )(near_places, after(far_places, messages[ORDER[0]]), out_weight)

    def joined(pair):
        return jnp.concatenate([arrived[slot][: 4 * rows] for slot in pair], axis=0)

    arrived = {slot: to_slot(messages[slot], slot) for slot in PAIRS[0]}
    here, there = (arrived[slot] for slot in PAIRS[0])
    fresh_other = other_guide(fresh_send)
    stream_other = other_guide(stream_sent)
    here, there, fresh_other, stream_other, weight_sent = lax.optimization_barrier(
        (here, there, fresh_other, stream_other, weight_sent)
    )
    arrived = dict(zip(PAIRS[0], (here, there)))
    for slot in PAIRS[1]:
        arrived[slot] = to_slot(after(messages[slot], here, there), slot)
    early = joined(PAIRS[0])
    early_y, early_core = other_y(early), other_core(early)
    early_y_core = other_core(early_y)
    late = joined(PAIRS[1])
    late_y, late_core = other_y(late), other_core(late)
    whole_lot = sum(LOTS, ())
    state = stage(PAIRS[0], 1, whole_lot, arrived, [early_core, early, early_y, early_y_core], None)
    weight_other = other_core(after(weight_sent, early_y))
    late_y, weight_other, *state = lax.optimization_barrier((late_y, weight_other, *state))
    late_y_core = other_core(late_y)
    state = stage(PAIRS[1], 0, whole_lot, arrived, [late, late_core], state)
    mine, its = [None] * SLOTS, [None] * SLOTS
    at, done = guide_at, 0
    for n, lot in enumerate(LOTS):
        slot = lot[0][0]
        keep, send = stage(PAIRS[1], None, lot, arrived, [late_y, late_y_core], state, at, done * rows)
        done += len(lot)
        mine[slot], its[slot] = from_slot(keep, slot), from_slot_to_other_guide(send, slot)
        back = LOTS[n - 1][0][0]
        at = after(guide_at, keep, *([mine[back], its[back]] if n else []))

    mixed = pl.pallas_call(
        combine_kernel,
        out_shape=jax.ShapeDtypeStruct((heads, half, HEAD_DIM), jnp.bfloat16),
        in_specs=[SMEM, SMEM] + [VMEM] * 10,
        out_specs=VMEM,
        compiler_params=params(32),
        name="combine",
    )(z, guide_at, *mine, fresh_keep, *its, fresh_other)

    share = jax.ShapeDtypeStruct((half, width), jnp.float32)
    sent = jax.ShapeDtypeStruct((half, width), jnp.bfloat16)
    shares = pl.pallas_call(
        project_kernel,
        out_shape=[share, sent, sent, sent],
        in_specs=[VMEM] * 4,
        out_specs=[VMEM] * 4,
        compiler_params=params(32),
        cost_estimate=pl.CostEstimate(
            flops=2 * half * width * width * 8, bytes_accessed=10 * 2**20, transcendentals=0
        ),
        name="project",
    )(mixed, other_core(mixed), weight_own, weight_other)
    term = shares[0]
    for s in range(1, 4):
        term = term + shift_x(shares[s], s).astype(jnp.float32)

    gate = lax.dynamic_index_in_dim(gate_table, step_index[0], 0, keepdims=False)
    near, far = stream_mine.astype(jnp.float32), stream_other.astype(jnp.float32)
    cond = jnp.where(guide == 0, near, far)
    uncond = jnp.where(guide == 0, far, near)
    guided = (uncond + guide_scale * (cond - uncond) + gate[None, :] * term).astype(jnp.bfloat16)
    own_cols = width // 2
    stays = lax.dynamic_slice_in_dim(guided, guide * own_cols, own_cols, 1)
    goes = lax.dynamic_slice_in_dim(guided, (1 - guide) * own_cols, own_cols, 1)
    got = other_guide(goes)
    return jnp.where(
        guide == 0, jnp.concatenate([stays, got], axis=0), jnp.concatenate([got, stays], axis=0)
    )


def solution(mesh):
    in_specs = (
        P("guide", "patch", "tensor"),
        P("guide", "patch", "tensor"),
        P("guide", "patch", "tensor"),
        P("guide", "patch", "tensor"),
        P("guide", "patch", "tensor"),
        P("tensor", None),
        P("guide", "patch", "tensor"),
        P(None, "tensor"),
        P(),
    )
    out_specs = P("patch", ("tensor", "guide"))
    return jax.shard_map(
        on_device, mesh=mesh, in_specs=in_specs, out_specs=out_specs, check_vma=False
    )
```

```python
import functools

import jax
import jax.numpy as jnp
from jax import lax
from jax.experimental import pallas as pl
from jax.experimental.pallas import tpu as pltpu
from jax.sharding import PartitionSpec as P

HEAD_DIM = 128
SLOTS = 4
RING = 8
ROWS = 512
HALF = ROWS // 2
BLOCK = HALF + 16
SCALE2 = 1.4426950408889634 / HEAD_DIM**0.5
SAFE_SUM = 2.0**100
VMEM = pl.BlockSpec(memory_space=pltpu.VMEM)
SMEM = pl.BlockSpec(memory_space=pltpu.SMEM)
ANY = pl.BlockSpec(memory_space=pl.ANY)
PLACE = ("patch", "tensor")
PAIRS = ((1, 3), (0, 2))
ORDER = PAIRS[0] + PAIRS[1]
WHOLE = ("early", "early_y", "early_core", "early_y_core")
QUERIES = ((1, 0), (3, 0), (2, 0), (0, 0), (0, 1))
ROW_BY_ROW = (((1,), (1,)), ((), ()))

guide_scale = 5.0


def params(mib):
    return pltpu.CompilerParams(vmem_limit_bytes=mib * 2**20)


def slot_pairs(slot, back):
    pairs = []
    for y in range(2):
        for z in range(RING):
            for x in range(4):
                for core in range(2):
                    there = SLOTS * core + (z + slot) % SLOTS
                    source = (y * RING + z) * 8 + x * 2 + core
                    target = (y * RING + there) * 8 + x * 2 + z // SLOTS
                    pairs.append((target, source) if back else (source, target))
    return pairs


def to_slot(value, slot):
    return lax.ppermute(value, PLACE, slot_pairs(slot, False))


def from_slot(value, slot):
    return lax.ppermute(value, PLACE, slot_pairs(slot, True))


def from_slot_to_other_guide(value, slot):
    pairs = [(2 * i + g, 2 * j + 1 - g) for i, j in slot_pairs(slot, True) for g in range(2)]
    return lax.ppermute(value, PLACE + ("guide",), pairs)


def other_y(value):
    return lax.ppermute(value, "patch", [(i, (i + RING) % (2 * RING)) for i in range(2 * RING)])


def other_core(value):
    return lax.ppermute(value, "tensor", [(i, i ^ 1) for i in range(8)])


def other_guide(value):
    return lax.ppermute(value, "guide", [(0, 1), (1, 0)])


def shift_x(value, step):
    return lax.ppermute(value, "tensor", [(i, (i + 2 * step) % 8) for i in range(8)])


def scores(queries, keys):
    return lax.dot_general(queries, keys, ROW_BY_ROW, preferred_element_type=jnp.float32)


def lay_out(z_ref, query, key, value, *refs):
    messages, (held, loaded, stored, *buffers) = refs[:SLOTS], refs[SLOTS:]
    z = z_ref[0]
    loads = [pltpu.make_async_copy(src, held.at[i], loaded.at[i]) for i, src in enumerate((key, value, query))]
    for load in loads:
        load.start()
    for load in loads:
        load.wait()
    last = slice(SLOTS * HEAD_DIM, (SLOTS + 1) * HEAD_DIM)
    stores = []
    for slot in ORDER:
        message, buffer = messages[slot], buffers[slot]
        head = pl.ds(pl.multiple_of(lax.rem(z + slot, SLOTS) * HEAD_DIM, HEAD_DIM), HEAD_DIM)
        buffer[0:ROWS, :] = held[0, :, head]
        buffer[ROWS : 2 * ROWS, :] = held[1, :, head]
        buffer[2 * ROWS : 3 * ROWS, :] = held[0, :, last]
        buffer[3 * ROWS : 4 * ROWS, :] = held[1, :, last]
        buffer[4 * ROWS : 5 * ROWS, :] = held[2, :, head]
        if slot == 0:
            buffer[5 * ROWS : 6 * ROWS, :] = held[2, :, last]
        stores.append(pltpu.make_async_copy(buffer, message, stored.at[slot]))
        stores[-1].start()
    for store in stores:
        store.wait()


def with_ones(values):
    return jnp.concatenate([values, jnp.ones(values.shape, values.dtype)], axis=1)


def write_level(target, row, level_at, half):
    tile = HEAD_DIM
    lines = []
    for i in range(half * HALF // tile, (half + 1) * HALF // tile):
        lines.append(jnp.transpose(level_at[i * tile : (i + 1) * tile, :])[0:1, :])
    level = jnp.concatenate(lines, axis=0)
    high = level.astype(jnp.bfloat16).astype(jnp.float32)
    rest = level - high
    middle = rest.astype(jnp.bfloat16).astype(jnp.float32)
    rows = jnp.concatenate([high, middle, rest - middle, jnp.zeros((10, tile), jnp.float32)], axis=0)
    target[row : row + BLOCK - HALF, :] = rows.astype(jnp.bfloat16)


def write_halves(guide, row, attended, level_at, keep, send):
    for half in range(2):
        for mine, target in ((True, keep), (False, send)):

            @pl.when((guide == half) == mine)
            def _(half=half, target=target):
                target[row : row + HALF, :] = attended[half * HALF : (half + 1) * HALF, :]
                write_level(target, row + HALF, level_at, half)


def fresh_kernel(guide_ref, query, key, value, keep, send, attended, level_at):
    for h in range(query.shape[1] // HEAD_DIM):
        cols = slice(h * HEAD_DIM, (h + 1) * HEAD_DIM)
        score = scores(query[:, cols], key[:, cols])
        peak = jnp.max(score, axis=1, keepdims=True) * SCALE2
        weights = jnp.exp2(score * SCALE2 - peak).astype(jnp.bfloat16)
        both = jnp.dot(weights, with_ones(value[:, cols]), preferred_element_type=jnp.float32)
        total = both[:, HEAD_DIM:]
        attended[...] = (both[:, :HEAD_DIM] / total).astype(jnp.bfloat16)
        level_at[...] = peak + jnp.log2(total)
        write_halves(guide_ref[0], h * BLOCK, attended, level_at, keep, send)


def stage_kernel(work, first, last, with_tail, *refs):
    if last:
        guide_ref, *refs = refs
    slots = sorted({slot for slot, _, _, _ in work})
    arrays_used = sorted({a for _, _, _, places in work for a, _ in places})
    messages, refs = dict(zip(slots, refs)), refs[len(slots) :]
    arrays, refs = dict(zip(arrays_used, refs)), refs[len(arrays_used) :]
    if not first:
        (summed_in, stat_in), refs = refs[:2], refs[2:]
    if with_tail:
        (summed_tail, stat_tail), refs = refs[:2], refs[2:]
    if last:
        outs, (attended, level_at, held) = refs[: 2 * len(slots)], refs[2 * len(slots) :]
    else:
        summed_out, stat_out, held = refs
    middle = HEAD_DIM // 2
    lane = lax.broadcasted_iota(jnp.int32, (HALF, HEAD_DIM), 1)

    def before(row, begin):
        summed, stat = summed_in, stat_in
        if with_tail and row == SLOTS * ROWS:
            row, summed, stat = 0, summed_tail, stat_tail
        span = pl.ds(row + begin, HALF)
        stat = stat[span, :]
        total = jnp.broadcast_to(stat[:, 0:1], stat.shape)
        return jnp.concatenate([summed[span, :], total], axis=1), stat[:, middle : middle + 1]

    def finish(row, n, begin, both, peak):
        total = both[:, HEAD_DIM:]
        if last:
            span = pl.ds(n * ROWS + begin, HALF)
            attended[span, :] = (both[:, :HEAD_DIM] / total).astype(jnp.bfloat16)
            level_at[span, :] = peak + jnp.log2(total)
        else:
            span = pl.ds(row + begin, HALF)
            summed_out[span, :] = both[:, :HEAD_DIM]
            stat_out[span, :] = jnp.where(lane < middle, total, peak)

    largest = None
    for n, (slot, part, row, places) in enumerate(work):
        for begin in (0, HALF):
            queries = messages[slot][(4 + part) * ROWS + begin : (4 + part) * ROWS + begin + HALF, :]
            both, peak = (None, None) if first else before(row, begin)
            for a, base in places:
                score = scores(queries, arrays[a][base : base + ROWS, :])
                if peak is None:
                    peak = jnp.max(score, axis=1, keepdims=True) * SCALE2
                weights = jnp.exp2(score * SCALE2 - peak).astype(jnp.bfloat16)
                values = arrays[a][base + ROWS : base + 2 * ROWS, :]
                more = jnp.dot(weights, with_ones(values), preferred_element_type=jnp.float32)
                both = more if both is None else both + more
            finish(row, n, begin, both, peak)
            largest = both[:, HEAD_DIM:] if largest is None else jnp.maximum(largest, both[:, HEAD_DIM:])

    @pl.when(jnp.logical_not(jnp.max(largest) < SAFE_SUM))
    def _():
        for n, (slot, part, row, places) in enumerate(work):
            for at, (a, base) in enumerate(places):
                held[at] = arrays[a][base : base + 2 * ROWS, :]

            def chunk_step(c, carry, n=n, slot=slot, part=part, row=row, count=len(places)):
                begin = pl.multiple_of(c * HALF, HALF)
                queries = messages[slot][pl.ds((4 + part) * ROWS + begin, HALF), :]

                def follow(at, state):
                    both, peak = state
                    score = scores(queries, held[at, :ROWS, :]) * SCALE2
                    higher = jnp.maximum(peak, jnp.max(score, axis=1, keepdims=True))
                    weights = jnp.exp2(score - higher).astype(jnp.bfloat16)
                    more = jnp.dot(weights, with_ones(held[at, ROWS:, :]), preferred_element_type=jnp.float32)
                    return both * jnp.exp2(peak - higher) + more, higher

                if first:
                    start = (jnp.zeros((HALF, 2 * HEAD_DIM), jnp.float32), jnp.full((HALF, 1), -1e30, jnp.float32))
                else:
                    start = before(row, begin)
                finish(row, n, begin, *lax.fori_loop(0, count, follow, start))
                return carry

            lax.fori_loop(0, 2, chunk_step, 0)

    if last:
        for n, (slot, part, _, _) in enumerate(work):
            here = pl.ds(n * ROWS, ROWS)
            keep, send = outs[2 * slots.index(slot) : 2 * slots.index(slot) + 2]
            write_halves(guide_ref[0], part * BLOCK, attended.at[here, :], level_at.at[here, :], keep, send)


def stage(work, messages, arrays, state, guide=None, tail=()):
    first, last = state is None, guide is not None
    slots = sorted({slot for slot, _, _, _ in work})
    arrays_used = sorted({a for _, _, _, places in work for a, _ in places})
    operands = [guide] if last else []
    operands += [messages[s] for s in slots] + [arrays[a] for a in arrays_used] + ([] if first else list(state)) + list(tail)
    lines = len(work) * ROWS
    if last:
        out_shape = [
            jax.ShapeDtypeStruct(((2 if slot == 0 else 1) * BLOCK, HEAD_DIM), jnp.bfloat16)
            for slot in slots
            for _ in range(2)
        ]
    else:
        out_shape = [jax.ShapeDtypeStruct((lines, HEAD_DIM), jnp.float32)] * 2
    scratch = [pltpu.VMEM((max(len(places) for _, _, _, places in work), 2 * ROWS, HEAD_DIM), jnp.bfloat16)]
    if last:
        scratch = [pltpu.VMEM((lines, HEAD_DIM), jnp.bfloat16), pltpu.VMEM((lines, HEAD_DIM), jnp.float32)] + scratch
    units = sum(len(places) for _, _, _, places in work)
    return pl.pallas_call(
        functools.partial(stage_kernel, work, first, last, len(tail) > 0),
        out_shape=out_shape,
        in_specs=([SMEM] if last else []) + [VMEM] * (len(operands) - last),
        out_specs=[VMEM] * len(out_shape),
        scratch_shapes=scratch,
        compiler_params=params(32),
        cost_estimate=pl.CostEstimate(
            flops=units * ROWS * ROWS * 4 * HEAD_DIM * 4,
            bytes_accessed=9 * 2**20,
            transcendentals=units * ROWS * ROWS,
        ),
        name="stage",
    )(*operands)


def combine_kernel(z_ref, guide_ref, *refs):
    sides, out = (refs[0:5], refs[5:10]), refs[10]
    z = z_ref[0]
    first = guide_ref[0] == 0
    factors = (
        jnp.where(first, guide_scale, 1.0 - guide_scale),
        jnp.where(first, 1.0 - guide_scale, guide_scale),
    )
    tile = HEAD_DIM
    todo = [(s, 0, lax.rem(z + s, SLOTS)) for s in range(SLOTS)] + [(0, BLOCK, SLOTS)]

    def level_of(ref, start):
        stat = ref[pl.ds(start, BLOCK - HALF), :].astype(jnp.float32)
        level = stat[0:2, :] + stat[2:4, :] + stat[4:6, :]
        return [jnp.transpose(jnp.broadcast_to(level[i : i + 1, :], (tile, tile))) for i in range(HALF // tile)]

    for s, row, head in todo:
        at = pl.multiple_of(head * BLOCK, BLOCK - HALF)
        mixed = None
        for side, factor in zip(sides, factors):
            came, fresh = side[s], side[4]
            there = jnp.concatenate(level_of(came, row + HALF), axis=0)
            here = jnp.concatenate(level_of(fresh, at + HALF), axis=0)
            share = 1.0 / (1.0 + jnp.exp2(here - there))
            old = came[row : row + HALF, :].astype(jnp.float32)
            new = fresh[pl.ds(at, HALF), :].astype(jnp.float32)
            joined = (new + (old - new) * share) * factor
            mixed = joined if mixed is None else mixed + joined
        out[head] = mixed.astype(jnp.bfloat16)


def pick_kernel(near_ref, far_ref, weight, near, far, buffer, loaded, stored):
    width = weight.shape[0]
    loads, stores = [], []
    for i, (places, target) in enumerate(((far_ref, far), (near_ref, near))):
        for s in range(4):
            cols = pl.ds(pl.multiple_of(places[s] * width, width), width)
            at = 4 * i + s
            loads.append(pltpu.make_async_copy(weight.at[:, cols], buffer.at[at], loaded.at[at]))
            stores.append(pltpu.make_async_copy(buffer.at[at], target.at[s], stored.at[at]))
    for load in loads:
        load.start()
    for load, store in zip(loads, stores):
        load.wait()
        store.start()
    for store in stores:
        store.wait()


def project_kernel(own, other, weight, other_weight, out0, out1, out2, out3):
    mine = jnp.concatenate([own[h] for h in range(own.shape[0])], axis=1)
    its = jnp.concatenate([other[h] for h in range(own.shape[0])], axis=1)
    for s, out in ((1, out1), (2, out2), (3, out3), (0, out0)):
        share = jnp.dot(mine, weight[s], preferred_element_type=jnp.float32)
        share = share + jnp.dot(its, other_weight[s], preferred_element_type=jnp.float32)
        out[...] = share.astype(out.dtype)


def on_device(
    query,
    key_fresh,
    value_fresh,
    key_stale,
    value_stale,
    out_weight,
    stream,
    gate_table,
    step_index,
):
    rows, width = query.shape[1:]
    heads = width // HEAD_DIM
    half = rows // 2
    patch = lax.axis_index("patch")
    tensor = lax.axis_index("tensor")
    guide = lax.axis_index("guide")
    z = (patch % RING).astype(jnp.int32).reshape(1)
    guide_at = guide.astype(jnp.int32).reshape(1)

    def after(value, *others):
        return lax.optimization_barrier((value, *others))[0]

    sizes = [(6 if s == 0 else 5) * rows for s in range(SLOTS)]
    messages = pl.pallas_call(
        lay_out,
        out_shape=[jax.ShapeDtypeStruct((size, HEAD_DIM), jnp.bfloat16) for size in sizes],
        in_specs=[SMEM] + [ANY] * 3,
        out_specs=[ANY] * SLOTS,
        scratch_shapes=[
            pltpu.VMEM((3, rows, width), jnp.bfloat16),
            pltpu.SemaphoreType.DMA((3,)),
            pltpu.SemaphoreType.DMA((SLOTS,)),
        ]
        + [pltpu.VMEM((size, HEAD_DIM), jnp.bfloat16) for size in sizes],
        compiler_params=params(58),
        name="lay_out",
    )(z, query[0], key_stale[0], value_stale[0])

    stream_mine = lax.dynamic_slice_in_dim(stream[0], guide * half, half, 0)
    stream_sent = lax.dynamic_slice_in_dim(stream[0], (1 - guide) * half, half, 0)

    fresh_shape = jax.ShapeDtypeStruct((heads * BLOCK, HEAD_DIM), jnp.bfloat16)
    fresh_keep, fresh_send = pl.pallas_call(
        fresh_kernel,
        out_shape=[fresh_shape, fresh_shape],
        in_specs=[SMEM] + [VMEM] * 3,
        out_specs=[VMEM] * 2,
        scratch_shapes=[pltpu.VMEM((rows, HEAD_DIM), jnp.bfloat16), pltpu.VMEM((rows, HEAD_DIM), jnp.float32)],
        compiler_params=params(32),
        cost_estimate=pl.CostEstimate(flops=2**10, bytes_accessed=2**10, transcendentals=0),
        name="fresh",
    )(guide_at, query[0], key_fresh[0], value_fresh[0])

    x, core = tensor // 2, tensor % 2
    chips = (x + jnp.arange(4, dtype=jnp.int32)) % 4
    near_places = (2 * chips + core).astype(jnp.int32)
    far_places = (2 * chips + 1 - core).astype(jnp.int32)
    blocks_shape = jax.ShapeDtypeStruct((4, width, width), jnp.bfloat16)
    weight_own, weight_sent = pl.pallas_call(
        pick_kernel,
        out_shape=[blocks_shape, blocks_shape],
        in_specs=[SMEM, SMEM, ANY],
        out_specs=[ANY, ANY],
        scratch_shapes=[
            pltpu.VMEM((8, width, width), jnp.bfloat16),
            pltpu.SemaphoreType.DMA((8,)),
            pltpu.SemaphoreType.DMA((8,)),
        ],
        compiler_params=params(48),
        cost_estimate=pl.CostEstimate(flops=0, bytes_accessed=2**10, transcendentals=0),
        name="pick",
    )(near_places, after(far_places, messages[ORDER[0]]), out_weight)

    def joined(pair, begin, count):
        return jnp.concatenate([arrived[slot][begin * rows : (begin + count) * rows] for slot in pair], axis=0)

    def work_on(queries, arrays, pair, own, part_arrays=None):
        work = []
        for slot, part in queries:
            places = []
            for a in part_arrays[part] if part_arrays else arrays:
                for i, other in enumerate(pair):
                    if a == own and other == slot:
                        continue
                    places.append((a, (4 * i + 2 * part if a in WHOLE else 2 * i) * rows))
            work.append((slot, part, QUERIES.index((slot, part)) * rows, tuple(places)))
        return tuple(work)

    arrived = {slot: to_slot(messages[slot], slot) for slot in PAIRS[0]}
    here, there = (arrived[slot] for slot in PAIRS[0])
    fresh_other = other_guide(fresh_send)
    stream_other = other_guide(stream_sent)
    here, there, fresh_other, stream_other, weight_sent = lax.optimization_barrier(
        (here, there, fresh_other, stream_other, weight_sent)
    )
    arrived = dict(zip(PAIRS[0], (here, there)))
    for slot in PAIRS[1]:
        arrived[slot] = to_slot(after(messages[slot], here, there), slot)
    early = joined(PAIRS[0], 0, 4)
    early_y, early_core = other_y(early), other_core(early)
    *pair, early_y, early_core = lax.optimization_barrier(
        (*(arrived[slot] for slot in PAIRS[1]), early_y, early_core)
    )
    arrived.update(zip(PAIRS[1], pair))
    arrays = {"early": early, "early_y": early_y, "early_core": early_core}
    own, last_own = joined(PAIRS[1], 0, 2), joined(PAIRS[1], 2, 2)
    arrays["own", 0], arrays["core", 0], over = own, other_core(own), other_y(own)
    arrays["early_y_core"] = other_core(early_y)
    first_work = work_on(QUERIES, ("early_core", "early", "early_y"), PAIRS[0], "early")
    state = stage(first_work, arrived, arrays, None)
    over, *state = lax.optimization_barrier((over, *state))
    over_core = other_core(over)
    state = stage(work_on(QUERIES, ("early_y_core",), PAIRS[0], None), arrived, arrays, state)
    over_core, last_own, *state = lax.optimization_barrier((over_core, last_own, *state))
    arrays["y", 0], arrays["y_core", 0] = over, over_core
    over = other_y(last_own)
    arrays["own", 1], arrays["core", 1], arrays["y", 1] = last_own, other_core(last_own), over
    arrays["y_core", 1] = other_core(over)
    arrays = {str(name): array for name, array in arrays.items()}

    def late(part, *names):
        return [str((name, part)) for name in names]

    own_main, core_main = late(0, "own", "core")
    parts = {0: [own_main, core_main]}
    rest = stage(work_on(QUERIES[:SLOTS], (), PAIRS[1], own_main, parts), arrived, arrays, state)
    parts = {0: late(0, "y", "y_core"), 1: late(1, "core", "own", "y", "y_core")}
    mine, its = [None] * SLOTS, [None] * SLOTS
    at, back = guide_at, None
    for slot, part in QUERIES[:SLOTS]:
        lot = ((0, 0), (0, 1)) if slot == 0 else ((slot, part),)
        work = work_on(lot, (), PAIRS[1], str(("own", 1)), parts)
        if slot == 0:
            tail = [part_of[SLOTS * rows :] for part_of in state]
            keep, send = stage(work, arrived, arrays, rest, at, tail)
        else:
            keep, send = stage(work, arrived, arrays, rest, at)
        if back is None:
            weight_other = other_core(after(weight_sent, keep))
        mine[slot], its[slot] = from_slot(keep, slot), from_slot_to_other_guide(send, slot)
        at = after(guide_at, keep, *([mine[back], its[back]] if back is not None else []))
        back = slot

    mixed = pl.pallas_call(
        combine_kernel,
        out_shape=jax.ShapeDtypeStruct((heads, half, HEAD_DIM), jnp.bfloat16),
        in_specs=[SMEM, SMEM] + [VMEM] * 10,
        out_specs=VMEM,
        compiler_params=params(32),
        name="combine",
    )(z, guide_at, *mine, fresh_keep, *its, fresh_other)

    share = jax.ShapeDtypeStruct((half, width), jnp.float32)
    sent = jax.ShapeDtypeStruct((half, width), jnp.bfloat16)
    shares = pl.pallas_call(
        project_kernel,
        out_shape=[share, sent, sent, sent],
        in_specs=[VMEM] * 4,
        out_specs=[VMEM] * 4,
        compiler_params=params(32),
        cost_estimate=pl.CostEstimate(
            flops=2 * half * width * width * 8, bytes_accessed=10 * 2**20, transcendentals=0
        ),
        name="project",
    )(mixed, other_core(mixed), weight_own, weight_other)
    term = shares[0]
    for s in range(1, 4):
        term = term + shift_x(shares[s], s).astype(jnp.float32)

    gate = lax.dynamic_index_in_dim(gate_table, step_index[0], 0, keepdims=False)
    near, far = stream_mine.astype(jnp.float32), stream_other.astype(jnp.float32)
    cond = jnp.where(guide == 0, near, far)
    uncond = jnp.where(guide == 0, far, near)
    guided = (uncond + guide_scale * (cond - uncond) + gate[None, :] * term).astype(jnp.bfloat16)
    own_cols = width // 2
    stays = lax.dynamic_slice_in_dim(guided, guide * own_cols, own_cols, 1)
    goes = lax.dynamic_slice_in_dim(guided, (1 - guide) * own_cols, own_cols, 1)
    got = other_guide(goes)
    return jnp.where(
        guide == 0, jnp.concatenate([stays, got], axis=0), jnp.concatenate([got, stays], axis=0)
    )


def solution(mesh):
    in_specs = (
        P("guide", "patch", "tensor"),
        P("guide", "patch", "tensor"),
        P("guide", "patch", "tensor"),
        P("guide", "patch", "tensor"),
        P("guide", "patch", "tensor"),
        P("tensor", None),
        P("guide", "patch", "tensor"),
        P(None, "tensor"),
        P(),
    )
    out_specs = P("patch", ("tensor", "guide"))
    return jax.shard_map(
        on_device, mesh=mesh, in_specs=in_specs, out_specs=out_specs, check_vma=False
    )
```

```python
import functools

import jax
import jax.numpy as jnp
from jax import lax
from jax.experimental import pallas as pl
from jax.experimental.pallas import tpu as pltpu
from jax.sharding import PartitionSpec as P

HEAD_DIM = 128
SLOTS = 4
RING = 8
ROWS = 512
HALF = ROWS // 2
BLOCK = HALF + 16
SCALE2 = 1.4426950408889634 / HEAD_DIM**0.5
SAFE_SUM = 2.0**100
VMEM = pl.BlockSpec(memory_space=pltpu.VMEM)
SMEM = pl.BlockSpec(memory_space=pltpu.SMEM)
ANY = pl.BlockSpec(memory_space=pl.ANY)
PLACE = ("patch", "tensor")
PAIRS = ((1, 3), (0, 2))
ORDER = PAIRS[0] + PAIRS[1]
WHOLE = ("early", "early_y", "early_core", "early_y_core")
QUERIES = ((1, 0), (3, 0), (2, 0), (0, 0), (0, 1))
ROW_BY_ROW = (((1,), (1,)), ((), ()))

guide_scale = 5.0


def params(mib):
    return pltpu.CompilerParams(vmem_limit_bytes=mib * 2**20)


def slot_pairs(slot, back):
    pairs = []
    for y in range(2):
        for z in range(RING):
            for x in range(4):
                for core in range(2):
                    there = SLOTS * core + (z + slot) % SLOTS
                    source = (y * RING + z) * 8 + x * 2 + core
                    target = (y * RING + there) * 8 + x * 2 + z // SLOTS
                    pairs.append((target, source) if back else (source, target))
    return pairs


def to_slot(value, slot):
    return lax.ppermute(value, PLACE, slot_pairs(slot, False))


def from_slot(value, slot):
    return lax.ppermute(value, PLACE, slot_pairs(slot, True))


def other_y(value):
    return lax.ppermute(value, "patch", [(i, (i + RING) % (2 * RING)) for i in range(2 * RING)])


def other_core(value):
    return lax.ppermute(value, "tensor", [(i, i ^ 1) for i in range(8)])


def other_guide(value):
    return lax.ppermute(value, "guide", [(0, 1), (1, 0)])


def shift_x(value, step):
    return lax.ppermute(value, "tensor", [(i, (i + 2 * step) % 8) for i in range(8)])


def scores(queries, keys):
    return lax.dot_general(queries, keys, ROW_BY_ROW, preferred_element_type=jnp.float32)


def lay_out(z_ref, query, key, value, *refs):
    messages, (held, loaded, stored, *buffers) = refs[:SLOTS], refs[SLOTS:]
    z = z_ref[0]
    loads = [pltpu.make_async_copy(src, held.at[i], loaded.at[i]) for i, src in enumerate((key, value, query))]
    for load in loads:
        load.start()
    for load in loads:
        load.wait()
    last = slice(SLOTS * HEAD_DIM, (SLOTS + 1) * HEAD_DIM)
    stores = []
    for slot in ORDER:
        message, buffer = messages[slot], buffers[slot]
        head = pl.ds(pl.multiple_of(lax.rem(z + slot, SLOTS) * HEAD_DIM, HEAD_DIM), HEAD_DIM)
        buffer[0:ROWS, :] = held[0, :, head]
        buffer[ROWS : 2 * ROWS, :] = held[1, :, head]
        buffer[2 * ROWS : 3 * ROWS, :] = held[0, :, last]
        buffer[3 * ROWS : 4 * ROWS, :] = held[1, :, last]
        buffer[4 * ROWS : 5 * ROWS, :] = held[2, :, head]
        if slot == 0:
            buffer[5 * ROWS : 6 * ROWS, :] = held[2, :, last]
        stores.append(pltpu.make_async_copy(buffer, message, stored.at[slot]))
        stores[-1].start()
    for store in stores:
        store.wait()


def with_ones(values):
    return jnp.concatenate([values, jnp.ones(values.shape, values.dtype)], axis=1)


def write_level(target, row, level_at, half):
    tile = HEAD_DIM
    lines = []
    for i in range(half * HALF // tile, (half + 1) * HALF // tile):
        lines.append(jnp.transpose(level_at[i * tile : (i + 1) * tile, :])[0:1, :])
    level = jnp.concatenate(lines, axis=0)
    high = level.astype(jnp.bfloat16).astype(jnp.float32)
    rest = level - high
    middle = rest.astype(jnp.bfloat16).astype(jnp.float32)
    rows = jnp.concatenate([high, middle, rest - middle, jnp.zeros((10, tile), jnp.float32)], axis=0)
    target[row : row + BLOCK - HALF, :] = rows.astype(jnp.bfloat16)


def write_halves(guide, row, attended, level_at, keep, send):
    for half in range(2):
        for mine, target in ((True, keep), (False, send)):

            @pl.when((guide == half) == mine)
            def _(half=half, target=target):
                target[row : row + HALF, :] = attended[half * HALF : (half + 1) * HALF, :]
                write_level(target, row + HALF, level_at, half)


def fresh_kernel(guide_ref, query, key, value, keep, send, attended, level_at):
    for h in range(query.shape[1] // HEAD_DIM):
        cols = slice(h * HEAD_DIM, (h + 1) * HEAD_DIM)
        score = scores(query[:, cols], key[:, cols])
        peak = jnp.max(score, axis=1, keepdims=True) * SCALE2
        weights = jnp.exp2(score * SCALE2 - peak).astype(jnp.bfloat16)
        both = jnp.dot(weights, with_ones(value[:, cols]), preferred_element_type=jnp.float32)
        total = both[:, HEAD_DIM:]
        attended[...] = (both[:, :HEAD_DIM] / total).astype(jnp.bfloat16)
        level_at[...] = peak + jnp.log2(total)
        write_halves(guide_ref[0], h * BLOCK, attended, level_at, keep, send)


def stage_kernel(work, first, last, with_tail, *refs):
    if last:
        guide_ref, *refs = refs
    slots = sorted({slot for slot, _, _, _ in work})
    arrays_used = sorted({a for _, _, _, places in work for a, _ in places})
    messages, refs = dict(zip(slots, refs)), refs[len(slots) :]
    arrays, refs = dict(zip(arrays_used, refs)), refs[len(arrays_used) :]
    if not first:
        (summed_in, stat_in), refs = refs[:2], refs[2:]
    if with_tail:
        (summed_tail, stat_tail), refs = refs[:2], refs[2:]
    if last:
        keep, send, attended, level_at, held = refs
    else:
        summed_out, stat_out, held = refs
    middle = HEAD_DIM // 2
    lane = lax.broadcasted_iota(jnp.int32, (HALF, HEAD_DIM), 1)

    def before(row, begin):
        summed, stat = summed_in, stat_in
        if with_tail and row == SLOTS * ROWS:
            row, summed, stat = 0, summed_tail, stat_tail
        span = pl.ds(row + begin, HALF)
        stat = stat[span, :]
        total = jnp.broadcast_to(stat[:, 0:1], stat.shape)
        return jnp.concatenate([summed[span, :], total], axis=1), stat[:, middle : middle + 1]

    def finish(row, n, begin, both, peak):
        total = both[:, HEAD_DIM:]
        if last:
            span = pl.ds(n * ROWS + begin, HALF)
            attended[span, :] = (both[:, :HEAD_DIM] / total).astype(jnp.bfloat16)
            level_at[span, :] = peak + jnp.log2(total)
        else:
            span = pl.ds(row + begin, HALF)
            summed_out[span, :] = both[:, :HEAD_DIM]
            stat_out[span, :] = jnp.where(lane < middle, total, peak)

    largest = None
    for n, (slot, part, row, places) in enumerate(work):
        for begin in (0, HALF):
            queries = messages[slot][(4 + part) * ROWS + begin : (4 + part) * ROWS + begin + HALF, :]
            both, peak = (None, None) if first else before(row, begin)
            for a, base in places:
                score = scores(queries, arrays[a][base : base + ROWS, :])
                if peak is None:
                    peak = jnp.max(score, axis=1, keepdims=True) * SCALE2
                weights = jnp.exp2(score * SCALE2 - peak).astype(jnp.bfloat16)
                values = arrays[a][base + ROWS : base + 2 * ROWS, :]
                more = jnp.dot(weights, with_ones(values), preferred_element_type=jnp.float32)
                both = more if both is None else both + more
            finish(row, n, begin, both, peak)
            largest = both[:, HEAD_DIM:] if largest is None else jnp.maximum(largest, both[:, HEAD_DIM:])

    @pl.when(jnp.logical_not(jnp.max(largest) < SAFE_SUM))
    def _():
        for n, (slot, part, row, places) in enumerate(work):
            for at, (a, base) in enumerate(places):
                held[at] = arrays[a][base : base + 2 * ROWS, :]

            def chunk_step(c, carry, n=n, slot=slot, part=part, row=row, count=len(places)):
                begin = pl.multiple_of(c * HALF, HALF)
                queries = messages[slot][pl.ds((4 + part) * ROWS + begin, HALF), :]

                def follow(at, state):
                    both, peak = state
                    score = scores(queries, held[at, :ROWS, :]) * SCALE2
                    higher = jnp.maximum(peak, jnp.max(score, axis=1, keepdims=True))
                    weights = jnp.exp2(score - higher).astype(jnp.bfloat16)
                    more = jnp.dot(weights, with_ones(held[at, ROWS:, :]), preferred_element_type=jnp.float32)
                    return both * jnp.exp2(peak - higher) + more, higher

                if first:
                    start = (jnp.zeros((HALF, 2 * HEAD_DIM), jnp.float32), jnp.full((HALF, 1), -1e30, jnp.float32))
                else:
                    start = before(row, begin)
                finish(row, n, begin, *lax.fori_loop(0, count, follow, start))
                return carry

            lax.fori_loop(0, 2, chunk_step, 0)

    if last:
        for n in range(len(work)):
            here = pl.ds(n * ROWS, ROWS)
            write_halves(guide_ref[0], n * BLOCK, attended.at[here, :], level_at.at[here, :], keep, send)


def stage(work, messages, arrays, state, guide=None, tail=()):
    first, last = state is None, guide is not None
    slots = sorted({slot for slot, _, _, _ in work})
    arrays_used = sorted({a for _, _, _, places in work for a, _ in places})
    operands = [guide] if last else []
    operands += [messages[s] for s in slots] + [arrays[a] for a in arrays_used] + ([] if first else list(state)) + list(tail)
    lines = len(work) * ROWS
    if last:
        out_shape = [jax.ShapeDtypeStruct((len(work) * BLOCK, HEAD_DIM), jnp.bfloat16)] * 2
    else:
        out_shape = [jax.ShapeDtypeStruct((lines, HEAD_DIM), jnp.float32)] * 2
    scratch = [pltpu.VMEM((max(len(places) for _, _, _, places in work), 2 * ROWS, HEAD_DIM), jnp.bfloat16)]
    if last:
        scratch = [pltpu.VMEM((lines, HEAD_DIM), jnp.bfloat16), pltpu.VMEM((lines, HEAD_DIM), jnp.float32)] + scratch
    units = sum(len(places) for _, _, _, places in work)
    return pl.pallas_call(
        functools.partial(stage_kernel, work, first, last, len(tail) > 0),
        out_shape=out_shape,
        in_specs=([SMEM] if last else []) + [VMEM] * (len(operands) - last),
        out_specs=[VMEM] * len(out_shape),
        scratch_shapes=scratch,
        compiler_params=params(32),
        cost_estimate=pl.CostEstimate(
            flops=units * ROWS * ROWS * 4 * HEAD_DIM * 4,
            bytes_accessed=9 * 2**20,
            transcendentals=units * ROWS * ROWS,
        ),
        name="stage",
    )(*operands)


def combine_kernel(z_ref, guide_ref, *refs):
    came, (fresh_own, fresh_other, out) = refs[:SLOTS], refs[SLOTS:]
    z = z_ref[0]
    first = guide_ref[0] == 0
    factors = (
        jnp.where(first, guide_scale, 1.0 - guide_scale),
        jnp.where(first, 1.0 - guide_scale, guide_scale),
    )
    tile = HEAD_DIM
    todo = [(s, 0, lax.rem(z + s, SLOTS)) for s in range(SLOTS)] + [(0, BLOCK, SLOTS)]

    def level_of(ref, start):
        stat = ref[pl.ds(start, BLOCK - HALF), :].astype(jnp.float32)
        level = stat[0:2, :] + stat[2:4, :] + stat[4:6, :]
        return [jnp.transpose(jnp.broadcast_to(level[i : i + 1, :], (tile, tile))) for i in range(HALF // tile)]

    for s, row, head in todo:
        at = pl.multiple_of(head * BLOCK, BLOCK - HALF)
        mixed = None
        for side, (fresh, factor) in enumerate(zip((fresh_own, fresh_other), factors)):
            start = side * (came[s].shape[0] // 2) + row
            there = jnp.concatenate(level_of(came[s], start + HALF), axis=0)
            here = jnp.concatenate(level_of(fresh, at + HALF), axis=0)
            share = 1.0 / (1.0 + jnp.exp2(here - there))
            old = came[s][start : start + HALF, :].astype(jnp.float32)
            new = fresh[pl.ds(at, HALF), :].astype(jnp.float32)
            joined = (new + (old - new) * share) * factor
            mixed = joined if mixed is None else mixed + joined
        out[head] = mixed.astype(jnp.bfloat16)


def pick_kernel(near_ref, far_ref, weight, near, far, buffer, loaded, stored):
    width = weight.shape[0]
    loads, stores = [], []
    for i, (places, target) in enumerate(((far_ref, far), (near_ref, near))):
        for s in range(4):
            cols = pl.ds(pl.multiple_of(places[s] * width, width), width)
            at = 4 * i + s
            loads.append(pltpu.make_async_copy(weight.at[:, cols], buffer.at[at], loaded.at[at]))
            stores.append(pltpu.make_async_copy(buffer.at[at], target.at[s], stored.at[at]))
    for load in loads:
        load.start()
    for load, store in zip(loads, stores):
        load.wait()
        store.start()
    for store in stores:
        store.wait()


def project_kernel(own, other, weight, other_weight, out0, out1, out2, out3):
    mine = jnp.concatenate([own[h] for h in range(own.shape[0])], axis=1)
    its = jnp.concatenate([other[h] for h in range(own.shape[0])], axis=1)
    for s, out in ((1, out1), (2, out2), (3, out3), (0, out0)):
        share = jnp.dot(mine, weight[s], preferred_element_type=jnp.float32)
        share = share + jnp.dot(its, other_weight[s], preferred_element_type=jnp.float32)
        out[...] = share.astype(out.dtype)


def on_device(
    query,
    key_fresh,
    value_fresh,
    key_stale,
    value_stale,
    out_weight,
    stream,
    gate_table,
    step_index,
):
    rows, width = query.shape[1:]
    heads = width // HEAD_DIM
    half = rows // 2
    patch = lax.axis_index("patch")
    tensor = lax.axis_index("tensor")
    guide = lax.axis_index("guide")
    z = (patch % RING).astype(jnp.int32).reshape(1)
    guide_at = guide.astype(jnp.int32).reshape(1)

    def after(value, *others):
        return lax.optimization_barrier((value, *others))[0]

    sizes = [(6 if s == 0 else 5) * rows for s in range(SLOTS)]
    messages = pl.pallas_call(
        lay_out,
        out_shape=[jax.ShapeDtypeStruct((size, HEAD_DIM), jnp.bfloat16) for size in sizes],
        in_specs=[SMEM] + [ANY] * 3,
        out_specs=[ANY] * SLOTS,
        scratch_shapes=[
            pltpu.VMEM((3, rows, width), jnp.bfloat16),
            pltpu.SemaphoreType.DMA((3,)),
            pltpu.SemaphoreType.DMA((SLOTS,)),
        ]
        + [pltpu.VMEM((size, HEAD_DIM), jnp.bfloat16) for size in sizes],
        compiler_params=params(58),
        name="lay_out",
    )(z, query[0], key_stale[0], value_stale[0])

    stream_mine = lax.dynamic_slice_in_dim(stream[0], guide * half, half, 0)
    stream_sent = lax.dynamic_slice_in_dim(stream[0], (1 - guide) * half, half, 0)

    fresh_shape = jax.ShapeDtypeStruct((heads * BLOCK, HEAD_DIM), jnp.bfloat16)
    fresh_keep, fresh_send = pl.pallas_call(
        fresh_kernel,
        out_shape=[fresh_shape, fresh_shape],
        in_specs=[SMEM] + [VMEM] * 3,
        out_specs=[VMEM] * 2,
        scratch_shapes=[pltpu.VMEM((rows, HEAD_DIM), jnp.bfloat16), pltpu.VMEM((rows, HEAD_DIM), jnp.float32)],
        compiler_params=params(32),
        cost_estimate=pl.CostEstimate(flops=2**10, bytes_accessed=2**10, transcendentals=0),
        name="fresh",
    )(guide_at, query[0], key_fresh[0], value_fresh[0])

    x, core = tensor // 2, tensor % 2
    chips = (x + jnp.arange(4, dtype=jnp.int32)) % 4
    near_places = (2 * chips + core).astype(jnp.int32)
    far_places = (2 * chips + 1 - core).astype(jnp.int32)
    blocks_shape = jax.ShapeDtypeStruct((4, width, width), jnp.bfloat16)
    weight_own, weight_sent = pl.pallas_call(
        pick_kernel,
        out_shape=[blocks_shape, blocks_shape],
        in_specs=[SMEM, SMEM, ANY],
        out_specs=[ANY, ANY],
        scratch_shapes=[
            pltpu.VMEM((8, width, width), jnp.bfloat16),
            pltpu.SemaphoreType.DMA((8,)),
            pltpu.SemaphoreType.DMA((8,)),
        ],
        compiler_params=params(48),
        cost_estimate=pl.CostEstimate(flops=0, bytes_accessed=2**10, transcendentals=0),
        name="pick",
    )(near_places, after(far_places, messages[ORDER[0]]), out_weight)

    def joined(pair, begin, count):
        return jnp.concatenate([arrived[slot][begin * rows : (begin + count) * rows] for slot in pair], axis=0)

    def work_on(queries, arrays, pair, own, part_arrays=None):
        work = []
        for slot, part in queries:
            places = []
            for a in part_arrays[part] if part_arrays else arrays:
                for i, other in enumerate(pair):
                    if a == own and other == slot:
                        continue
                    places.append((a, (4 * i + 2 * part if a in WHOLE else 2 * i) * rows))
            work.append((slot, part, QUERIES.index((slot, part)) * rows, tuple(places)))
        return tuple(work)

    arrived = {slot: to_slot(messages[slot], slot) for slot in PAIRS[0]}
    here, there = (arrived[slot] for slot in PAIRS[0])
    fresh_other = other_guide(fresh_send)
    stream_other = other_guide(stream_sent)
    here, there, fresh_other, stream_other, weight_sent = lax.optimization_barrier(
        (here, there, fresh_other, stream_other, weight_sent)
    )
    arrived = dict(zip(PAIRS[0], (here, there)))
    for slot in PAIRS[1]:
        arrived[slot] = to_slot(after(messages[slot], here, there), slot)
    early = joined(PAIRS[0], 0, 4)
    early_y, early_core = other_y(early), other_core(early)
    *pair, early_y, early_core = lax.optimization_barrier(
        (*(arrived[slot] for slot in PAIRS[1]), early_y, early_core)
    )
    arrived.update(zip(PAIRS[1], pair))
    arrays = {"early": early, "early_y": early_y, "early_core": early_core}
    own, last_own = joined(PAIRS[1], 0, 2), joined(PAIRS[1], 2, 2)
    arrays["own", 0], arrays["core", 0], over = own, other_core(own), other_y(own)
    arrays["early_y_core"] = other_core(early_y)
    first_work = work_on(QUERIES, ("early_core", "early", "early_y"), PAIRS[0], "early")
    state = stage(first_work, arrived, arrays, None)
    over, *state = lax.optimization_barrier((over, *state))
    over_core, last_over = other_core(over), other_y(after(last_own, over))
    state = stage(work_on(QUERIES, ("early_y_core",), PAIRS[0], None), arrived, arrays, state)
    over_core, *state = lax.optimization_barrier((over_core, *state))
    arrays["y", 0], arrays["y_core", 0] = over, over_core
    arrays["own", 1], arrays["core", 1] = last_own, other_core(after(last_own, state[0]))
    arrays = {str(name): array for name, array in arrays.items()}

    def late(part, *names):
        return [str((name, part)) for name in names]

    own_main, core_main = late(0, "own", "core")
    parts = {0: [own_main, core_main]}
    rest = stage(work_on(QUERIES[:SLOTS], (), PAIRS[1], own_main, parts), arrived, arrays, state)
    last_over, *rest = lax.optimization_barrier((last_over, *rest))
    last = late(1, "core", "own", "y", "y_core")
    arrays[last[2]], arrays[last[3]] = last_over, other_core(last_over)
    parts = {0: late(0, "y", "y_core"), 1: last}
    came = [None] * SLOTS
    tail = [part_of[SLOTS * rows :] for part_of in state]
    at = guide_at
    for lot, more in ((QUERIES[:3], ()), (QUERIES[3:], tail)):
        work = work_on(lot, (), PAIRS[1], last[1], parts)
        keep, send = stage(work, arrived, arrays, rest, at, more)
        got = other_guide(send)
        blocks = 2 if more else 1
        for n, slot in enumerate(dict(lot)):
            span = slice(n * BLOCK, (n + blocks) * BLOCK)
            came[slot] = from_slot(jnp.concatenate([keep[span], got[span]], axis=0), slot)
        at = after(guide_at, keep)
        if not more:
            weight_other = other_core(after(weight_sent, keep))

    mixed = pl.pallas_call(
        combine_kernel,
        out_shape=jax.ShapeDtypeStruct((heads, half, HEAD_DIM), jnp.bfloat16),
        in_specs=[SMEM, SMEM] + [VMEM] * 6,
        out_specs=VMEM,
        compiler_params=params(32),
        name="combine",
    )(z, guide_at, *came, fresh_keep, fresh_other)

    share = jax.ShapeDtypeStruct((half, width), jnp.float32)
    sent = jax.ShapeDtypeStruct((half, width), jnp.bfloat16)
    shares = pl.pallas_call(
        project_kernel,
        out_shape=[share, sent, sent, sent],
        in_specs=[VMEM] * 4,
        out_specs=[VMEM] * 4,
        compiler_params=params(32),
        cost_estimate=pl.CostEstimate(
            flops=2 * half * width * width * 8, bytes_accessed=10 * 2**20, transcendentals=0
        ),
        name="project",
    )(mixed, other_core(mixed), weight_own, weight_other)
    term = shares[0]
    for s in range(1, 4):
        term = term + shift_x(shares[s], s).astype(jnp.float32)

    gate = lax.dynamic_index_in_dim(gate_table, step_index[0], 0, keepdims=False)
    near, far = stream_mine.astype(jnp.float32), stream_other.astype(jnp.float32)
    cond = jnp.where(guide == 0, near, far)
    uncond = jnp.where(guide == 0, far, near)
    guided = (uncond + guide_scale * (cond - uncond) + gate[None, :] * term).astype(jnp.bfloat16)
    own_cols = width // 2
    stays = lax.dynamic_slice_in_dim(guided, guide * own_cols, own_cols, 1)
    goes = lax.dynamic_slice_in_dim(guided, (1 - guide) * own_cols, own_cols, 1)
    got = other_guide(goes)
    return jnp.where(
        guide == 0, jnp.concatenate([stays, got], axis=0), jnp.concatenate([got, stays], axis=0)
    )


def solution(mesh):
    in_specs = (
        P("guide", "patch", "tensor"),
        P("guide", "patch", "tensor"),
        P("guide", "patch", "tensor"),
        P("guide", "patch", "tensor"),
        P("guide", "patch", "tensor"),
        P("tensor", None),
        P("guide", "patch", "tensor"),
        P(None, "tensor"),
        P(),
    )
    out_specs = P("patch", ("tensor", "guide"))
    return jax.shard_map(
        on_device, mesh=mesh, in_specs=in_specs, out_specs=out_specs, check_vma=False
    )
```

```python
import functools

import jax
import jax.numpy as jnp
from jax import lax
from jax.experimental import pallas as pl
from jax.experimental.pallas import tpu as pltpu
from jax.sharding import PartitionSpec as P

HEAD_DIM = 128
SLOTS = 4
RING = 8
ROWS = 512
HALF = ROWS // 2
BLOCK = HALF + 16
SCALE2 = 1.4426950408889634 / HEAD_DIM**0.5
SAFE_SUM = 2.0**100
VMEM = pl.BlockSpec(memory_space=pltpu.VMEM)
SMEM = pl.BlockSpec(memory_space=pltpu.SMEM)
ANY = pl.BlockSpec(memory_space=pl.ANY)
PLACE = ("patch", "tensor")
PAIRS = ((1, 3), (0, 2))
ORDER = PAIRS[0] + PAIRS[1]
WHOLE = ("early", "early_y", "early_core", "early_y_core")
QUERIES = ((1, 0), (3, 0), (2, 0), (0, 0), (0, 1))
ROW_BY_ROW = (((1,), (1,)), ((), ()))
SMALL = pl.CostEstimate(flops=2**10, bytes_accessed=2**10, transcendentals=0)

guide_scale = 5.0


def params(mib):
    return pltpu.CompilerParams(vmem_limit_bytes=mib * 2**20)


def slot_pairs(slot, back):
    pairs = []
    for y in range(2):
        for z in range(RING):
            for x in range(4):
                for core in range(2):
                    there = SLOTS * core + (z + slot) % SLOTS
                    source = (y * RING + z) * 8 + x * 2 + core
                    target = (y * RING + there) * 8 + x * 2 + z // SLOTS
                    pairs.append((target, source) if back else (source, target))
    return pairs


def to_slot(value, slot):
    return lax.ppermute(value, PLACE, slot_pairs(slot, False))


def from_slot(value, slot):
    return lax.ppermute(value, PLACE, slot_pairs(slot, True))


def other_y(value):
    return lax.ppermute(value, "patch", [(i, (i + RING) % (2 * RING)) for i in range(2 * RING)])


def other_core(value):
    return lax.ppermute(value, "tensor", [(i, i ^ 1) for i in range(8)])


def other_guide(value):
    return lax.ppermute(value, "guide", [(0, 1), (1, 0)])


def shift_x(value, step):
    return lax.ppermute(value, "tensor", [(i, (i + 2 * step) % 8) for i in range(8)])


def scores(queries, keys):
    return lax.dot_general(queries, keys, ROW_BY_ROW, preferred_element_type=jnp.float32)


def lay_out(z_ref, query, key, value, *refs):
    messages, (held, loaded, stored, *buffers) = refs[:SLOTS], refs[SLOTS:]
    z = z_ref[0]
    loads = [pltpu.make_async_copy(src, held.at[i], loaded.at[i]) for i, src in enumerate((key, value, query))]
    for load in loads:
        load.start()
    for load in loads:
        load.wait()
    last = slice(SLOTS * HEAD_DIM, (SLOTS + 1) * HEAD_DIM)
    stores = []
    for slot in ORDER:
        message, buffer = messages[slot], buffers[slot]
        head = pl.ds(pl.multiple_of(lax.rem(z + slot, SLOTS) * HEAD_DIM, HEAD_DIM), HEAD_DIM)
        buffer[0:ROWS, :] = held[0, :, head]
        buffer[ROWS : 2 * ROWS, :] = held[1, :, head]
        buffer[2 * ROWS : 3 * ROWS, :] = held[0, :, last]
        buffer[3 * ROWS : 4 * ROWS, :] = held[1, :, last]
        buffer[4 * ROWS : 5 * ROWS, :] = held[2, :, head]
        if slot == 0:
            buffer[5 * ROWS : 6 * ROWS, :] = held[2, :, last]
        stores.append(pltpu.make_async_copy(buffer, message, stored.at[slot]))
        stores[-1].start()
    for store in stores:
        store.wait()


def with_ones(values):
    return jnp.concatenate([values, jnp.ones(values.shape, values.dtype)], axis=1)


def write_level(target, row, level_at, half):
    tile = HEAD_DIM
    lines = []
    for i in range(half * HALF // tile, (half + 1) * HALF // tile):
        lines.append(jnp.transpose(level_at[i * tile : (i + 1) * tile, :])[0:1, :])
    level = jnp.concatenate(lines, axis=0)
    high = level.astype(jnp.bfloat16).astype(jnp.float32)
    rest = level - high
    middle = rest.astype(jnp.bfloat16).astype(jnp.float32)
    rows = jnp.concatenate([high, middle, rest - middle, jnp.zeros((10, tile), jnp.float32)], axis=0)
    target[row : row + BLOCK - HALF, :] = rows.astype(jnp.bfloat16)


def write_halves(guide, row, attended, level_at, keep, send):
    for half in range(2):
        for mine, target in ((True, keep), (False, send)):

            @pl.when((guide == half) == mine)
            def _(half=half, target=target):
                target[row : row + HALF, :] = attended[half * HALF : (half + 1) * HALF, :]
                write_level(target, row + HALF, level_at, half)


def fresh_kernel(guide_ref, query, key, value, keep, send, attended, level_at):
    for h in range(query.shape[1] // HEAD_DIM):
        cols = slice(h * HEAD_DIM, (h + 1) * HEAD_DIM)
        score = scores(query[:, cols], key[:, cols])
        peak = jnp.max(score, axis=1, keepdims=True) * SCALE2
        weights = jnp.exp2(score * SCALE2 - peak).astype(jnp.bfloat16)
        both = jnp.dot(weights, with_ones(value[:, cols]), preferred_element_type=jnp.float32)
        total = both[:, HEAD_DIM:]
        attended[...] = (both[:, :HEAD_DIM] / total).astype(jnp.bfloat16)
        level_at[...] = peak + jnp.log2(total)
        write_halves(guide_ref[0], h * BLOCK, attended, level_at, keep, send)


def stage_kernel(work, first, last, with_tail, *refs):
    if last:
        guide_ref, *refs = refs
    slots = sorted({slot for slot, _, _, _ in work})
    arrays_used = sorted({a for _, _, _, places in work for a, _ in places})
    messages, refs = dict(zip(slots, refs)), refs[len(slots) :]
    arrays, refs = dict(zip(arrays_used, refs)), refs[len(arrays_used) :]
    if not first:
        (summed_in, stat_in), refs = refs[:2], refs[2:]
    if with_tail:
        (summed_tail, stat_tail), refs = refs[:2], refs[2:]
    if last:
        keep, send, attended, level_at, held = refs
    else:
        summed_out, stat_out, held = refs
    middle = HEAD_DIM // 2
    lane = lax.broadcasted_iota(jnp.int32, (HALF, HEAD_DIM), 1)

    def before(row, begin):
        summed, stat = summed_in, stat_in
        if with_tail and row == SLOTS * ROWS:
            row, summed, stat = 0, summed_tail, stat_tail
        span = pl.ds(row + begin, HALF)
        stat = stat[span, :]
        total = jnp.broadcast_to(stat[:, 0:1], stat.shape)
        return jnp.concatenate([summed[span, :], total], axis=1), stat[:, middle : middle + 1]

    def finish(row, n, begin, both, peak):
        total = both[:, HEAD_DIM:]
        if last:
            span = pl.ds(n * ROWS + begin, HALF)
            attended[span, :] = (both[:, :HEAD_DIM] / total).astype(jnp.bfloat16)
            level_at[span, :] = peak + jnp.log2(total)
        else:
            span = pl.ds(row + begin, HALF)
            summed_out[span, :] = both[:, :HEAD_DIM]
            stat_out[span, :] = jnp.where(lane < middle, total, peak)

    largest = None
    for n, (slot, part, row, places) in enumerate(work):
        for begin in (0, HALF):
            queries = messages[slot][(4 + part) * ROWS + begin : (4 + part) * ROWS + begin + HALF, :]
            both, peak = (None, None) if first else before(row, begin)
            for a, base in places:
                score = scores(queries, arrays[a][base : base + ROWS, :])
                if peak is None:
                    peak = jnp.max(score, axis=1, keepdims=True) * SCALE2
                weights = jnp.exp2(score * SCALE2 - peak).astype(jnp.bfloat16)
                values = arrays[a][base + ROWS : base + 2 * ROWS, :]
                more = jnp.dot(weights, with_ones(values), preferred_element_type=jnp.float32)
                both = more if both is None else both + more
            finish(row, n, begin, both, peak)
            largest = both[:, HEAD_DIM:] if largest is None else jnp.maximum(largest, both[:, HEAD_DIM:])

    @pl.when(jnp.logical_not(jnp.max(largest) < SAFE_SUM))
    def _():
        for n, (slot, part, row, places) in enumerate(work):
            for at, (a, base) in enumerate(places):
                held[at] = arrays[a][base : base + 2 * ROWS, :]

            def chunk_step(c, carry, n=n, slot=slot, part=part, row=row, count=len(places)):
                begin = pl.multiple_of(c * HALF, HALF)
                queries = messages[slot][pl.ds((4 + part) * ROWS + begin, HALF), :]

                def follow(at, state):
                    both, peak = state
                    score = scores(queries, held[at, :ROWS, :]) * SCALE2
                    higher = jnp.maximum(peak, jnp.max(score, axis=1, keepdims=True))
                    weights = jnp.exp2(score - higher).astype(jnp.bfloat16)
                    more = jnp.dot(weights, with_ones(held[at, ROWS:, :]), preferred_element_type=jnp.float32)
                    return both * jnp.exp2(peak - higher) + more, higher

                if first:
                    start = (jnp.zeros((HALF, 2 * HEAD_DIM), jnp.float32), jnp.full((HALF, 1), -1e30, jnp.float32))
                else:
                    start = before(row, begin)
                finish(row, n, begin, *lax.fori_loop(0, count, follow, start))
                return carry

            lax.fori_loop(0, 2, chunk_step, 0)

    if last:
        for n in range(len(work)):
            here = pl.ds(n * ROWS, ROWS)
            write_halves(guide_ref[0], n * BLOCK, attended.at[here, :], level_at.at[here, :], keep, send)


def stage(work, messages, arrays, state, guide=None, tail=()):
    first, last = state is None, guide is not None
    slots = sorted({slot for slot, _, _, _ in work})
    arrays_used = sorted({a for _, _, _, places in work for a, _ in places})
    operands = [guide] if last else []
    operands += [messages[s] for s in slots] + [arrays[a] for a in arrays_used] + ([] if first else list(state)) + list(tail)
    lines = len(work) * ROWS
    if last:
        out_shape = [jax.ShapeDtypeStruct((len(work) * BLOCK, HEAD_DIM), jnp.bfloat16)] * 2
    else:
        out_shape = [jax.ShapeDtypeStruct((lines, HEAD_DIM), jnp.float32)] * 2
    scratch = [pltpu.VMEM((max(len(places) for _, _, _, places in work), 2 * ROWS, HEAD_DIM), jnp.bfloat16)]
    if last:
        scratch = [pltpu.VMEM((lines, HEAD_DIM), jnp.bfloat16), pltpu.VMEM((lines, HEAD_DIM), jnp.float32)] + scratch
    return pl.pallas_call(
        functools.partial(stage_kernel, work, first, last, len(tail) > 0),
        out_shape=out_shape,
        in_specs=([SMEM] if last else []) + [VMEM] * (len(operands) - last),
        out_specs=[VMEM] * len(out_shape),
        scratch_shapes=scratch,
        compiler_params=params(32),
        cost_estimate=SMALL,
        name="stage",
    )(*operands)


def combine_kernel(z_ref, guide_ref, *refs):
    came, (fresh_own, fresh_other, out) = refs[:SLOTS], refs[SLOTS:]
    z = z_ref[0]
    first = guide_ref[0] == 0
    factors = (
        jnp.where(first, guide_scale, 1.0 - guide_scale),
        jnp.where(first, 1.0 - guide_scale, guide_scale),
    )
    tile = HEAD_DIM
    todo = [(s, 0, lax.rem(z + s, SLOTS)) for s in range(SLOTS)] + [(0, BLOCK, SLOTS)]

    def level_of(ref, start):
        stat = ref[pl.ds(start, BLOCK - HALF), :].astype(jnp.float32)
        level = stat[0:2, :] + stat[2:4, :] + stat[4:6, :]
        return [jnp.transpose(jnp.broadcast_to(level[i : i + 1, :], (tile, tile))) for i in range(HALF // tile)]

    for s, row, head in todo:
        at = pl.multiple_of(head * BLOCK, BLOCK - HALF)
        mixed = None
        for side, (fresh, factor) in enumerate(zip((fresh_own, fresh_other), factors)):
            start = side * (came[s].shape[0] // 2) + row
            there = jnp.concatenate(level_of(came[s], start + HALF), axis=0)
            here = jnp.concatenate(level_of(fresh, at + HALF), axis=0)
            share = 1.0 / (1.0 + jnp.exp2(here - there))
            old = came[s][start : start + HALF, :].astype(jnp.float32)
            new = fresh[pl.ds(at, HALF), :].astype(jnp.float32)
            joined = (new + (old - new) * share) * factor
            mixed = joined if mixed is None else mixed + joined
        out[head] = mixed.astype(jnp.bfloat16)


def pick_kernel(near_ref, far_ref, weight, near, far, buffer, loaded, stored):
    width = weight.shape[0]
    loads, stores = [], []
    for i, (places, target) in enumerate(((far_ref, far), (near_ref, near))):
        for s in range(4):
            cols = pl.ds(pl.multiple_of(places[s] * width, width), width)
            at = 4 * i + s
            loads.append(pltpu.make_async_copy(weight.at[:, cols], buffer.at[at], loaded.at[at]))
            stores.append(pltpu.make_async_copy(buffer.at[at], target.at[s], stored.at[at]))
    for load in loads:
        load.start()
    for load, store in zip(loads, stores):
        load.wait()
        store.start()
    for store in stores:
        store.wait()


def project_kernel(own, other, weight, other_weight, out0, out1, out2, out3):
    mine = jnp.concatenate([own[h] for h in range(own.shape[0])], axis=1)
    its = jnp.concatenate([other[h] for h in range(own.shape[0])], axis=1)
    for s, out in ((1, out1), (2, out2), (3, out3), (0, out0)):
        share = jnp.dot(mine, weight[s], preferred_element_type=jnp.float32)
        share = share + jnp.dot(its, other_weight[s], preferred_element_type=jnp.float32)
        out[...] = share.astype(out.dtype)


def on_device(
    query,
    key_fresh,
    value_fresh,
    key_stale,
    value_stale,
    out_weight,
    stream,
    gate_table,
    step_index,
):
    rows, width = query.shape[1:]
    heads = width // HEAD_DIM
    half = rows // 2
    patch = lax.axis_index("patch")
    tensor = lax.axis_index("tensor")
    guide = lax.axis_index("guide")
    z = (patch % RING).astype(jnp.int32).reshape(1)
    guide_at = guide.astype(jnp.int32).reshape(1)

    def after(value, *others):
        return lax.optimization_barrier((value, *others))[0]

    sizes = [(6 if s == 0 else 5) * rows for s in range(SLOTS)]
    messages = pl.pallas_call(
        lay_out,
        out_shape=[jax.ShapeDtypeStruct((size, HEAD_DIM), jnp.bfloat16) for size in sizes],
        in_specs=[SMEM] + [ANY] * 3,
        out_specs=[ANY] * SLOTS,
        scratch_shapes=[
            pltpu.VMEM((3, rows, width), jnp.bfloat16),
            pltpu.SemaphoreType.DMA((3,)),
            pltpu.SemaphoreType.DMA((SLOTS,)),
        ]
        + [pltpu.VMEM((size, HEAD_DIM), jnp.bfloat16) for size in sizes],
        compiler_params=params(58),
        name="lay_out",
    )(z, query[0], key_stale[0], value_stale[0])

    stream_mine = lax.dynamic_slice_in_dim(stream[0], guide * half, half, 0)
    stream_sent = lax.dynamic_slice_in_dim(stream[0], (1 - guide) * half, half, 0)

    fresh_shape = jax.ShapeDtypeStruct((heads * BLOCK, HEAD_DIM), jnp.bfloat16)
    fresh_keep, fresh_send = pl.pallas_call(
        fresh_kernel,
        out_shape=[fresh_shape, fresh_shape],
        in_specs=[SMEM] + [VMEM] * 3,
        out_specs=[VMEM] * 2,
        scratch_shapes=[pltpu.VMEM((rows, HEAD_DIM), jnp.bfloat16), pltpu.VMEM((rows, HEAD_DIM), jnp.float32)],
        compiler_params=params(32),
        cost_estimate=SMALL,
        name="fresh",
    )(guide_at, query[0], key_fresh[0], value_fresh[0])

    x, core = tensor // 2, tensor % 2
    chips = (x + jnp.arange(4, dtype=jnp.int32)) % 4
    near_places = (2 * chips + core).astype(jnp.int32)
    far_places = (2 * chips + 1 - core).astype(jnp.int32)
    blocks_shape = jax.ShapeDtypeStruct((4, width, width), jnp.bfloat16)
    weight_own, weight_sent = pl.pallas_call(
        pick_kernel,
        out_shape=[blocks_shape, blocks_shape],
        in_specs=[SMEM, SMEM, ANY],
        out_specs=[ANY, ANY],
        scratch_shapes=[
            pltpu.VMEM((8, width, width), jnp.bfloat16),
            pltpu.SemaphoreType.DMA((8,)),
            pltpu.SemaphoreType.DMA((8,)),
        ],
        compiler_params=params(48),
        cost_estimate=SMALL,
        name="pick",
    )(near_places, after(far_places, messages[ORDER[0]]), out_weight)

    def joined(pair, begin, count):
        return jnp.concatenate([arrived[slot][begin * rows : (begin + count) * rows] for slot in pair], axis=0)

    def work_on(queries, arrays, pair, own, part_arrays=None):
        work = []
        for slot, part in queries:
            places = []
            for a in part_arrays[part] if part_arrays else arrays:
                for i, other in enumerate(pair):
                    if a == own and other == slot:
                        continue
                    places.append((a, (4 * i + 2 * part if a in WHOLE else 2 * i) * rows))
            work.append((slot, part, QUERIES.index((slot, part)) * rows, tuple(places)))
        return tuple(work)

    early_slots, last_slot = ORDER[:3], ORDER[3]
    arrived = {slot: to_slot(messages[slot], slot) for slot in early_slots}
    fresh_other = other_guide(fresh_send)
    stream_other = other_guide(stream_sent)
    *some, fresh_other, stream_other, weight_sent, message = lax.optimization_barrier(
        (*(arrived[slot] for slot in early_slots), fresh_other, stream_other, weight_sent, messages[last_slot])
    )
    arrived = dict(zip(early_slots, some))
    arrived[last_slot] = to_slot(message, last_slot)
    early = joined(PAIRS[0], 0, 4)
    early_y, early_core = other_y(early), other_core(early)
    arrived[last_slot], early_y, early_core = lax.optimization_barrier((arrived[last_slot], early_y, early_core))
    arrays = {"early": early, "early_y": early_y, "early_core": early_core}
    own, last_own = joined(PAIRS[1], 0, 2), joined(PAIRS[1], 2, 2)
    arrays["own", 0], arrays["core", 0], over = own, other_core(own), other_y(own)
    arrays["early_y_core"] = other_core(early_y)
    first_work = work_on(QUERIES, ("early_core", "early", "early_y"), PAIRS[0], "early")
    state = stage(first_work, arrived, arrays, None)
    over, *state = lax.optimization_barrier((over, *state))
    over_core, last_over = other_core(over), other_y(after(last_own, over))
    state = stage(work_on(QUERIES, ("early_y_core",), PAIRS[0], None), arrived, arrays, state)
    over_core, *state = lax.optimization_barrier((over_core, *state))
    arrays["y", 0], arrays["y_core", 0] = over, over_core
    arrays["own", 1], arrays["core", 1] = last_own, other_core(after(last_own, state[0]))
    arrays = {str(name): array for name, array in arrays.items()}

    def late(part, *names):
        return [str((name, part)) for name in names]

    own_main, core_main = late(0, "own", "core")
    parts = {0: [own_main, core_main]}
    rest = stage(work_on(QUERIES[:SLOTS], (), PAIRS[1], own_main, parts), arrived, arrays, state)
    last = late(1, "core", "own", "y", "y_core")
    parts = {0: late(0, "y", "y_core"), 1: last}
    came = [None] * SLOTS
    tail = [part_of[SLOTS * rows :] for part_of in state]
    at = guide_at
    for lot, more in ((QUERIES[:3], ()), (QUERIES[3:], tail)):
        work = work_on(lot, (), PAIRS[1], last[1], parts)
        keep, send = stage(work, arrived, arrays, rest, at, more)
        got = other_guide(send)
        blocks = 2 if more else 1
        for n, slot in enumerate(dict(lot)):
            span = slice(n * BLOCK, (n + blocks) * BLOCK)
            if more:
                got = after(got, *(came[other] for other, _ in QUERIES[:3]))
            came[slot] = from_slot(jnp.concatenate([keep[span], got[span]], axis=0), slot)
        at = after(guide_at, keep)
        if not more:
            last_over = after(last_over, keep)
            arrays[last[2]], arrays[last[3]] = last_over, other_core(last_over)
    weight_other = other_core(after(weight_sent, at))

    mixed = pl.pallas_call(
        combine_kernel,
        out_shape=jax.ShapeDtypeStruct((heads, half, HEAD_DIM), jnp.bfloat16),
        in_specs=[SMEM, SMEM] + [VMEM] * 6,
        out_specs=VMEM,
        compiler_params=params(32),
        name="combine",
    )(z, guide_at, *came, fresh_keep, fresh_other)

    share = jax.ShapeDtypeStruct((half, width), jnp.float32)
    sent = jax.ShapeDtypeStruct((half, width), jnp.bfloat16)
    shares = pl.pallas_call(
        project_kernel,
        out_shape=[share, sent, sent, sent],
        in_specs=[VMEM] * 4,
        out_specs=[VMEM] * 4,
        compiler_params=params(32),
        cost_estimate=SMALL,
        name="project",
    )(mixed, other_core(mixed), weight_own, weight_other)
    term = shares[0]
    for s in range(1, 4):
        term = term + shift_x(shares[s], s).astype(jnp.float32)

    gate = lax.dynamic_index_in_dim(gate_table, step_index[0], 0, keepdims=False)
    near, far = stream_mine.astype(jnp.float32), stream_other.astype(jnp.float32)
    cond = jnp.where(guide == 0, near, far)
    uncond = jnp.where(guide == 0, far, near)
    guided = (uncond + guide_scale * (cond - uncond) + gate[None, :] * term).astype(jnp.bfloat16)
    own_cols = width // 2
    stays = lax.dynamic_slice_in_dim(guided, guide * own_cols, own_cols, 1)
    goes = lax.dynamic_slice_in_dim(guided, (1 - guide) * own_cols, own_cols, 1)
    got = other_guide(goes)
    return jnp.where(
        guide == 0, jnp.concatenate([stays, got], axis=0), jnp.concatenate([got, stays], axis=0)
    )


def solution(mesh):
    in_specs = (
        P("guide", "patch", "tensor"),
        P("guide", "patch", "tensor"),
        P("guide", "patch", "tensor"),
        P("guide", "patch", "tensor"),
        P("guide", "patch", "tensor"),
        P("tensor", None),
        P("guide", "patch", "tensor"),
        P(None, "tensor"),
        P(),
    )
    out_specs = P("patch", ("tensor", "guide"))
    return jax.shard_map(
        on_device, mesh=mesh, in_specs=in_specs, out_specs=out_specs, check_vma=False
    )
```

```python
import functools

import jax
import jax.numpy as jnp
from jax import lax
from jax.experimental import pallas as pl
from jax.experimental.pallas import tpu as pltpu
from jax.sharding import PartitionSpec as P

HEAD_DIM = 128
SLOTS = 4
RING = 8
ROWS = 512
HALF = ROWS // 2
BLOCK = ROWS + 16
SCALE2 = 1.4426950408889634 / HEAD_DIM**0.5
SAFE_SUM = 2.0**100
VMEM = pl.BlockSpec(memory_space=pltpu.VMEM)
SMEM = pl.BlockSpec(memory_space=pltpu.SMEM)
ANY = pl.BlockSpec(memory_space=pl.ANY)
PLACE = ("patch", "tensor")
PAIRS = ((1, 3), (0, 2))
ORDER = PAIRS[0] + PAIRS[1]
WHOLE = ("early", "early_y", "early_core", "early_y_core")
QUERIES = ((1, 0), (3, 0), (2, 0), (0, 0), (0, 1))
ROW_BY_ROW = (((1,), (1,)), ((), ()))
SMALL = pl.CostEstimate(flops=2**10, bytes_accessed=2**10, transcendentals=0)

guide_scale = 5.0


def params(mib):
    return pltpu.CompilerParams(vmem_limit_bytes=mib * 2**20)


def slot_pairs(slot, back):
    pairs = []
    for y in range(2):
        for z in range(RING):
            for x in range(4):
                for core in range(2):
                    there = SLOTS * core + (z + slot) % SLOTS
                    source = (y * RING + z) * 8 + x * 2 + core
                    target = (y * RING + there) * 8 + x * 2 + z // SLOTS
                    pairs.append((target, source) if back else (source, target))
    return pairs


def to_slot(value, slot):
    return lax.ppermute(value, PLACE, slot_pairs(slot, False))


def from_slot(value, slot):
    return lax.ppermute(value, PLACE, slot_pairs(slot, True))


def other_y(value):
    return lax.ppermute(value, "patch", [(i, (i + RING) % (2 * RING)) for i in range(2 * RING)])


def other_core(value):
    return lax.ppermute(value, "tensor", [(i, i ^ 1) for i in range(8)])


def other_guide(value):
    return lax.ppermute(value, "guide", [(0, 1), (1, 0)])


def shift_x(value, step):
    return lax.ppermute(value, "tensor", [(i, (i + 2 * step) % 8) for i in range(8)])


def scores(queries, keys):
    return lax.dot_general(queries, keys, ROW_BY_ROW, preferred_element_type=jnp.float32)


def lay_out(z_ref, query, key, value, *refs):
    messages, (held, loaded, stored, *buffers) = refs[:SLOTS], refs[SLOTS:]
    z = z_ref[0]
    loads = [pltpu.make_async_copy(src, held.at[i], loaded.at[i]) for i, src in enumerate((key, value, query))]
    for load in loads:
        load.start()
    for load in loads:
        load.wait()
    last = slice(SLOTS * HEAD_DIM, (SLOTS + 1) * HEAD_DIM)
    stores = []
    for slot in ORDER:
        message, buffer = messages[slot], buffers[slot]
        head = pl.ds(pl.multiple_of(lax.rem(z + slot, SLOTS) * HEAD_DIM, HEAD_DIM), HEAD_DIM)
        buffer[0:ROWS, :] = held[0, :, head]
        buffer[ROWS : 2 * ROWS, :] = held[1, :, head]
        buffer[2 * ROWS : 3 * ROWS, :] = held[0, :, last]
        buffer[3 * ROWS : 4 * ROWS, :] = held[1, :, last]
        buffer[4 * ROWS : 5 * ROWS, :] = held[2, :, head]
        if slot == 0:
            buffer[5 * ROWS : 6 * ROWS, :] = held[2, :, last]
        stores.append(pltpu.make_async_copy(buffer, message, stored.at[slot]))
        stores[-1].start()
    for store in stores:
        store.wait()


def with_ones(values):
    return jnp.concatenate([values, jnp.ones(values.shape, values.dtype)], axis=1)


def write_block(target, row, attended, level_at):
    target[row : row + ROWS, :] = attended
    tile = HEAD_DIM
    lines = [jnp.transpose(level_at[i * tile : (i + 1) * tile, :])[0:1, :] for i in range(ROWS // tile)]
    level = jnp.concatenate(lines, axis=0)
    high = level.astype(jnp.bfloat16).astype(jnp.float32)
    rest = level - high
    middle = rest.astype(jnp.bfloat16).astype(jnp.float32)
    rows = jnp.concatenate([high, middle, rest - middle, jnp.zeros_like(level)], axis=0)
    target[row + ROWS : row + BLOCK, :] = rows.astype(jnp.bfloat16)


def fresh_kernel(query, key, value, out):
    for h in range(query.shape[1] // HEAD_DIM):
        cols = slice(h * HEAD_DIM, (h + 1) * HEAD_DIM)
        score = scores(query[:, cols], key[:, cols])
        peak = jnp.max(score, axis=1, keepdims=True) * SCALE2
        weights = jnp.exp2(score * SCALE2 - peak).astype(jnp.bfloat16)
        both = jnp.dot(weights, with_ones(value[:, cols]), preferred_element_type=jnp.float32)
        total = both[:, HEAD_DIM:]
        attended = (both[:, :HEAD_DIM] / total).astype(jnp.bfloat16)
        write_block(out, h * BLOCK, attended, peak + jnp.log2(total))


def stage_kernel(work, first, last, with_tail, *refs):
    slots = sorted({slot for slot, _, _, _ in work})
    arrays_used = sorted({a for _, _, _, places in work for a, _ in places})
    messages, refs = dict(zip(slots, refs)), refs[len(slots) :]
    arrays, refs = dict(zip(arrays_used, refs)), refs[len(arrays_used) :]
    if not first:
        (summed_in, stat_in), refs = refs[:2], refs[2:]
    if with_tail:
        (summed_tail, stat_tail), refs = refs[:2], refs[2:]
    if last:
        outs, (attended, level_at, held) = refs[: len(slots)], refs[len(slots) :]
    else:
        summed_out, stat_out, held = refs
    middle = HEAD_DIM // 2
    lane = lax.broadcasted_iota(jnp.int32, (HALF, HEAD_DIM), 1)

    def before(row, begin):
        summed, stat = summed_in, stat_in
        if with_tail and row == SLOTS * ROWS:
            row, summed, stat = 0, summed_tail, stat_tail
        span = pl.ds(row + begin, HALF)
        stat = stat[span, :]
        total = jnp.broadcast_to(stat[:, 0:1], stat.shape)
        return jnp.concatenate([summed[span, :], total], axis=1), stat[:, middle : middle + 1]

    def finish(row, n, begin, both, peak):
        total = both[:, HEAD_DIM:]
        if last:
            span = pl.ds(n * ROWS + begin, HALF)
            attended[span, :] = (both[:, :HEAD_DIM] / total).astype(jnp.bfloat16)
            level_at[span, :] = peak + jnp.log2(total)
        else:
            span = pl.ds(row + begin, HALF)
            summed_out[span, :] = both[:, :HEAD_DIM]
            stat_out[span, :] = jnp.where(lane < middle, total, peak)

    largest = None
    for n, (slot, part, row, places) in enumerate(work):
        for begin in (0, HALF):
            queries = messages[slot][(4 + part) * ROWS + begin : (4 + part) * ROWS + begin + HALF, :]
            both, peak = (None, None) if first else before(row, begin)
            for a, base in places:
                score = scores(queries, arrays[a][base : base + ROWS, :])
                if peak is None:
                    peak = jnp.max(score, axis=1, keepdims=True) * SCALE2
                weights = jnp.exp2(score * SCALE2 - peak).astype(jnp.bfloat16)
                values = arrays[a][base + ROWS : base + 2 * ROWS, :]
                more = jnp.dot(weights, with_ones(values), preferred_element_type=jnp.float32)
                both = more if both is None else both + more
            finish(row, n, begin, both, peak)
            largest = both[:, HEAD_DIM:] if largest is None else jnp.maximum(largest, both[:, HEAD_DIM:])

    @pl.when(jnp.logical_not(jnp.max(largest) < SAFE_SUM))
    def _():
        for n, (slot, part, row, places) in enumerate(work):
            for at, (a, base) in enumerate(places):
                held[at] = arrays[a][base : base + 2 * ROWS, :]

            def chunk_step(c, carry, n=n, slot=slot, part=part, row=row, count=len(places)):
                begin = pl.multiple_of(c * HALF, HALF)
                queries = messages[slot][pl.ds((4 + part) * ROWS + begin, HALF), :]

                def follow(at, state):
                    both, peak = state
                    score = scores(queries, held[at, :ROWS, :]) * SCALE2
                    higher = jnp.maximum(peak, jnp.max(score, axis=1, keepdims=True))
                    weights = jnp.exp2(score - higher).astype(jnp.bfloat16)
                    more = jnp.dot(weights, with_ones(held[at, ROWS:, :]), preferred_element_type=jnp.float32)
                    return both * jnp.exp2(peak - higher) + more, higher

                if first:
                    start = (jnp.zeros((HALF, 2 * HEAD_DIM), jnp.float32), jnp.full((HALF, 1), -1e30, jnp.float32))
                else:
                    start = before(row, begin)
                finish(row, n, begin, *lax.fori_loop(0, count, follow, start))
                return carry

            lax.fori_loop(0, 2, chunk_step, 0)

    if last:
        for n, (slot, part, _, _) in enumerate(work):
            here = slice(n * ROWS, (n + 1) * ROWS)
            write_block(outs[slots.index(slot)], part * BLOCK, attended[here, :], level_at.at[n * ROWS : (n + 1) * ROWS, :])


def stage(work, messages, arrays, state, last=False, tail=()):
    first = state is None
    slots = sorted({slot for slot, _, _, _ in work})
    arrays_used = sorted({a for _, _, _, places in work for a, _ in places})
    operands = [messages[s] for s in slots] + [arrays[a] for a in arrays_used] + ([] if first else list(state)) + list(tail)
    lines = len(work) * ROWS
    if last:
        blocks = [sum(slot == other for other, _, _, _ in work) for slot in slots]
        out_shape = [jax.ShapeDtypeStruct((count * BLOCK, HEAD_DIM), jnp.bfloat16) for count in blocks]
    else:
        out_shape = [jax.ShapeDtypeStruct((lines, HEAD_DIM), jnp.float32)] * 2
    scratch = [pltpu.VMEM((max(len(places) for _, _, _, places in work), 2 * ROWS, HEAD_DIM), jnp.bfloat16)]
    if last:
        scratch = [pltpu.VMEM((lines, HEAD_DIM), jnp.bfloat16), pltpu.VMEM((lines, HEAD_DIM), jnp.float32)] + scratch
    return pl.pallas_call(
        functools.partial(stage_kernel, work, first, last, len(tail) > 0),
        out_shape=out_shape,
        in_specs=[VMEM] * len(operands),
        out_specs=[VMEM] * len(out_shape),
        scratch_shapes=scratch,
        compiler_params=params(32),
        cost_estimate=SMALL,
        name="stage",
    )(*operands)


def combine_kernel(z_ref, guide_ref, r0, r1, r2, r3, fresh, keep, send):
    z, guide = z_ref[0], guide_ref[0]
    tile = HEAD_DIM
    todo = [(r, 0, lax.rem(z + s, SLOTS)) for s, r in enumerate((r0, r1, r2, r3))] + [(r0, BLOCK, SLOTS)]

    def levels(ref, start):
        stat = ref[pl.ds(start, BLOCK - ROWS), :].astype(jnp.float32)
        level = stat[0:4, :] + stat[4:8, :] + stat[8:12, :]
        return [jnp.transpose(jnp.broadcast_to(level[i : i + 1, :], (tile, tile))) for i in range(ROWS // tile)]

    for came, row, head in todo:
        at = pl.multiple_of(head * BLOCK, BLOCK - ROWS)
        there = jnp.concatenate(levels(came, row + ROWS), axis=0)
        here = jnp.concatenate(levels(fresh, at + ROWS), axis=0)
        share = 1.0 / (1.0 + jnp.exp2(here - there))
        old = came[row : row + ROWS, :].astype(jnp.float32)
        new = fresh[pl.ds(at, ROWS), :].astype(jnp.float32)
        joined = (new + (old - new) * share).astype(jnp.bfloat16)
        for half in range(2):
            rows = joined[half * HALF : (half + 1) * HALF, :]
            for mine, target in ((True, keep), (False, send)):

                @pl.when((guide == half) == mine)
                def _(rows=rows, target=target, head=head):
                    target[head] = rows


def pick_kernel(near_ref, far_ref, weight, near, far, buffer, loaded, stored):
    width = weight.shape[0]
    loads, stores = [], []
    for i, (places, target) in enumerate(((far_ref, far), (near_ref, near))):
        for s in range(4):
            cols = pl.ds(pl.multiple_of(places[s] * width, width), width)
            at = 4 * i + s
            loads.append(pltpu.make_async_copy(weight.at[:, cols], buffer.at[at], loaded.at[at]))
            stores.append(pltpu.make_async_copy(buffer.at[at], target.at[s], stored.at[at]))
    for load in loads:
        load.start()
    for load, store in zip(loads, stores):
        load.wait()
        store.start()
    for store in stores:
        store.wait()


def project_kernel(guide_ref, own, other, far_own, far_other, weight, far_weight, out0, out1, out2, out3):
    first = guide_ref[0] == 0
    by_own = jnp.where(first, guide_scale, 1.0 - guide_scale)
    by_other = jnp.where(first, 1.0 - guide_scale, guide_scale)

    def mixed(own, other):
        heads = [own[h].astype(jnp.float32) * by_own + other[h].astype(jnp.float32) * by_other for h in range(own.shape[0])]
        return jnp.concatenate([head.astype(jnp.bfloat16) for head in heads], axis=1)

    mine, its = mixed(own, other), mixed(far_own, far_other)
    for s, out in ((1, out1), (2, out2), (3, out3), (0, out0)):
        share = jnp.dot(mine, weight[s], preferred_element_type=jnp.float32)
        share = share + jnp.dot(its, far_weight[s], preferred_element_type=jnp.float32)
        out[...] = share.astype(out.dtype)


def on_device(
    query,
    key_fresh,
    value_fresh,
    key_stale,
    value_stale,
    out_weight,
    stream,
    gate_table,
    step_index,
):
    rows, width = query.shape[1:]
    heads = width // HEAD_DIM
    half = rows // 2
    patch = lax.axis_index("patch")
    tensor = lax.axis_index("tensor")
    guide = lax.axis_index("guide")
    z = (patch % RING).astype(jnp.int32).reshape(1)
    guide_at = guide.astype(jnp.int32).reshape(1)

    def after(value, *others):
        return lax.optimization_barrier((value, *others))[0]

    sizes = [(6 if s == 0 else 5) * rows for s in range(SLOTS)]
    messages = pl.pallas_call(
        lay_out,
        out_shape=[jax.ShapeDtypeStruct((size, HEAD_DIM), jnp.bfloat16) for size in sizes],
        in_specs=[SMEM] + [ANY] * 3,
        out_specs=[ANY] * SLOTS,
        scratch_shapes=[
            pltpu.VMEM((3, rows, width), jnp.bfloat16),
            pltpu.SemaphoreType.DMA((3,)),
            pltpu.SemaphoreType.DMA((SLOTS,)),
        ]
        + [pltpu.VMEM((size, HEAD_DIM), jnp.bfloat16) for size in sizes],
        compiler_params=params(58),
        name="lay_out",
    )(z, query[0], key_stale[0], value_stale[0])

    stream_mine = lax.dynamic_slice_in_dim(stream[0], guide * half, half, 0)
    stream_sent = lax.dynamic_slice_in_dim(stream[0], (1 - guide) * half, half, 0)

    fresh_shape = jax.ShapeDtypeStruct((heads * BLOCK, HEAD_DIM), jnp.bfloat16)
    fresh = pl.pallas_call(
        fresh_kernel,
        out_shape=fresh_shape,
        in_specs=[VMEM] * 3,
        out_specs=VMEM,
        compiler_params=params(32),
        cost_estimate=SMALL,
        name="fresh",
    )(query[0], key_fresh[0], value_fresh[0])

    x, core = tensor // 2, tensor % 2
    chips = (x + jnp.arange(4, dtype=jnp.int32)) % 4
    near_places = (2 * chips + core).astype(jnp.int32)
    far_places = (2 * chips + 1 - core).astype(jnp.int32)
    blocks_shape = jax.ShapeDtypeStruct((4, width, width), jnp.bfloat16)
    weight_own, weight_sent = pl.pallas_call(
        pick_kernel,
        out_shape=[blocks_shape, blocks_shape],
        in_specs=[SMEM, SMEM, ANY],
        out_specs=[ANY, ANY],
        scratch_shapes=[
            pltpu.VMEM((8, width, width), jnp.bfloat16),
            pltpu.SemaphoreType.DMA((8,)),
            pltpu.SemaphoreType.DMA((8,)),
        ],
        compiler_params=params(48),
        cost_estimate=SMALL,
        name="pick",
    )(near_places, after(far_places, messages[ORDER[0]]), out_weight)

    def joined(pair, begin, count):
        return jnp.concatenate([arrived[slot][begin * rows : (begin + count) * rows] for slot in pair], axis=0)

    def work_on(queries, arrays, pair, own, part_arrays=None):
        work = []
        for slot, part in queries:
            places = []
            for a in part_arrays[part] if part_arrays else arrays:
                for i, other in enumerate(pair):
                    if a == own and other == slot:
                        continue
                    places.append((a, (4 * i + 2 * part if a in WHOLE else 2 * i) * rows))
            work.append((slot, part, QUERIES.index((slot, part)) * rows, tuple(places)))
        return tuple(work)

    arrived = {slot: to_slot(messages[slot], slot) for slot in PAIRS[0]}
    stream_other = other_guide(stream_sent)
    here, there, fresh, stream_other, weight_sent, *rest = lax.optimization_barrier(
        (*arrived.values(), fresh, stream_other, weight_sent, *(messages[slot] for slot in PAIRS[1]))
    )
    arrived = dict(zip(PAIRS[0], (here, there)))
    for slot, message in zip(PAIRS[1], rest):
        arrived[slot] = to_slot(message, slot)
    early = joined(PAIRS[0], 0, 4)
    early_y, early_core = other_y(early), other_core(early)
    *pair, early_y, early_core = lax.optimization_barrier(
        (*(arrived[slot] for slot in PAIRS[1]), early_y, early_core)
    )
    arrived.update(zip(PAIRS[1], pair))
    arrays = {"early": early, "early_y": early_y, "early_core": early_core}
    own, last_own = joined(PAIRS[1], 0, 2), joined(PAIRS[1], 2, 2)
    arrays["own", 0], arrays["core", 0], over = own, other_core(own), other_y(own)
    arrays["early_y_core"] = other_core(early_y)
    first_work = work_on(QUERIES, ("early_core", "early", "early_y"), PAIRS[0], "early")
    state = stage(first_work, arrived, arrays, None)
    over, *state = lax.optimization_barrier((over, *state))
    over_core, last_over = other_core(over), other_y(after(last_own, over))
    state = stage(work_on(QUERIES, ("early_y_core",), PAIRS[0], None), arrived, arrays, state)
    over_core, *state = lax.optimization_barrier((over_core, *state))
    arrays["y", 0], arrays["y_core", 0] = over, over_core
    arrays["own", 1], arrays["core", 1] = last_own, other_core(after(last_own, state[0]))
    arrays = {str(name): array for name, array in arrays.items()}

    def late(part, *names):
        return [str((name, part)) for name in names]

    own_main, core_main = late(0, "own", "core")
    parts = {0: [own_main, core_main]}
    rest = stage(work_on(QUERIES[:SLOTS], (), PAIRS[1], own_main, parts), arrived, arrays, state)
    last = late(1, "core", "own", "y", "y_core")
    parts = {0: late(0, "y", "y_core"), 1: last}
    came = [None] * SLOTS
    tail = [part_of[SLOTS * rows :] for part_of in state]
    lot = QUERIES[:3]
    outs = stage(work_on(lot, (), PAIRS[1], last[1], parts), arrived, arrays, rest, True)
    for slot, out in zip(sorted(dict(lot)), outs):
        came[slot] = from_slot(out, slot)
    last_over = after(last_over, outs[0])
    arrays[last[2]], arrays[last[3]] = last_over, other_core(last_over)
    (out,) = stage(work_on(QUERIES[3:], (), PAIRS[1], last[1], parts), arrived, arrays, rest, True, tail)
    weight_other = other_core(weight_sent)
    came[0] = from_slot(out, 0)

    att_shape = jax.ShapeDtypeStruct((heads, half, HEAD_DIM), jnp.bfloat16)
    keep, send = pl.pallas_call(
        combine_kernel,
        out_shape=[att_shape, att_shape],
        in_specs=[SMEM, SMEM] + [VMEM] * 5,
        out_specs=[VMEM] * 2,
        compiler_params=params(32),
        cost_estimate=SMALL,
        name="combine",
    )(z, guide_at, *came, fresh)
    other = other_guide(send)

    share = jax.ShapeDtypeStruct((half, width), jnp.float32)
    sent = jax.ShapeDtypeStruct((half, width), jnp.bfloat16)
    shares = pl.pallas_call(
        project_kernel,
        out_shape=[share, sent, sent, sent],
        in_specs=[SMEM] + [VMEM] * 6,
        out_specs=[VMEM] * 4,
        compiler_params=params(32),
        cost_estimate=SMALL,
        name="project",
    )(guide_at, keep, other, other_core(keep), other_core(other), weight_own, weight_other)
    term = shares[0]
    for s in range(1, 4):
        term = term + shift_x(shares[s], s).astype(jnp.float32)

    gate = lax.dynamic_index_in_dim(gate_table, step_index[0], 0, keepdims=False)
    near, far = stream_mine.astype(jnp.float32), stream_other.astype(jnp.float32)
    cond = jnp.where(guide == 0, near, far)
    uncond = jnp.where(guide == 0, far, near)
    guided = (uncond + guide_scale * (cond - uncond) + gate[None, :] * term).astype(jnp.bfloat16)
    own_cols = width // 2
    stays = lax.dynamic_slice_in_dim(guided, guide * own_cols, own_cols, 1)
    goes = lax.dynamic_slice_in_dim(guided, (1 - guide) * own_cols, own_cols, 1)
    got = other_guide(goes)
    return jnp.where(
        guide == 0, jnp.concatenate([stays, got], axis=0), jnp.concatenate([got, stays], axis=0)
    )


def solution(mesh):
    in_specs = (
        P("guide", "patch", "tensor"),
        P("guide", "patch", "tensor"),
        P("guide", "patch", "tensor"),
        P("guide", "patch", "tensor"),
        P("guide", "patch", "tensor"),
        P("tensor", None),
        P("guide", "patch", "tensor"),
        P(None, "tensor"),
        P(),
    )
    out_specs = P("patch", ("tensor", "guide"))
    return jax.shard_map(
        on_device, mesh=mesh, in_specs=in_specs, out_specs=out_specs, check_vma=False
    )
```

```python
import functools

import jax
import jax.numpy as jnp
from jax import lax
from jax.experimental import pallas as pl
from jax.experimental.pallas import tpu as pltpu
from jax.sharding import PartitionSpec as P

HEAD_DIM = 128
SLOTS = 4
RING = 8
ROWS = 512
HALF = ROWS // 2
BLOCK = ROWS + 16
SCALE2 = 1.4426950408889634 / HEAD_DIM**0.5
SAFE_SUM = 2.0**100
VMEM = pl.BlockSpec(memory_space=pltpu.VMEM)
SMEM = pl.BlockSpec(memory_space=pltpu.SMEM)
ANY = pl.BlockSpec(memory_space=pl.ANY)
PLACE = ("patch", "tensor")
PAIRS = ((1, 3), (0, 2))
ORDER = PAIRS[0] + PAIRS[1]
WHOLE = ("early_core", "early", "early_y", "early_y_core")
QUERIES = ((1, 0), (3, 0), (2, 0), (0, 0), (0, 1))
ROW_BY_ROW = (((1,), (1,)), ((), ()))
SMALL = pl.CostEstimate(flops=2**10, bytes_accessed=2**10, transcendentals=0)

guide_scale = 5.0


def params(mib):
    return pltpu.CompilerParams(vmem_limit_bytes=mib * 2**20)


def slot_pairs(slot, back):
    pairs = []
    for y in range(2):
        for z in range(RING):
            for x in range(4):
                for core in range(2):
                    there = SLOTS * core + (z + slot) % SLOTS
                    source = (y * RING + z) * 8 + x * 2 + core
                    target = (y * RING + there) * 8 + x * 2 + z // SLOTS
                    pairs.append((target, source) if back else (source, target))
    return pairs


def to_slot(value, slot):
    return lax.ppermute(value, PLACE, slot_pairs(slot, False))


def from_slot(value, slot):
    return lax.ppermute(value, PLACE, slot_pairs(slot, True))


def other_y(value):
    return lax.ppermute(value, "patch", [(i, (i + RING) % (2 * RING)) for i in range(2 * RING)])


def other_core(value):
    return lax.ppermute(value, "tensor", [(i, i ^ 1) for i in range(8)])


def other_guide(value):
    return lax.ppermute(value, "guide", [(0, 1), (1, 0)])


def shift_x(value, step):
    return lax.ppermute(value, "tensor", [(i, (i + 2 * step) % 8) for i in range(8)])


def scores(queries, keys):
    return lax.dot_general(queries, keys, ROW_BY_ROW, preferred_element_type=jnp.float32)


def lay_out(z_ref, query, key, value, *refs):
    messages, (held, loaded, stored, *buffers) = refs[:SLOTS], refs[SLOTS:]
    z = z_ref[0]
    loads = [pltpu.make_async_copy(src, held.at[i], loaded.at[i]) for i, src in enumerate((key, value, query))]
    for load in loads:
        load.start()
    for load in loads:
        load.wait()
    last = slice(SLOTS * HEAD_DIM, (SLOTS + 1) * HEAD_DIM)
    stores = []
    for slot in ORDER:
        message, buffer = messages[slot], buffers[slot]
        head = pl.ds(pl.multiple_of(lax.rem(z + slot, SLOTS) * HEAD_DIM, HEAD_DIM), HEAD_DIM)
        buffer[0:ROWS, :] = held[0, :, head]
        buffer[ROWS : 2 * ROWS, :] = held[1, :, head]
        buffer[2 * ROWS : 3 * ROWS, :] = held[0, :, last]
        buffer[3 * ROWS : 4 * ROWS, :] = held[1, :, last]
        buffer[4 * ROWS : 5 * ROWS, :] = held[2, :, head]
        if slot == 0:
            buffer[5 * ROWS : 6 * ROWS, :] = held[2, :, last]
        stores.append(pltpu.make_async_copy(buffer, message, stored.at[slot]))
        stores[-1].start()
    for store in stores:
        store.wait()


def with_ones(values):
    return jnp.concatenate([values, jnp.ones(values.shape, values.dtype)], axis=1)


def write_block(target, row, attended, level_at):
    target[row : row + ROWS, :] = attended
    tile = HEAD_DIM
    lines = [jnp.transpose(level_at[i * tile : (i + 1) * tile, :])[0:1, :] for i in range(ROWS // tile)]
    level = jnp.concatenate(lines, axis=0)
    high = level.astype(jnp.bfloat16).astype(jnp.float32)
    rest = level - high
    middle = rest.astype(jnp.bfloat16).astype(jnp.float32)
    rows = jnp.concatenate([high, middle, rest - middle, jnp.zeros_like(level)], axis=0)
    target[row + ROWS : row + BLOCK, :] = rows.astype(jnp.bfloat16)


def fresh_kernel(query, key, value, out):
    for h in range(query.shape[1] // HEAD_DIM):
        cols = slice(h * HEAD_DIM, (h + 1) * HEAD_DIM)
        score = scores(query[:, cols], key[:, cols])
        peak = jnp.max(score, axis=1, keepdims=True) * SCALE2
        weights = jnp.exp2(score * SCALE2 - peak).astype(jnp.bfloat16)
        both = jnp.dot(weights, with_ones(value[:, cols]), preferred_element_type=jnp.float32)
        total = both[:, HEAD_DIM:]
        attended = (both[:, :HEAD_DIM] / total).astype(jnp.bfloat16)
        write_block(out, h * BLOCK, attended, peak + jnp.log2(total))


def stage_kernel(work, first, last, with_tail, *refs):
    slots = sorted({slot for slot, _, _, _ in work})
    arrays_used = sorted({a for _, _, _, places in work for a, _ in places})
    messages, refs = dict(zip(slots, refs)), refs[len(slots) :]
    arrays, refs = dict(zip(arrays_used, refs)), refs[len(arrays_used) :]
    if not first:
        (summed_in, stat_in), refs = refs[:2], refs[2:]
    if with_tail:
        (summed_tail, stat_tail), refs = refs[:2], refs[2:]
    if last:
        outs, (attended, level_at, held) = refs[: len(work)], refs[len(work) :]
    else:
        summed_out, stat_out, held = refs
    middle = HEAD_DIM // 2
    lane = lax.broadcasted_iota(jnp.int32, (HALF, HEAD_DIM), 1)

    def before(row, begin):
        summed, stat = summed_in, stat_in
        if with_tail and row == SLOTS * ROWS:
            row, summed, stat = 0, summed_tail, stat_tail
        span = pl.ds(row + begin, HALF)
        stat = stat[span, :]
        total = jnp.broadcast_to(stat[:, 0:1], stat.shape)
        return jnp.concatenate([summed[span, :], total], axis=1), stat[:, middle : middle + 1]

    def finish(row, n, begin, both, peak):
        total = both[:, HEAD_DIM:]
        if last:
            span = pl.ds(n * ROWS + begin, HALF)
            attended[span, :] = (both[:, :HEAD_DIM] / total).astype(jnp.bfloat16)
            level_at[span, :] = peak + jnp.log2(total)
        else:
            span = pl.ds(row + begin, HALF)
            summed_out[span, :] = both[:, :HEAD_DIM]
            stat_out[span, :] = jnp.where(lane < middle, total, peak)

    largest = None
    for n, (slot, part, row, places) in enumerate(work):
        for begin in (0, HALF):
            queries = messages[slot][(4 + part) * ROWS + begin : (4 + part) * ROWS + begin + HALF, :]
            both, peak = (None, None) if first else before(row, begin)
            for a, base in places:
                score = scores(queries, arrays[a][base : base + ROWS, :])
                if peak is None:
                    peak = jnp.max(score, axis=1, keepdims=True) * SCALE2
                weights = jnp.exp2(score * SCALE2 - peak).astype(jnp.bfloat16)
                values = arrays[a][base + ROWS : base + 2 * ROWS, :]
                more = jnp.dot(weights, with_ones(values), preferred_element_type=jnp.float32)
                both = more if both is None else both + more
            finish(row, n, begin, both, peak)
            largest = both[:, HEAD_DIM:] if largest is None else jnp.maximum(largest, both[:, HEAD_DIM:])

    @pl.when(jnp.logical_not(jnp.max(largest) < SAFE_SUM))
    def _():
        for n, (slot, part, row, places) in enumerate(work):
            for at, (a, base) in enumerate(places):
                held[at] = arrays[a][base : base + 2 * ROWS, :]

            def chunk_step(c, carry, n=n, slot=slot, part=part, row=row, count=len(places)):
                begin = pl.multiple_of(c * HALF, HALF)
                queries = messages[slot][pl.ds((4 + part) * ROWS + begin, HALF), :]

                def follow(at, state):
                    both, peak = state
                    score = scores(queries, held[at, :ROWS, :]) * SCALE2
                    higher = jnp.maximum(peak, jnp.max(score, axis=1, keepdims=True))
                    weights = jnp.exp2(score - higher).astype(jnp.bfloat16)
                    more = jnp.dot(weights, with_ones(held[at, ROWS:, :]), preferred_element_type=jnp.float32)
                    return both * jnp.exp2(peak - higher) + more, higher

                if first:
                    start = (jnp.zeros((HALF, 2 * HEAD_DIM), jnp.float32), jnp.full((HALF, 1), -1e30, jnp.float32))
                else:
                    start = before(row, begin)
                finish(row, n, begin, *lax.fori_loop(0, count, follow, start))
                return carry

            lax.fori_loop(0, 2, chunk_step, 0)

    if last:
        for n, out in enumerate(outs):
            here = slice(n * ROWS, (n + 1) * ROWS)
            write_block(out, 0, attended[here, :], level_at.at[n * ROWS : (n + 1) * ROWS, :])


def stage(work, messages, arrays, state, last=False, tail=()):
    first = state is None
    slots = sorted({slot for slot, _, _, _ in work})
    arrays_used = sorted({a for _, _, _, places in work for a, _ in places})
    operands = [messages[s] for s in slots] + [arrays[a] for a in arrays_used] + ([] if first else list(state)) + list(tail)
    lines = len(work) * ROWS
    if last:
        out_shape = [jax.ShapeDtypeStruct((BLOCK, HEAD_DIM), jnp.bfloat16)] * len(work)
    else:
        out_shape = [jax.ShapeDtypeStruct((lines, HEAD_DIM), jnp.float32)] * 2
    scratch = [pltpu.VMEM((max(len(places) for _, _, _, places in work), 2 * ROWS, HEAD_DIM), jnp.bfloat16)]
    if last:
        scratch = [pltpu.VMEM((lines, HEAD_DIM), jnp.bfloat16), pltpu.VMEM((lines, HEAD_DIM), jnp.float32)] + scratch
    return pl.pallas_call(
        functools.partial(stage_kernel, work, first, last, len(tail) > 0),
        out_shape=out_shape,
        in_specs=[VMEM] * len(operands),
        out_specs=[VMEM] * len(out_shape),
        scratch_shapes=scratch,
        compiler_params=params(32),
        cost_estimate=SMALL,
        name="stage",
    )(*operands)


def combine_kernel(z_ref, guide_ref, r0, r1, r2, r3, r4, fresh, keep, send):
    z, guide = z_ref[0], guide_ref[0]
    tile = HEAD_DIM
    todo = [(r, 0, lax.rem(z + s, SLOTS)) for s, r in enumerate((r0, r1, r2, r3))] + [(r4, 0, SLOTS)]

    def levels(ref, start):
        stat = ref[pl.ds(start, BLOCK - ROWS), :].astype(jnp.float32)
        level = stat[0:4, :] + stat[4:8, :] + stat[8:12, :]
        return [jnp.transpose(jnp.broadcast_to(level[i : i + 1, :], (tile, tile))) for i in range(ROWS // tile)]

    for came, row, head in todo:
        at = pl.multiple_of(head * BLOCK, BLOCK - ROWS)
        there = jnp.concatenate(levels(came, row + ROWS), axis=0)
        here = jnp.concatenate(levels(fresh, at + ROWS), axis=0)
        share = 1.0 / (1.0 + jnp.exp2(here - there))
        old = came[row : row + ROWS, :].astype(jnp.float32)
        new = fresh[pl.ds(at, ROWS), :].astype(jnp.float32)
        joined = (new + (old - new) * share).astype(jnp.bfloat16)
        for half in range(2):
            rows = joined[half * HALF : (half + 1) * HALF, :]
            for mine, target in ((True, keep), (False, send)):

                @pl.when((guide == half) == mine)
                def _(rows=rows, target=target, head=head):
                    target[head] = rows


def pick_kernel(near_ref, far_ref, weight, near, far, buffer, loaded, stored):
    width = weight.shape[0]
    loads, stores = [], []
    for i, (places, target) in enumerate(((far_ref, far), (near_ref, near))):
        for s in range(4):
            cols = pl.ds(pl.multiple_of(places[s] * width, width), width)
            at = 4 * i + s
            loads.append(pltpu.make_async_copy(weight.at[:, cols], buffer.at[at], loaded.at[at]))
            stores.append(pltpu.make_async_copy(buffer.at[at], target.at[s], stored.at[at]))
    for load in loads:
        load.start()
    for load, store in zip(loads, stores):
        load.wait()
        store.start()
    for store in stores:
        store.wait()


def project_kernel(guide_ref, own, other, far_own, far_other, weight, far_weight, out0, out1, out2, out3):
    first = guide_ref[0] == 0
    by_own = jnp.where(first, guide_scale, 1.0 - guide_scale)
    by_other = jnp.where(first, 1.0 - guide_scale, guide_scale)

    def mixed(own, other):
        heads = [own[h].astype(jnp.float32) * by_own + other[h].astype(jnp.float32) * by_other for h in range(own.shape[0])]
        return jnp.concatenate([head.astype(jnp.bfloat16) for head in heads], axis=1)

    mine, its = mixed(own, other), mixed(far_own, far_other)
    for s, out in ((1, out1), (2, out2), (3, out3), (0, out0)):
        share = jnp.dot(mine, weight[s], preferred_element_type=jnp.float32)
        share = share + jnp.dot(its, far_weight[s], preferred_element_type=jnp.float32)
        out[...] = share.astype(out.dtype)


def on_device(
    query,
    key_fresh,
    value_fresh,
    key_stale,
    value_stale,
    out_weight,
    stream,
    gate_table,
    step_index,
):
    rows, width = query.shape[1:]
    heads = width // HEAD_DIM
    half = rows // 2
    patch = lax.axis_index("patch")
    tensor = lax.axis_index("tensor")
    guide = lax.axis_index("guide")
    z = (patch % RING).astype(jnp.int32).reshape(1)
    guide_at = guide.astype(jnp.int32).reshape(1)

    def after(value, *others):
        return lax.optimization_barrier((value, *others))[0]

    sizes = [(6 if s == 0 else 5) * rows for s in range(SLOTS)]
    messages = pl.pallas_call(
        lay_out,
        out_shape=[jax.ShapeDtypeStruct((size, HEAD_DIM), jnp.bfloat16) for size in sizes],
        in_specs=[SMEM] + [ANY] * 3,
        out_specs=[ANY] * SLOTS,
        scratch_shapes=[
            pltpu.VMEM((3, rows, width), jnp.bfloat16),
            pltpu.SemaphoreType.DMA((3,)),
            pltpu.SemaphoreType.DMA((SLOTS,)),
        ]
        + [pltpu.VMEM((size, HEAD_DIM), jnp.bfloat16) for size in sizes],
        compiler_params=params(58),
        name="lay_out",
    )(z, query[0], key_stale[0], value_stale[0])

    stream_mine = lax.dynamic_slice_in_dim(stream[0], guide * half, half, 0)
    stream_sent = lax.dynamic_slice_in_dim(stream[0], (1 - guide) * half, half, 0)

    fresh_shape = jax.ShapeDtypeStruct((heads * BLOCK, HEAD_DIM), jnp.bfloat16)
    fresh = pl.pallas_call(
        fresh_kernel,
        out_shape=fresh_shape,
        in_specs=[VMEM] * 3,
        out_specs=VMEM,
        compiler_params=params(32),
        cost_estimate=SMALL,
        name="fresh",
    )(query[0], key_fresh[0], value_fresh[0])

    x, core = tensor // 2, tensor % 2
    chips = (x + jnp.arange(4, dtype=jnp.int32)) % 4
    near_places = (2 * chips + core).astype(jnp.int32)
    far_places = (2 * chips + 1 - core).astype(jnp.int32)
    blocks_shape = jax.ShapeDtypeStruct((4, width, width), jnp.bfloat16)
    weight_own, weight_sent = pl.pallas_call(
        pick_kernel,
        out_shape=[blocks_shape, blocks_shape],
        in_specs=[SMEM, SMEM, ANY],
        out_specs=[ANY, ANY],
        scratch_shapes=[
            pltpu.VMEM((8, width, width), jnp.bfloat16),
            pltpu.SemaphoreType.DMA((8,)),
            pltpu.SemaphoreType.DMA((8,)),
        ],
        compiler_params=params(48),
        cost_estimate=SMALL,
        name="pick",
    )(near_places, after(far_places, messages[ORDER[0]]), out_weight)

    def joined(pair, begin, count):
        return jnp.concatenate([arrived[slot][begin * rows : (begin + count) * rows] for slot in pair], axis=0)

    def work_on(queries, names, pair, own=None):
        work = []
        for slot, part in queries:
            places = []
            for name in names[part]:
                for i, other in enumerate(pair):
                    if not (name in (own, str((own, part))) and other == slot):
                        places.append((name, (4 * i + 2 * part if name in WHOLE else 2 * i) * rows))
            work.append((slot, part, QUERIES.index((slot, part)) * rows, tuple(places)))
        return tuple(work)

    arrived = {slot: to_slot(messages[slot], slot) for slot in PAIRS[0]}
    stream_other = other_guide(stream_sent)
    here, there, fresh, stream_other, weight_sent, *rest = lax.optimization_barrier(
        (*arrived.values(), fresh, stream_other, weight_sent, *(messages[slot] for slot in PAIRS[1]))
    )
    arrived = dict(zip(PAIRS[0], (here, there)))
    for slot, message in zip(PAIRS[1], rest):
        arrived[slot] = to_slot(message, slot)
    early = joined(PAIRS[0], 0, 4)
    early_y, early_core = other_y(early), other_core(early)
    early_y, early_core, a, b = lax.optimization_barrier((early_y, early_core, *(arrived[slot] for slot in PAIRS[1])))
    arrived.update(zip(PAIRS[1], (a, b)))
    arrays = {"early": early, "early_y": early_y, "early_core": early_core, "early_y_core": other_core(early_y)}
    own, last_own = joined(PAIRS[1], 0, 2), joined(PAIRS[1], 2, 2)
    arrays["own", 0], arrays["core", 0], over = own, other_core(own), other_y(own)

    def named(part, *names):
        return [str((name, part)) for name in names]

    def both_parts(*names):
        return {part: named(part, *names) for part in range(2)}

    first_work = work_on(QUERIES, [WHOLE[:3]] * 2, PAIRS[0], "early")
    state = stage(first_work, arrived, {str(name): array for name, array in arrays.items()}, None)
    over, *state = lax.optimization_barrier((over, *state))
    over_core, last_over = other_core(over), other_y(after(last_own, over))
    work = work_on(QUERIES, [WHOLE[3:]] * 2, PAIRS[0])
    state = stage(work, arrived, {str(name): array for name, array in arrays.items()}, state)
    last_core = other_core(last_own)
    over_core, last_core, *state = lax.optimization_barrier((over_core, last_core, *state))
    arrays["y", 0], arrays["y_core", 0] = over, over_core
    arrays["own", 1], arrays["core", 1] = last_own, last_core
    arrays = {str(name): array for name, array in arrays.items()}

    rest = stage(work_on(QUERIES[:SLOTS], both_parts("own", "core"), PAIRS[1], "own"), arrived, arrays, state)
    last = named(1, "core", "own", "y", "y_core")
    parts = {0: named(0, "y", "y_core"), 1: last}
    tail = [part_of[SLOTS * rows :] for part_of in state]
    came = {}
    outs = stage(work_on(QUERIES[:3], parts, PAIRS[1]), arrived, arrays, rest, True)
    for (slot, _), out in zip(QUERIES[:3], outs):
        came[slot] = from_slot(out, slot)
    last_over = after(last_over, outs[0])
    arrays[last[2]], arrays[last[3]] = last_over, other_core(last_over)
    outs = stage(work_on(QUERIES[3:], parts, PAIRS[1], "own"), arrived, arrays, rest, True, tail)
    came[0], came[SLOTS] = (from_slot(out, 0) for out in outs)
    came = [came[slot] for slot in range(SLOTS + 1)]
    weight_other = other_core(weight_sent)

    att_shape = jax.ShapeDtypeStruct((heads, half, HEAD_DIM), jnp.bfloat16)
    keep, send = pl.pallas_call(
        combine_kernel,
        out_shape=[att_shape, att_shape],
        in_specs=[SMEM, SMEM] + [VMEM] * 6,
        out_specs=[VMEM] * 2,
        compiler_params=params(32),
        cost_estimate=SMALL,
        name="combine",
    )(z, guide_at, *came, fresh)
    other = other_guide(send)

    share = jax.ShapeDtypeStruct((half, width), jnp.float32)
    sent = jax.ShapeDtypeStruct((half, width), jnp.bfloat16)
    shares = pl.pallas_call(
        project_kernel,
        out_shape=[share, sent, sent, sent],
        in_specs=[SMEM] + [VMEM] * 6,
        out_specs=[VMEM] * 4,
        compiler_params=params(32),
        cost_estimate=SMALL,
        name="project",
    )(guide_at, keep, other, other_core(keep), other_core(other), weight_own, weight_other)
    term = shares[0]
    for s in range(1, 4):
        term = term + shift_x(shares[s], s).astype(jnp.float32)

    gate = lax.dynamic_index_in_dim(gate_table, step_index[0], 0, keepdims=False)
    near, far = stream_mine.astype(jnp.float32), stream_other.astype(jnp.float32)
    cond = jnp.where(guide == 0, near, far)
    uncond = jnp.where(guide == 0, far, near)
    guided = (uncond + guide_scale * (cond - uncond) + gate[None, :] * term).astype(jnp.bfloat16)
    own_cols = width // 2
    stays = lax.dynamic_slice_in_dim(guided, guide * own_cols, own_cols, 1)
    goes = lax.dynamic_slice_in_dim(guided, (1 - guide) * own_cols, own_cols, 1)
    got = other_guide(goes)
    return jnp.where(
        guide == 0, jnp.concatenate([stays, got], axis=0), jnp.concatenate([got, stays], axis=0)
    )


def solution(mesh):
    in_specs = (
        P("guide", "patch", "tensor"),
        P("guide", "patch", "tensor"),
        P("guide", "patch", "tensor"),
        P("guide", "patch", "tensor"),
        P("guide", "patch", "tensor"),
        P("tensor", None),
        P("guide", "patch", "tensor"),
        P(None, "tensor"),
        P(),
    )
    out_specs = P("patch", ("tensor", "guide"))
    return jax.shard_map(
        on_device, mesh=mesh, in_specs=in_specs, out_specs=out_specs, check_vma=False
    )
```

```python
import functools

import jax
import jax.numpy as jnp
from jax import lax
from jax.experimental import pallas as pl
from jax.experimental.pallas import tpu as pltpu
from jax.sharding import PartitionSpec as P

HEAD_DIM = 128
SLOTS = 4
RING = 8
ROWS = 512
HALF = ROWS // 2
BLOCK = ROWS + 16
SCALE2 = 1.4426950408889634 / HEAD_DIM**0.5
SAFE_SUM = 2.0**100
VMEM = pl.BlockSpec(memory_space=pltpu.VMEM)
SMEM = pl.BlockSpec(memory_space=pltpu.SMEM)
ANY = pl.BlockSpec(memory_space=pl.ANY)
PLACE = ("patch", "tensor")
PAIRS = ((1, 3), (0, 2))
ORDER = PAIRS[0] + PAIRS[1]
WHOLE = ("early_core", "early", "early_y", "early_y_core")
QUERIES = ((1, 0), (3, 0), (2, 0), (0, 0), (0, 1))
ROW_BY_ROW = (((1,), (1,)), ((), ()))
SMALL = pl.CostEstimate(flops=2**10, bytes_accessed=2**10, transcendentals=0)

guide_scale = 5.0


def params(mib):
    return pltpu.CompilerParams(vmem_limit_bytes=mib * 2**20)


def slot_pairs(slot, back):
    pairs = []
    for y in range(2):
        for z in range(RING):
            for x in range(4):
                for core in range(2):
                    there = SLOTS * core + (z + slot) % SLOTS
                    source = (y * RING + z) * 8 + x * 2 + core
                    target = (y * RING + there) * 8 + x * 2 + z // SLOTS
                    pairs.append((target, source) if back else (source, target))
    return pairs


def to_slot(value, slot):
    return lax.ppermute(value, PLACE, slot_pairs(slot, False))


def from_slot(value, slot):
    return lax.ppermute(value, PLACE, slot_pairs(slot, True))


def other_y(value):
    return lax.ppermute(value, "patch", [(i, (i + RING) % (2 * RING)) for i in range(2 * RING)])


def other_core(value):
    return lax.ppermute(value, "tensor", [(i, i ^ 1) for i in range(8)])


def other_guide(value):
    return lax.ppermute(value, "guide", [(0, 1), (1, 0)])


def shift_x(value, step):
    return lax.ppermute(value, "tensor", [(i, (i + 2 * step) % 8) for i in range(8)])


def scores(queries, keys):
    return lax.dot_general(queries, keys, ROW_BY_ROW, preferred_element_type=jnp.float32)


def lay_out(z_ref, query, key, value, *refs):
    messages, (held, loaded, stored, *buffers) = refs[:SLOTS], refs[SLOTS:]
    z = z_ref[0]
    loads = [pltpu.make_async_copy(src, held.at[i], loaded.at[i]) for i, src in enumerate((key, value, query))]
    for load in loads:
        load.start()
    for load in loads:
        load.wait()
    last = slice(SLOTS * HEAD_DIM, (SLOTS + 1) * HEAD_DIM)
    stores = []
    for slot in ORDER:
        message, buffer = messages[slot], buffers[slot]
        head = pl.ds(pl.multiple_of(lax.rem(z + slot, SLOTS) * HEAD_DIM, HEAD_DIM), HEAD_DIM)
        buffer[0:ROWS, :] = held[0, :, head]
        buffer[ROWS : 2 * ROWS, :] = held[1, :, head]
        buffer[2 * ROWS : 3 * ROWS, :] = held[0, :, last]
        buffer[3 * ROWS : 4 * ROWS, :] = held[1, :, last]
        buffer[4 * ROWS : 5 * ROWS, :] = held[2, :, head]
        if slot == 0:
            buffer[5 * ROWS : 6 * ROWS, :] = held[2, :, last]
        stores.append(pltpu.make_async_copy(buffer, message, stored.at[slot]))
        stores[-1].start()
    for store in stores:
        store.wait()


def with_ones(values):
    return jnp.concatenate([values, jnp.ones(values.shape, values.dtype)], axis=1)


def write_block(target, row, attended, level_at):
    target[row : row + ROWS, :] = attended
    tile = HEAD_DIM
    lines = [jnp.transpose(level_at[i * tile : (i + 1) * tile, :])[0:1, :] for i in range(ROWS // tile)]
    level = jnp.concatenate(lines, axis=0)
    high = level.astype(jnp.bfloat16).astype(jnp.float32)
    rest = level - high
    middle = rest.astype(jnp.bfloat16).astype(jnp.float32)
    rows = jnp.concatenate([high, middle, rest - middle, jnp.zeros_like(level)], axis=0)
    target[row + ROWS : row + BLOCK, :] = rows.astype(jnp.bfloat16)


def fresh_kernel(query, key, value, out):
    for h in range(query.shape[1] // HEAD_DIM):
        cols = slice(h * HEAD_DIM, (h + 1) * HEAD_DIM)
        score = scores(query[:, cols], key[:, cols])
        peak = jnp.max(score, axis=1, keepdims=True) * SCALE2
        weights = jnp.exp2(score * SCALE2 - peak).astype(jnp.bfloat16)
        both = jnp.dot(weights, with_ones(value[:, cols]), preferred_element_type=jnp.float32)
        total = both[:, HEAD_DIM:]
        attended = (both[:, :HEAD_DIM] / total).astype(jnp.bfloat16)
        write_block(out, h * BLOCK, attended, peak + jnp.log2(total))


def stage_kernel(work, first, last, *refs):
    slots = sorted({slot for slot, _, _, _ in work})
    arrays_used = sorted({a for _, _, _, places in work for a, _ in places})
    messages, refs = dict(zip(slots, refs)), refs[len(slots) :]
    arrays, refs = dict(zip(arrays_used, refs)), refs[len(arrays_used) :]
    if not first:
        (summed_in, stat_in), refs = refs[:2], refs[2:]
    if last:
        outs, (attended, level_at, held) = refs[: len(work)], refs[len(work) :]
    else:
        summed_out, stat_out, held = refs
    middle = HEAD_DIM // 2
    lane = lax.broadcasted_iota(jnp.int32, (HALF, HEAD_DIM), 1)

    def before(row, begin):
        span = pl.ds(row + begin, HALF)
        stat = stat_in[span, :]
        total = jnp.broadcast_to(stat[:, 0:1], stat.shape)
        return jnp.concatenate([summed_in[span, :], total], axis=1), stat[:, middle : middle + 1]

    def finish(row, n, begin, both, peak):
        total = both[:, HEAD_DIM:]
        if last:
            span = pl.ds(n * ROWS + begin, HALF)
            attended[span, :] = (both[:, :HEAD_DIM] / total).astype(jnp.bfloat16)
            level_at[span, :] = peak + jnp.log2(total)
        else:
            span = pl.ds(row + begin, HALF)
            summed_out[span, :] = both[:, :HEAD_DIM]
            stat_out[span, :] = jnp.where(lane < middle, total, peak)

    largest = None
    for n, (slot, part, row, places) in enumerate(work):
        for begin in (0, HALF):
            queries = messages[slot][(4 + part) * ROWS + begin : (4 + part) * ROWS + begin + HALF, :]
            both, peak = (None, None) if first else before(row, begin)
            for a, base in places:
                score = scores(queries, arrays[a][base : base + ROWS, :])
                if peak is None:
                    peak = jnp.max(score, axis=1, keepdims=True) * SCALE2
                weights = jnp.exp2(score * SCALE2 - peak).astype(jnp.bfloat16)
                values = arrays[a][base + ROWS : base + 2 * ROWS, :]
                more = jnp.dot(weights, with_ones(values), preferred_element_type=jnp.float32)
                both = more if both is None else both + more
            finish(row, n, begin, both, peak)
            largest = both[:, HEAD_DIM:] if largest is None else jnp.maximum(largest, both[:, HEAD_DIM:])

    @pl.when(jnp.logical_not(jnp.max(largest) < SAFE_SUM))
    def _():
        for n, (slot, part, row, places) in enumerate(work):
            for at, (a, base) in enumerate(places):
                held[at] = arrays[a][base : base + 2 * ROWS, :]

            def chunk_step(c, carry, n=n, slot=slot, part=part, row=row, count=len(places)):
                begin = pl.multiple_of(c * HALF, HALF)
                queries = messages[slot][pl.ds((4 + part) * ROWS + begin, HALF), :]

                def follow(at, state):
                    both, peak = state
                    score = scores(queries, held[at, :ROWS, :]) * SCALE2
                    higher = jnp.maximum(peak, jnp.max(score, axis=1, keepdims=True))
                    weights = jnp.exp2(score - higher).astype(jnp.bfloat16)
                    more = jnp.dot(weights, with_ones(held[at, ROWS:, :]), preferred_element_type=jnp.float32)
                    return both * jnp.exp2(peak - higher) + more, higher

                if first:
                    start = (jnp.zeros((HALF, 2 * HEAD_DIM), jnp.float32), jnp.full((HALF, 1), -1e30, jnp.float32))
                else:
                    start = before(row, begin)
                finish(row, n, begin, *lax.fori_loop(0, count, follow, start))
                return carry

            lax.fori_loop(0, 2, chunk_step, 0)

    if last:
        for n, out in enumerate(outs):
            here = slice(n * ROWS, (n + 1) * ROWS)
            write_block(out, 0, attended[here, :], level_at.at[n * ROWS : (n + 1) * ROWS, :])


def stage(work, messages, arrays, state, last=False):
    first = state is None
    slots = sorted({slot for slot, _, _, _ in work})
    arrays_used = sorted({a for _, _, _, places in work for a, _ in places})
    operands = [messages[s] for s in slots] + [arrays[a] for a in arrays_used] + ([] if first else list(state))
    lines = len(work) * ROWS
    if last:
        out_shape = [jax.ShapeDtypeStruct((BLOCK, HEAD_DIM), jnp.bfloat16)] * len(work)
    else:
        out_shape = [jax.ShapeDtypeStruct((lines, HEAD_DIM), jnp.float32)] * 2
    scratch = [pltpu.VMEM((max(len(places) for _, _, _, places in work), 2 * ROWS, HEAD_DIM), jnp.bfloat16)]
    if last:
        scratch = [pltpu.VMEM((lines, HEAD_DIM), jnp.bfloat16), pltpu.VMEM((lines, HEAD_DIM), jnp.float32)] + scratch
    return pl.pallas_call(
        functools.partial(stage_kernel, work, first, last),
        out_shape=out_shape,
        in_specs=[VMEM] * len(operands),
        out_specs=[VMEM] * len(out_shape),
        scratch_shapes=scratch,
        compiler_params=params(32),
        cost_estimate=SMALL,
        name="stage",
    )(*operands)


def combine_kernel(z_ref, guide_ref, r0, r1, r2, r3, r4, fresh, keep, send):
    z, guide = z_ref[0], guide_ref[0]
    tile = HEAD_DIM
    todo = [(r, 0, lax.rem(z + s, SLOTS)) for s, r in enumerate((r0, r1, r2, r3))] + [(r4, 0, SLOTS)]

    def levels(ref, start):
        stat = ref[pl.ds(start, BLOCK - ROWS), :].astype(jnp.float32)
        level = stat[0:4, :] + stat[4:8, :] + stat[8:12, :]
        return [jnp.transpose(jnp.broadcast_to(level[i : i + 1, :], (tile, tile))) for i in range(ROWS // tile)]

    for came, row, head in todo:
        at = pl.multiple_of(head * BLOCK, BLOCK - ROWS)
        there = jnp.concatenate(levels(came, row + ROWS), axis=0)
        here = jnp.concatenate(levels(fresh, at + ROWS), axis=0)
        share = 1.0 / (1.0 + jnp.exp2(here - there))
        old = came[row : row + ROWS, :].astype(jnp.float32)
        new = fresh[pl.ds(at, ROWS), :].astype(jnp.float32)
        joined = (new + (old - new) * share).astype(jnp.bfloat16)
        for half in range(2):
            rows = joined[half * HALF : (half + 1) * HALF, :]
            for mine, target in ((True, keep), (False, send)):

                @pl.when((guide == half) == mine)
                def _(rows=rows, target=target, head=head):
                    target[head] = rows


def pick_kernel(near_ref, far_ref, weight, near, far, buffer, loaded, stored):
    width = weight.shape[0]
    loads, stores = [], []
    for i, (places, target) in enumerate(((far_ref, far), (near_ref, near))):
        for s in range(4):
            cols = pl.ds(pl.multiple_of(places[s] * width, width), width)
            at = 4 * i + s
            loads.append(pltpu.make_async_copy(weight.at[:, cols], buffer.at[at], loaded.at[at]))
            stores.append(pltpu.make_async_copy(buffer.at[at], target.at[s], stored.at[at]))
    for load in loads:
        load.start()
    for load, store in zip(loads, stores):
        load.wait()
        store.start()
    for store in stores:
        store.wait()


def project_kernel(guide_ref, own, other, far_own, far_other, weight, far_weight, out0, out1, out2, out3):
    first = guide_ref[0] == 0
    by_own = jnp.where(first, guide_scale, 1.0 - guide_scale)
    by_other = jnp.where(first, 1.0 - guide_scale, guide_scale)

    def mixed(own, other):
        heads = [own[h].astype(jnp.float32) * by_own + other[h].astype(jnp.float32) * by_other for h in range(own.shape[0])]
        return jnp.concatenate([head.astype(jnp.bfloat16) for head in heads], axis=1)

    mine, its = mixed(own, other), mixed(far_own, far_other)
    for s, out in ((1, out1), (2, out2), (3, out3), (0, out0)):
        share = jnp.dot(mine, weight[s], preferred_element_type=jnp.float32)
        share = share + jnp.dot(its, far_weight[s], preferred_element_type=jnp.float32)
        out[...] = share.astype(out.dtype)


def on_device(
    query,
    key_fresh,
    value_fresh,
    key_stale,
    value_stale,
    out_weight,
    stream,
    gate_table,
    step_index,
):
    rows, width = query.shape[1:]
    heads = width // HEAD_DIM
    half = rows // 2
    patch = lax.axis_index("patch")
    tensor = lax.axis_index("tensor")
    guide = lax.axis_index("guide")
    z = (patch % RING).astype(jnp.int32).reshape(1)
    guide_at = guide.astype(jnp.int32).reshape(1)

    def after(value, *others):
        return lax.optimization_barrier((value, *others))[0]

    sizes = [(6 if s == 0 else 5) * rows for s in range(SLOTS)]
    messages = pl.pallas_call(
        lay_out,
        out_shape=[jax.ShapeDtypeStruct((size, HEAD_DIM), jnp.bfloat16) for size in sizes],
        in_specs=[SMEM] + [ANY] * 3,
        out_specs=[ANY] * SLOTS,
        scratch_shapes=[
            pltpu.VMEM((3, rows, width), jnp.bfloat16),
            pltpu.SemaphoreType.DMA((3,)),
            pltpu.SemaphoreType.DMA((SLOTS,)),
        ]
        + [pltpu.VMEM((size, HEAD_DIM), jnp.bfloat16) for size in sizes],
        compiler_params=params(58),
        name="lay_out",
    )(z, query[0], key_stale[0], value_stale[0])

    stream_mine = lax.dynamic_slice_in_dim(stream[0], guide * half, half, 0)
    stream_sent = lax.dynamic_slice_in_dim(stream[0], (1 - guide) * half, half, 0)

    fresh_shape = jax.ShapeDtypeStruct((heads * BLOCK, HEAD_DIM), jnp.bfloat16)
    fresh = pl.pallas_call(
        fresh_kernel,
        out_shape=fresh_shape,
        in_specs=[VMEM] * 3,
        out_specs=VMEM,
        compiler_params=params(32),
        cost_estimate=SMALL,
        name="fresh",
    )(query[0], key_fresh[0], value_fresh[0])

    x, core = tensor // 2, tensor % 2
    chips = (x + jnp.arange(4, dtype=jnp.int32)) % 4
    near_places = (2 * chips + core).astype(jnp.int32)
    far_places = (2 * chips + 1 - core).astype(jnp.int32)
    blocks_shape = jax.ShapeDtypeStruct((4, width, width), jnp.bfloat16)
    weight_own, weight_sent = pl.pallas_call(
        pick_kernel,
        out_shape=[blocks_shape, blocks_shape],
        in_specs=[SMEM, SMEM, ANY],
        out_specs=[ANY, ANY],
        scratch_shapes=[
            pltpu.VMEM((8, width, width), jnp.bfloat16),
            pltpu.SemaphoreType.DMA((8,)),
            pltpu.SemaphoreType.DMA((8,)),
        ],
        compiler_params=params(48),
        cost_estimate=SMALL,
        name="pick",
    )(near_places, after(far_places, messages[ORDER[0]]), out_weight)

    def joined(pair, begin, count):
        return jnp.concatenate([arrived[slot][begin * rows : (begin + count) * rows] for slot in pair], axis=0)

    def work_on(queries, names, pair, own=None):
        work = []
        for slot, part in queries:
            places = []
            for name in names[part]:
                for i, other in enumerate(pair):
                    if not (name in (own, str((own, part))) and other == slot):
                        places.append((name, (4 * i + 2 * part if name in WHOLE else 2 * i) * rows))
            work.append((slot, part, QUERIES.index((slot, part)) * rows, tuple(places)))
        return tuple(work)

    arrived = {slot: to_slot(messages[slot], slot) for slot in PAIRS[0]}
    stream_other = other_guide(stream_sent)
    here, there, fresh, stream_other, weight_sent, *rest = lax.optimization_barrier(
        (*arrived.values(), fresh, stream_other, weight_sent, *(messages[slot] for slot in PAIRS[1]))
    )
    arrived = dict(zip(PAIRS[0], (here, there)))
    for slot, message in zip(PAIRS[1], rest):
        arrived[slot] = to_slot(message, slot)
    early = joined(PAIRS[0], 0, 4)
    early_y, early_core = other_y(early), other_core(early)
    early_y, early_core, a, b = lax.optimization_barrier((early_y, early_core, *(arrived[slot] for slot in PAIRS[1])))
    arrived.update(zip(PAIRS[1], (a, b)))
    arrays = {"early": early, "early_y": early_y, "early_core": early_core}
    own, last_own = joined(PAIRS[1], 0, 2), joined(PAIRS[1], 2, 2)
    over = other_y(own)
    for part, piece in enumerate((own, last_own)):
        arrays[str(("own", part))], arrays[str(("core", part))] = piece, other_core(piece)

    def named(part, *names):
        return [str((name, part)) for name in names]

    def both_parts(*names):
        return {part: named(part, *names) for part in range(2)}

    state = stage(work_on(QUERIES, [WHOLE[:3]] * 2, PAIRS[0], "early"), arrived, arrays, None)
    core, last_core = both_parts("core")[0][0], both_parts("core")[1][0]
    over, arrays[core], arrays[last_core], *state = lax.optimization_barrier(
        (over, arrays[core], arrays[last_core], *state)
    )
    over_core, last_over = other_core(over), other_y(after(last_own, over))
    arrays["early_y_core"] = other_core(after(early_y, state[0]))
    state = stage(work_on(QUERIES, both_parts("own", "core"), PAIRS[1], "own"), arrived, arrays, state)
    over_core, *state = lax.optimization_barrier((over_core, *state))
    state = stage(work_on(QUERIES, [WHOLE[3:]] * 2, PAIRS[0]), arrived, arrays, state)
    parts = both_parts("y", "y_core")
    arrays.update(zip(parts[0], (over, over_core)))
    came = {}
    outs = stage(work_on(QUERIES[:SLOTS], parts, PAIRS[1]), arrived, arrays, state, True)
    for (slot, _), out in zip(QUERIES, outs):
        came[slot] = from_slot(out, slot)
    last_over = after(last_over, outs[0])
    arrays.update(zip(parts[1], (last_over, other_core(last_over))))
    (out,) = stage(work_on(QUERIES[SLOTS:], parts, PAIRS[1]), arrived, arrays, state, True)
    came[SLOTS] = from_slot(out, 0)
    came = [came[slot] for slot in range(SLOTS + 1)]
    weight_other = other_core(weight_sent)

    att_shape = jax.ShapeDtypeStruct((heads, half, HEAD_DIM), jnp.bfloat16)
    keep, send = pl.pallas_call(
        combine_kernel,
        out_shape=[att_shape, att_shape],
        in_specs=[SMEM, SMEM] + [VMEM] * 6,
        out_specs=[VMEM] * 2,
        compiler_params=params(32),
        cost_estimate=SMALL,
        name="combine",
    )(z, guide_at, *came, fresh)
    other = other_guide(send)

    share = jax.ShapeDtypeStruct((half, width), jnp.float32)
    sent = jax.ShapeDtypeStruct((half, width), jnp.bfloat16)
    shares = pl.pallas_call(
        project_kernel,
        out_shape=[share, sent, sent, sent],
        in_specs=[SMEM] + [VMEM] * 6,
        out_specs=[VMEM] * 4,
        compiler_params=params(32),
        cost_estimate=SMALL,
        name="project",
    )(guide_at, keep, other, other_core(keep), other_core(other), weight_own, weight_other)
    term = shares[0]
    for s in range(1, 4):
        term = term + shift_x(shares[s], s).astype(jnp.float32)

    gate = lax.dynamic_index_in_dim(gate_table, step_index[0], 0, keepdims=False)
    near, far = stream_mine.astype(jnp.float32), stream_other.astype(jnp.float32)
    cond = jnp.where(guide == 0, near, far)
    uncond = jnp.where(guide == 0, far, near)
    guided = (uncond + guide_scale * (cond - uncond) + gate[None, :] * term).astype(jnp.bfloat16)
    own_cols = width // 2
    stays = lax.dynamic_slice_in_dim(guided, guide * own_cols, own_cols, 1)
    goes = lax.dynamic_slice_in_dim(guided, (1 - guide) * own_cols, own_cols, 1)
    got = other_guide(goes)
    return jnp.where(
        guide == 0, jnp.concatenate([stays, got], axis=0), jnp.concatenate([got, stays], axis=0)
    )


def solution(mesh):
    in_specs = (
        P("guide", "patch", "tensor"),
        P("guide", "patch", "tensor"),
        P("guide", "patch", "tensor"),
        P("guide", "patch", "tensor"),
        P("guide", "patch", "tensor"),
        P("tensor", None),
        P("guide", "patch", "tensor"),
        P(None, "tensor"),
        P(),
    )
    out_specs = P("patch", ("tensor", "guide"))
    return jax.shard_map(
        on_device, mesh=mesh, in_specs=in_specs, out_specs=out_specs, check_vma=False
    )
```

```python
import functools

import jax
import jax.numpy as jnp
from jax import lax
from jax.experimental import pallas as pl
from jax.experimental.pallas import tpu as pltpu
from jax.sharding import PartitionSpec as P

HEAD_DIM = 128
SLOTS = 4
RING = 8
ROWS = 512
HALF = ROWS // 2
BLOCK = ROWS + 16
SCALE2 = 1.4426950408889634 / HEAD_DIM**0.5
SAFE_SUM = 2.0**100
VMEM = pl.BlockSpec(memory_space=pltpu.VMEM)
SMEM = pl.BlockSpec(memory_space=pltpu.SMEM)
ANY = pl.BlockSpec(memory_space=pl.ANY)
PLACE = ("patch", "tensor")
PAIRS = ((1, 3), (0, 2))
ORDER = PAIRS[0] + PAIRS[1]
WHOLE = ("early_core", "early", "early_y", "early_y_core")
QUERIES = ((1, 0), (3, 0), (2, 0), (0, 0), (0, 1))
ROW_BY_ROW = (((1,), (1,)), ((), ()))
SMALL = pl.CostEstimate(flops=2**10, bytes_accessed=2**10, transcendentals=0)

guide_scale = 5.0


def params(mib):
    return pltpu.CompilerParams(vmem_limit_bytes=mib * 2**20)


def slot_pairs(slot, back):
    pairs = []
    for y in range(2):
        for z in range(RING):
            for x in range(4):
                for core in range(2):
                    there = SLOTS * core + (z + slot) % SLOTS
                    source = (y * RING + z) * 8 + x * 2 + core
                    target = (y * RING + there) * 8 + x * 2 + z // SLOTS
                    pairs.append((target, source) if back else (source, target))
    return pairs


def to_slot(value, slot):
    return lax.ppermute(value, PLACE, slot_pairs(slot, False))


def from_slot(value, slot):
    return lax.ppermute(value, PLACE, slot_pairs(slot, True))


def other_y(value):
    return lax.ppermute(value, "patch", [(i, (i + RING) % (2 * RING)) for i in range(2 * RING)])


def other_core(value):
    return lax.ppermute(value, "tensor", [(i, i ^ 1) for i in range(8)])


def other_guide(value):
    return lax.ppermute(value, "guide", [(0, 1), (1, 0)])


def shift_x(value, step):
    return lax.ppermute(value, "tensor", [(i, (i + 2 * step) % 8) for i in range(8)])


def query_row(slot, part):
    return ((4 if slot in PAIRS[0] else 2) + part) * ROWS


def scores(queries, keys):
    return lax.dot_general(queries, keys, ROW_BY_ROW, preferred_element_type=jnp.float32)


def lay_out(z_ref, query, key, value, *refs):
    count = SLOTS + 2
    messages, (held, loaded, stored, *buffers) = refs[:count], refs[count:]
    z = z_ref[0]
    loads = [pltpu.make_async_copy(src, held.at[i], loaded.at[i]) for i, src in enumerate((key, value, query))]
    for load in loads:
        load.start()
    for load in loads:
        load.wait()
    last = slice(SLOTS * HEAD_DIM, (SLOTS + 1) * HEAD_DIM)
    stores = []
    for at in ORDER + (SLOTS, SLOTS + 1):
        buffer = buffers[at]
        if at >= SLOTS:
            parts = [(0, last), (1, last)]
        else:
            head = pl.ds(pl.multiple_of(lax.rem(z + at, SLOTS) * HEAD_DIM, HEAD_DIM), HEAD_DIM)
            parts = [(0, head), (1, head)] + ([(0, last), (1, last)] if at in PAIRS[0] else []) + [(2, head)]
            if at == 0:
                parts.append((2, last))
        for n, (which, cols) in enumerate(parts):
            buffer[n * ROWS : (n + 1) * ROWS, :] = held[which, :, cols]
        stores.append(pltpu.make_async_copy(buffer, messages[at], stored.at[at]))
        stores[-1].start()
    for store in stores:
        store.wait()


def with_ones(values):
    return jnp.concatenate([values, jnp.ones(values.shape, values.dtype)], axis=1)


def write_block(target, row, attended, level_at):
    target[row : row + ROWS, :] = attended
    tile = HEAD_DIM
    lines = [jnp.transpose(level_at[i * tile : (i + 1) * tile, :])[0:1, :] for i in range(ROWS // tile)]
    level = jnp.concatenate(lines, axis=0)
    high = level.astype(jnp.bfloat16).astype(jnp.float32)
    rest = level - high
    middle = rest.astype(jnp.bfloat16).astype(jnp.float32)
    rows = jnp.concatenate([high, middle, rest - middle, jnp.zeros_like(level)], axis=0)
    target[row + ROWS : row + BLOCK, :] = rows.astype(jnp.bfloat16)


def fresh_kernel(query, key, value, out):
    for h in range(query.shape[1] // HEAD_DIM):
        cols = slice(h * HEAD_DIM, (h + 1) * HEAD_DIM)
        score = scores(query[:, cols], key[:, cols])
        peak = jnp.max(score, axis=1, keepdims=True) * SCALE2
        weights = jnp.exp2(score * SCALE2 - peak).astype(jnp.bfloat16)
        both = jnp.dot(weights, with_ones(value[:, cols]), preferred_element_type=jnp.float32)
        total = both[:, HEAD_DIM:]
        attended = (both[:, :HEAD_DIM] / total).astype(jnp.bfloat16)
        write_block(out, h * BLOCK, attended, peak + jnp.log2(total))


def stage_kernel(work, first, last, *refs):
    slots = sorted({slot for slot, _, _, _ in work})
    arrays_used = sorted({a for _, _, _, places in work for a, _ in places})
    messages, refs = dict(zip(slots, refs)), refs[len(slots) :]
    arrays, refs = dict(zip(arrays_used, refs)), refs[len(arrays_used) :]
    if not first:
        (summed_in, stat_in), refs = refs[:2], refs[2:]
    if last:
        outs, (attended, level_at, held) = refs[: len(work)], refs[len(work) :]
    else:
        summed_out, stat_out, held = refs
    middle = HEAD_DIM // 2
    lane = lax.broadcasted_iota(jnp.int32, (HALF, HEAD_DIM), 1)

    def before(row, begin):
        span = pl.ds(row + begin, HALF)
        stat = stat_in[span, :]
        total = jnp.broadcast_to(stat[:, 0:1], stat.shape)
        return jnp.concatenate([summed_in[span, :], total], axis=1), stat[:, middle : middle + 1]

    def finish(row, n, begin, both, peak):
        total = both[:, HEAD_DIM:]
        if last:
            span = pl.ds(n * ROWS + begin, HALF)
            attended[span, :] = (both[:, :HEAD_DIM] / total).astype(jnp.bfloat16)
            level_at[span, :] = peak + jnp.log2(total)
        else:
            span = pl.ds(row + begin, HALF)
            summed_out[span, :] = both[:, :HEAD_DIM]
            stat_out[span, :] = jnp.where(lane < middle, total, peak)

    largest = None
    for n, (slot, part, row, places) in enumerate(work):
        for begin in (0, HALF):
            queries = messages[slot][query_row(slot, part) + begin : query_row(slot, part) + begin + HALF, :]
            both, peak = (None, None) if first else before(row, begin)
            for a, base in places:
                score = scores(queries, arrays[a][base : base + ROWS, :])
                if peak is None:
                    peak = jnp.max(score, axis=1, keepdims=True) * SCALE2
                weights = jnp.exp2(score * SCALE2 - peak).astype(jnp.bfloat16)
                values = arrays[a][base + ROWS : base + 2 * ROWS, :]
                more = jnp.dot(weights, with_ones(values), preferred_element_type=jnp.float32)
                both = more if both is None else both + more
            finish(row, n, begin, both, peak)
            largest = both[:, HEAD_DIM:] if largest is None else jnp.maximum(largest, both[:, HEAD_DIM:])

    @pl.when(jnp.logical_not(jnp.max(largest) < SAFE_SUM))
    def _():
        for n, (slot, part, row, places) in enumerate(work):
            for at, (a, base) in enumerate(places):
                held[at] = arrays[a][base : base + 2 * ROWS, :]

            def chunk_step(c, carry, n=n, slot=slot, part=part, row=row, count=len(places)):
                begin = pl.multiple_of(c * HALF, HALF)
                queries = messages[slot][pl.ds(query_row(slot, part) + begin, HALF), :]

                def follow(at, state):
                    both, peak = state
                    score = scores(queries, held[at, :ROWS, :]) * SCALE2
                    higher = jnp.maximum(peak, jnp.max(score, axis=1, keepdims=True))
                    weights = jnp.exp2(score - higher).astype(jnp.bfloat16)
                    more = jnp.dot(weights, with_ones(held[at, ROWS:, :]), preferred_element_type=jnp.float32)
                    return both * jnp.exp2(peak - higher) + more, higher

                if first:
                    start = (jnp.zeros((HALF, 2 * HEAD_DIM), jnp.float32), jnp.full((HALF, 1), -1e30, jnp.float32))
                else:
                    start = before(row, begin)
                finish(row, n, begin, *lax.fori_loop(0, count, follow, start))
                return carry

            lax.fori_loop(0, 2, chunk_step, 0)

    if last:
        for n, out in enumerate(outs):
            here = slice(n * ROWS, (n + 1) * ROWS)
            write_block(out, 0, attended[here, :], level_at.at[n * ROWS : (n + 1) * ROWS, :])


def stage(work, messages, arrays, state, last=False):
    first = state is None
    slots = sorted({slot for slot, _, _, _ in work})
    arrays_used = sorted({a for _, _, _, places in work for a, _ in places})
    operands = [messages[s] for s in slots] + [arrays[a] for a in arrays_used] + ([] if first else list(state))
    lines = len(work) * ROWS
    if last:
        out_shape = [jax.ShapeDtypeStruct((BLOCK, HEAD_DIM), jnp.bfloat16)] * len(work)
    else:
        out_shape = [jax.ShapeDtypeStruct((lines, HEAD_DIM), jnp.float32)] * 2
    scratch = [pltpu.VMEM((max(len(places) for _, _, _, places in work), 2 * ROWS, HEAD_DIM), jnp.bfloat16)]
    if last:
        scratch = [pltpu.VMEM((lines, HEAD_DIM), jnp.bfloat16), pltpu.VMEM((lines, HEAD_DIM), jnp.float32)] + scratch
    return pl.pallas_call(
        functools.partial(stage_kernel, work, first, last),
        out_shape=out_shape,
        in_specs=[VMEM] * len(operands),
        out_specs=[VMEM] * len(out_shape),
        scratch_shapes=scratch,
        compiler_params=params(32),
        cost_estimate=SMALL,
        name="stage",
    )(*operands)


def combine_kernel(z_ref, guide_ref, r0, r1, r2, r3, r4, fresh, keep, send):
    z, guide = z_ref[0], guide_ref[0]
    tile = HEAD_DIM
    todo = [(r, 0, lax.rem(z + s, SLOTS)) for s, r in enumerate((r0, r1, r2, r3))] + [(r4, 0, SLOTS)]

    def levels(ref, start):
        stat = ref[pl.ds(start, BLOCK - ROWS), :].astype(jnp.float32)
        level = stat[0:4, :] + stat[4:8, :] + stat[8:12, :]
        return [jnp.transpose(jnp.broadcast_to(level[i : i + 1, :], (tile, tile))) for i in range(ROWS // tile)]

    for came, row, head in todo:
        at = pl.multiple_of(head * BLOCK, BLOCK - ROWS)
        there = jnp.concatenate(levels(came, row + ROWS), axis=0)
        here = jnp.concatenate(levels(fresh, at + ROWS), axis=0)
        share = 1.0 / (1.0 + jnp.exp2(here - there))
        old = came[row : row + ROWS, :].astype(jnp.float32)
        new = fresh[pl.ds(at, ROWS), :].astype(jnp.float32)
        joined = (new + (old - new) * share).astype(jnp.bfloat16)
        for half in range(2):
            rows = joined[half * HALF : (half + 1) * HALF, :]
            for mine, target in ((True, keep), (False, send)):

                @pl.when((guide == half) == mine)
                def _(rows=rows, target=target, head=head):
                    target[head] = rows


def pick_kernel(near_ref, far_ref, weight, near, far, buffer, loaded, stored):
    width = weight.shape[0]
    loads, stores = [], []
    for i, (places, target) in enumerate(((far_ref, far), (near_ref, near))):
        for s in range(4):
            cols = pl.ds(pl.multiple_of(places[s] * width, width), width)
            at = 4 * i + s
            loads.append(pltpu.make_async_copy(weight.at[:, cols], buffer.at[at], loaded.at[at]))
            stores.append(pltpu.make_async_copy(buffer.at[at], target.at[s], stored.at[at]))
    for load in loads:
        load.start()
    for load, store in zip(loads, stores):
        load.wait()
        store.start()
    for store in stores:
        store.wait()


def project_kernel(guide_ref, own, other, far_own, far_other, weight, far_weight, out0, out1, out2, out3):
    first = guide_ref[0] == 0
    by_own = jnp.where(first, guide_scale, 1.0 - guide_scale)
    by_other = jnp.where(first, 1.0 - guide_scale, guide_scale)

    def mixed(own, other):
        heads = [own[h].astype(jnp.float32) * by_own + other[h].astype(jnp.float32) * by_other for h in range(own.shape[0])]
        return jnp.concatenate([head.astype(jnp.bfloat16) for head in heads], axis=1)

    mine, its = mixed(own, other), mixed(far_own, far_other)
    for s, out in ((1, out1), (2, out2), (3, out3), (0, out0)):
        share = jnp.dot(mine, weight[s], preferred_element_type=jnp.float32)
        share = share + jnp.dot(its, far_weight[s], preferred_element_type=jnp.float32)
        out[...] = share.astype(out.dtype)


def on_device(
    query,
    key_fresh,
    value_fresh,
    key_stale,
    value_stale,
    out_weight,
    stream,
    gate_table,
    step_index,
):
    rows, width = query.shape[1:]
    heads = width // HEAD_DIM
    half = rows // 2
    patch = lax.axis_index("patch")
    tensor = lax.axis_index("tensor")
    guide = lax.axis_index("guide")
    z = (patch % RING).astype(jnp.int32).reshape(1)
    guide_at = guide.astype(jnp.int32).reshape(1)

    def after(value, *others):
        return lax.optimization_barrier((value, *others))[0]

    sizes = [size * rows for size in (4, 5, 3, 5, 2, 2)]
    *messages, left0, left1 = pl.pallas_call(
        lay_out,
        out_shape=[jax.ShapeDtypeStruct((size, HEAD_DIM), jnp.bfloat16) for size in sizes],
        in_specs=[SMEM] + [ANY] * 3,
        out_specs=[ANY] * len(sizes),
        scratch_shapes=[
            pltpu.VMEM((3, rows, width), jnp.bfloat16),
            pltpu.SemaphoreType.DMA((3,)),
            pltpu.SemaphoreType.DMA((len(sizes),)),
        ]
        + [pltpu.VMEM((size, HEAD_DIM), jnp.bfloat16) for size in sizes],
        compiler_params=params(58),
        name="lay_out",
    )(z, query[0], key_stale[0], value_stale[0])

    stream_mine = lax.dynamic_slice_in_dim(stream[0], guide * half, half, 0)
    stream_sent = lax.dynamic_slice_in_dim(stream[0], (1 - guide) * half, half, 0)

    fresh_shape = jax.ShapeDtypeStruct((heads * BLOCK, HEAD_DIM), jnp.bfloat16)
    fresh = pl.pallas_call(
        fresh_kernel,
        out_shape=fresh_shape,
        in_specs=[VMEM] * 3,
        out_specs=VMEM,
        compiler_params=params(32),
        cost_estimate=SMALL,
        name="fresh",
    )(query[0], key_fresh[0], value_fresh[0])

    x, core = tensor // 2, tensor % 2
    chips = (x + jnp.arange(4, dtype=jnp.int32)) % 4
    near_places = (2 * chips + core).astype(jnp.int32)
    far_places = (2 * chips + 1 - core).astype(jnp.int32)
    blocks_shape = jax.ShapeDtypeStruct((4, width, width), jnp.bfloat16)
    weight_own, weight_sent = pl.pallas_call(
        pick_kernel,
        out_shape=[blocks_shape, blocks_shape],
        in_specs=[SMEM, SMEM, ANY],
        out_specs=[ANY, ANY],
        scratch_shapes=[
            pltpu.VMEM((8, width, width), jnp.bfloat16),
            pltpu.SemaphoreType.DMA((8,)),
            pltpu.SemaphoreType.DMA((8,)),
        ],
        compiler_params=params(48),
        cost_estimate=SMALL,
        name="pick",
    )(near_places, after(far_places, messages[ORDER[0]]), out_weight)

    def joined(pair, begin, count):
        return jnp.concatenate([arrived[slot][begin * rows : (begin + count) * rows] for slot in pair], axis=0)

    def work_on(queries, names, pair, own=None):
        work = []
        for slot, part in queries:
            places = []
            for name in names[part]:
                for i, other in enumerate(pair):
                    if not (name in (own, str((own, part))) and other == slot):
                        places.append((name, (4 * i + 2 * part if name in WHOLE else 2 * i) * rows))
            work.append((slot, part, QUERIES.index((slot, part)) * rows, tuple(places)))
        return tuple(work)

    arrived = {slot: to_slot(messages[slot], slot) for slot in PAIRS[0]}
    stream_other = other_guide(stream_sent)
    here, there, fresh, stream_other, weight_sent, *rest = lax.optimization_barrier(
        (*arrived.values(), fresh, stream_other, weight_sent, *(messages[slot] for slot in PAIRS[1]))
    )
    arrived = dict(zip(PAIRS[0], (here, there)))
    for slot, message in zip(PAIRS[1], rest):
        arrived[slot] = to_slot(message, slot)
    early = joined(PAIRS[0], 0, 4)
    early_y, early_core = other_y(early), other_core(early)
    early_y, early_core, a, b = lax.optimization_barrier((early_y, early_core, *(arrived[slot] for slot in PAIRS[1])))
    arrived.update(zip(PAIRS[1], (a, b)))
    arrays = {"early": early, "early_y": early_y, "early_core": early_core}
    own = joined(PAIRS[1], 0, 2)
    over = other_y(own)
    left0, left1 = to_slot(after(left0, a), PAIRS[1][0]), to_slot(after(left1, b), PAIRS[1][1])
    arrays["early_y_core"] = other_core(early_y)

    def named(part, *names):
        return [str((name, part)) for name in names]

    def both_parts(*names):
        return {part: named(part, *names) for part in range(2)}

    state = stage(work_on(QUERIES, [WHOLE[:3]] * 2, PAIRS[0], "early"), arrived, arrays, None)
    over, left0, left1, arrays["early_y_core"], *state = lax.optimization_barrier(
        (over, left0, left1, arrays["early_y_core"], *state)
    )
    last_own = jnp.concatenate([left0, left1], axis=0)
    core, last_core = other_core(own), other_core(last_own)
    over_core, last_over = other_core(over), other_y(last_own)
    state = stage(work_on(QUERIES, [WHOLE[3:]] * 2, PAIRS[0]), arrived, arrays, state)
    core, last_core, over_core, *state = lax.optimization_barrier((core, last_core, over_core, *state))
    parts = both_parts("own", "core")
    arrays.update(zip(parts[0] + parts[1], (own, core, last_own, last_core)))
    state = stage(work_on(QUERIES, parts, PAIRS[1], "own"), arrived, arrays, state)
    parts = both_parts("y", "y_core")
    arrays.update(zip(parts[0], (over, over_core)))
    came = {}
    outs = stage(work_on(QUERIES[:SLOTS], parts, PAIRS[1]), arrived, arrays, state, True)
    for (slot, _), out in zip(QUERIES, outs):
        came[slot] = from_slot(out, slot)
    last_over = after(last_over, outs[0])
    arrays.update(zip(parts[1], (last_over, other_core(last_over))))
    (out,) = stage(work_on(QUERIES[SLOTS:], parts, PAIRS[1]), arrived, arrays, state, True)
    came[SLOTS] = from_slot(out, 0)
    came = [came[slot] for slot in range(SLOTS + 1)]
    weight_other = other_core(weight_sent)

    att_shape = jax.ShapeDtypeStruct((heads, half, HEAD_DIM), jnp.bfloat16)
    keep, send = pl.pallas_call(
        combine_kernel,
        out_shape=[att_shape, att_shape],
        in_specs=[SMEM, SMEM] + [VMEM] * 6,
        out_specs=[VMEM] * 2,
        compiler_params=params(32),
        cost_estimate=SMALL,
        name="combine",
    )(z, guide_at, *came, fresh)
    other = other_guide(send)

    share = jax.ShapeDtypeStruct((half, width), jnp.float32)
    sent = jax.ShapeDtypeStruct((half, width), jnp.bfloat16)
    shares = pl.pallas_call(
        project_kernel,
        out_shape=[share, sent, sent, sent],
        in_specs=[SMEM] + [VMEM] * 6,
        out_specs=[VMEM] * 4,
        compiler_params=params(32),
        cost_estimate=SMALL,
        name="project",
    )(guide_at, keep, other, other_core(keep), other_core(other), weight_own, weight_other)
    term = shares[0]
    for s in range(1, 4):
        term = term + shift_x(shares[s], s).astype(jnp.float32)

    gate = lax.dynamic_index_in_dim(gate_table, step_index[0], 0, keepdims=False)
    near, far = stream_mine.astype(jnp.float32), stream_other.astype(jnp.float32)
    cond = jnp.where(guide == 0, near, far)
    uncond = jnp.where(guide == 0, far, near)
    guided = (uncond + guide_scale * (cond - uncond) + gate[None, :] * term).astype(jnp.bfloat16)
    own_cols = width // 2
    stays = lax.dynamic_slice_in_dim(guided, guide * own_cols, own_cols, 1)
    goes = lax.dynamic_slice_in_dim(guided, (1 - guide) * own_cols, own_cols, 1)
    got = other_guide(goes)
    return jnp.where(
        guide == 0, jnp.concatenate([stays, got], axis=0), jnp.concatenate([got, stays], axis=0)
    )


def solution(mesh):
    in_specs = (
        P("guide", "patch", "tensor"),
        P("guide", "patch", "tensor"),
        P("guide", "patch", "tensor"),
        P("guide", "patch", "tensor"),
        P("guide", "patch", "tensor"),
        P("tensor", None),
        P("guide", "patch", "tensor"),
        P(None, "tensor"),
        P(),
    )
    out_specs = P("patch", ("tensor", "guide"))
    return jax.shard_map(
        on_device, mesh=mesh, in_specs=in_specs, out_specs=out_specs, check_vma=False
    )
```

```python
import functools

import jax
import jax.numpy as jnp
from jax import lax
from jax.experimental import pallas as pl
from jax.experimental.pallas import tpu as pltpu
from jax.sharding import PartitionSpec as P

HEAD_DIM = 128
SLOTS = 4
RING = 8
ROWS = 512
HALF = ROWS // 2
BLOCK = ROWS + 16
SCALE2 = 1.4426950408889634 / HEAD_DIM**0.5
SAFE_SUM = 2.0**100
VMEM = pl.BlockSpec(memory_space=pltpu.VMEM)
SMEM = pl.BlockSpec(memory_space=pltpu.SMEM)
ANY = pl.BlockSpec(memory_space=pl.ANY)
PLACE = ("patch", "tensor")
PAIRS = ((1, 3), (0, 2))
ORDER = PAIRS[0] + PAIRS[1]
WHOLE = ("early_core", "early", "early_y", "early_y_core")
QUERIES = ((1, 0), (3, 0), (2, 0), (0, 0), (0, 1))
ROW_BY_ROW = (((1,), (1,)), ((), ()))
SMALL = pl.CostEstimate(flops=2**10, bytes_accessed=2**10, transcendentals=0)

guide_scale = 5.0


def params(mib):
    return pltpu.CompilerParams(vmem_limit_bytes=mib * 2**20)


def slot_pairs(slot, back):
    pairs = []
    for y in range(2):
        for z in range(RING):
            for x in range(4):
                for core in range(2):
                    there = SLOTS * core + (z + slot) % SLOTS
                    source = (y * RING + z) * 8 + x * 2 + core
                    target = (y * RING + there) * 8 + x * 2 + z // SLOTS
                    pairs.append((target, source) if back else (source, target))
    return pairs


def to_slot(value, slot):
    return lax.ppermute(value, PLACE, slot_pairs(slot, False))


def from_slot(value, slot):
    return lax.ppermute(value, PLACE, slot_pairs(slot, True))


def other_y(value):
    return lax.ppermute(value, "patch", [(i, (i + RING) % (2 * RING)) for i in range(2 * RING)])


def other_core(value):
    return lax.ppermute(value, "tensor", [(i, i ^ 1) for i in range(8)])


def other_guide(value):
    return lax.ppermute(value, "guide", [(0, 1), (1, 0)])


def shift_x(value, step):
    return lax.ppermute(value, "tensor", [(i, (i + 2 * step) % 8) for i in range(8)])


def query_row(slot, part):
    return ((4 if slot in PAIRS[0] else 2) + part) * ROWS


def scores(queries, keys):
    return lax.dot_general(queries, keys, ROW_BY_ROW, preferred_element_type=jnp.float32)


def lay_out(places, z_ref, query, key, value, *refs):
    count = len(places)
    messages, (held, loaded, stored, *buffers) = refs[:count], refs[count:]
    z = z_ref[0]
    loads = [pltpu.make_async_copy(src, held.at[i], loaded.at[i]) for i, src in enumerate((key, value, query))]
    for load in loads:
        load.start()
    for load in loads:
        load.wait()
    last = slice(SLOTS * HEAD_DIM, (SLOTS + 1) * HEAD_DIM)
    stores = []
    for i, at in enumerate(places):
        buffer = buffers[i]
        if at >= SLOTS:
            parts = [(0, last), (1, last)]
        else:
            head = pl.ds(pl.multiple_of(lax.rem(z + at, SLOTS) * HEAD_DIM, HEAD_DIM), HEAD_DIM)
            parts = [(0, head), (1, head)] + ([(0, last), (1, last)] if at in PAIRS[0] else []) + [(2, head)]
            if at == 0:
                parts.append((2, last))
        for n, (which, cols) in enumerate(parts):
            buffer[n * ROWS : (n + 1) * ROWS, :] = held[which, :, cols]
        stores.append(pltpu.make_async_copy(buffer, messages[i], stored.at[i]))
        stores[-1].start()
    for store in stores:
        store.wait()


def with_ones(values):
    return jnp.concatenate([values, jnp.ones(values.shape, values.dtype)], axis=1)


def write_block(target, row, attended, level_at):
    target[row : row + ROWS, :] = attended
    tile = HEAD_DIM
    lines = [jnp.transpose(level_at[i * tile : (i + 1) * tile, :])[0:1, :] for i in range(ROWS // tile)]
    level = jnp.concatenate(lines, axis=0)
    high = level.astype(jnp.bfloat16).astype(jnp.float32)
    rest = level - high
    middle = rest.astype(jnp.bfloat16).astype(jnp.float32)
    rows = jnp.concatenate([high, middle, rest - middle, jnp.zeros_like(level)], axis=0)
    target[row + ROWS : row + BLOCK, :] = rows.astype(jnp.bfloat16)


def fresh_kernel(query, key, value, out):
    for h in range(query.shape[1] // HEAD_DIM):
        cols = slice(h * HEAD_DIM, (h + 1) * HEAD_DIM)
        score = scores(query[:, cols], key[:, cols])
        peak = jnp.max(score, axis=1, keepdims=True) * SCALE2
        weights = jnp.exp2(score * SCALE2 - peak).astype(jnp.bfloat16)
        both = jnp.dot(weights, with_ones(value[:, cols]), preferred_element_type=jnp.float32)
        total = both[:, HEAD_DIM:]
        attended = (both[:, :HEAD_DIM] / total).astype(jnp.bfloat16)
        write_block(out, h * BLOCK, attended, peak + jnp.log2(total))


def stage_kernel(work, first, last, *refs):
    slots = sorted({slot for slot, _, _, _ in work})
    arrays_used = sorted({a for _, _, _, places in work for a, _ in places})
    messages, refs = dict(zip(slots, refs)), refs[len(slots) :]
    arrays, refs = dict(zip(arrays_used, refs)), refs[len(arrays_used) :]
    if not first:
        (summed_in, stat_in), refs = refs[:2], refs[2:]
    if last:
        outs, (attended, level_at, held) = refs[: len(work)], refs[len(work) :]
    else:
        summed_out, stat_out, held = refs
    middle = HEAD_DIM // 2
    lane = lax.broadcasted_iota(jnp.int32, (HALF, HEAD_DIM), 1)

    def before(row, begin):
        span = pl.ds(row + begin, HALF)
        stat = stat_in[span, :]
        total = jnp.broadcast_to(stat[:, 0:1], stat.shape)
        return jnp.concatenate([summed_in[span, :], total], axis=1), stat[:, middle : middle + 1]

    def finish(row, n, begin, both, peak):
        total = both[:, HEAD_DIM:]
        if last:
            span = pl.ds(n * ROWS + begin, HALF)
            attended[span, :] = (both[:, :HEAD_DIM] / total).astype(jnp.bfloat16)
            level_at[span, :] = peak + jnp.log2(total)
        else:
            span = pl.ds(row + begin, HALF)
            summed_out[span, :] = both[:, :HEAD_DIM]
            stat_out[span, :] = jnp.where(lane < middle, total, peak)

    largest = None
    for n, (slot, part, row, places) in enumerate(work):
        for begin in (0, HALF):
            queries = messages[slot][query_row(slot, part) + begin : query_row(slot, part) + begin + HALF, :]
            both, peak = (None, None) if first else before(row, begin)
            for a, base in places:
                score = scores(queries, arrays[a][base : base + ROWS, :])
                if peak is None:
                    peak = jnp.max(score, axis=1, keepdims=True) * SCALE2
                weights = jnp.exp2(score * SCALE2 - peak).astype(jnp.bfloat16)
                values = arrays[a][base + ROWS : base + 2 * ROWS, :]
                more = jnp.dot(weights, with_ones(values), preferred_element_type=jnp.float32)
                both = more if both is None else both + more
            finish(row, n, begin, both, peak)
            largest = both[:, HEAD_DIM:] if largest is None else jnp.maximum(largest, both[:, HEAD_DIM:])

    @pl.when(jnp.logical_not(jnp.max(largest) < SAFE_SUM))
    def _():
        for n, (slot, part, row, places) in enumerate(work):
            for at, (a, base) in enumerate(places):
                held[at] = arrays[a][base : base + 2 * ROWS, :]

            def chunk_step(c, carry, n=n, slot=slot, part=part, row=row, count=len(places)):
                begin = pl.multiple_of(c * HALF, HALF)
                queries = messages[slot][pl.ds(query_row(slot, part) + begin, HALF), :]

                def follow(at, state):
                    both, peak = state
                    score = scores(queries, held[at, :ROWS, :]) * SCALE2
                    higher = jnp.maximum(peak, jnp.max(score, axis=1, keepdims=True))
                    weights = jnp.exp2(score - higher).astype(jnp.bfloat16)
                    more = jnp.dot(weights, with_ones(held[at, ROWS:, :]), preferred_element_type=jnp.float32)
                    return both * jnp.exp2(peak - higher) + more, higher

                if first:
                    start = (jnp.zeros((HALF, 2 * HEAD_DIM), jnp.float32), jnp.full((HALF, 1), -1e30, jnp.float32))
                else:
                    start = before(row, begin)
                finish(row, n, begin, *lax.fori_loop(0, count, follow, start))
                return carry

            lax.fori_loop(0, 2, chunk_step, 0)

    if last:
        for n, out in enumerate(outs):
            here = slice(n * ROWS, (n + 1) * ROWS)
            write_block(out, 0, attended[here, :], level_at.at[n * ROWS : (n + 1) * ROWS, :])


def stage(work, messages, arrays, state, last=False):
    first = state is None
    slots = sorted({slot for slot, _, _, _ in work})
    arrays_used = sorted({a for _, _, _, places in work for a, _ in places})
    operands = [messages[s] for s in slots] + [arrays[a] for a in arrays_used] + ([] if first else list(state))
    lines = len(work) * ROWS
    if last:
        out_shape = [jax.ShapeDtypeStruct((BLOCK, HEAD_DIM), jnp.bfloat16)] * len(work)
    else:
        out_shape = [jax.ShapeDtypeStruct((lines, HEAD_DIM), jnp.float32)] * 2
    scratch = [pltpu.VMEM((max(len(places) for _, _, _, places in work), 2 * ROWS, HEAD_DIM), jnp.bfloat16)]
    if last:
        scratch = [pltpu.VMEM((lines, HEAD_DIM), jnp.bfloat16), pltpu.VMEM((lines, HEAD_DIM), jnp.float32)] + scratch
    return pl.pallas_call(
        functools.partial(stage_kernel, work, first, last),
        out_shape=out_shape,
        in_specs=[VMEM] * len(operands),
        out_specs=[VMEM] * len(out_shape),
        scratch_shapes=scratch,
        compiler_params=params(32),
        cost_estimate=SMALL,
        name="stage",
    )(*operands)


def combine_kernel(z_ref, guide_ref, r0, r1, r2, r3, r4, fresh, keep, send):
    z, guide = z_ref[0], guide_ref[0]
    tile = HEAD_DIM
    todo = [(r, 0, lax.rem(z + s, SLOTS)) for s, r in enumerate((r0, r1, r2, r3))] + [(r4, 0, SLOTS)]

    def levels(ref, start):
        stat = ref[pl.ds(start, BLOCK - ROWS), :].astype(jnp.float32)
        level = stat[0:4, :] + stat[4:8, :] + stat[8:12, :]
        return [jnp.transpose(jnp.broadcast_to(level[i : i + 1, :], (tile, tile))) for i in range(ROWS // tile)]

    for came, row, head in todo:
        at = pl.multiple_of(head * BLOCK, BLOCK - ROWS)
        there = jnp.concatenate(levels(came, row + ROWS), axis=0)
        here = jnp.concatenate(levels(fresh, at + ROWS), axis=0)
        share = 1.0 / (1.0 + jnp.exp2(here - there))
        old = came[row : row + ROWS, :].astype(jnp.float32)
        new = fresh[pl.ds(at, ROWS), :].astype(jnp.float32)
        joined = (new + (old - new) * share).astype(jnp.bfloat16)
        for half in range(2):
            rows = joined[half * HALF : (half + 1) * HALF, :]
            for mine, target in ((True, keep), (False, send)):

                @pl.when((guide == half) == mine)
                def _(rows=rows, target=target, head=head):
                    target[head] = rows


def pick_kernel(near_ref, far_ref, weight, near, far, buffer, loaded, stored):
    width = weight.shape[0]
    loads, stores = [], []
    for i, (places, target) in enumerate(((far_ref, far), (near_ref, near))):
        for s in range(4):
            cols = pl.ds(pl.multiple_of(places[s] * width, width), width)
            at = 4 * i + s
            loads.append(pltpu.make_async_copy(weight.at[:, cols], buffer.at[at], loaded.at[at]))
            stores.append(pltpu.make_async_copy(buffer.at[at], target.at[s], stored.at[at]))
    for load in loads:
        load.start()
    for load, store in zip(loads, stores):
        load.wait()
        store.start()
    for store in stores:
        store.wait()


def project_kernel(guide_ref, own, other, far_own, far_other, weight, far_weight, out0, out1, out2, out3):
    first = guide_ref[0] == 0
    by_own = jnp.where(first, guide_scale, 1.0 - guide_scale)
    by_other = jnp.where(first, 1.0 - guide_scale, guide_scale)

    def mixed(own, other):
        heads = [own[h].astype(jnp.float32) * by_own + other[h].astype(jnp.float32) * by_other for h in range(own.shape[0])]
        return jnp.concatenate([head.astype(jnp.bfloat16) for head in heads], axis=1)

    mine, its = mixed(own, other), mixed(far_own, far_other)
    for s, out in ((1, out1), (2, out2), (3, out3), (0, out0)):
        share = jnp.dot(mine, weight[s], preferred_element_type=jnp.float32)
        share = share + jnp.dot(its, far_weight[s], preferred_element_type=jnp.float32)
        out[...] = share.astype(out.dtype)


def on_device(
    query,
    key_fresh,
    value_fresh,
    key_stale,
    value_stale,
    out_weight,
    stream,
    gate_table,
    step_index,
):
    rows, width = query.shape[1:]
    heads = width // HEAD_DIM
    half = rows // 2
    patch = lax.axis_index("patch")
    tensor = lax.axis_index("tensor")
    guide = lax.axis_index("guide")
    z = (patch % RING).astype(jnp.int32).reshape(1)
    guide_at = guide.astype(jnp.int32).reshape(1)

    def after(value, *others):
        return lax.optimization_barrier((value, *others))[0]

    sizes = [size * rows for size in (4, 5, 3, 5, 2, 2)]
    messages = [None] * len(sizes)
    for places in (PAIRS[0], PAIRS[1] + (SLOTS, SLOTS + 1)):
        laid = pl.pallas_call(
            functools.partial(lay_out, places),
            out_shape=[jax.ShapeDtypeStruct((sizes[at], HEAD_DIM), jnp.bfloat16) for at in places],
            in_specs=[SMEM] + [ANY] * 3,
            out_specs=[ANY] * len(places),
            scratch_shapes=[
                pltpu.VMEM((3, rows, width), jnp.bfloat16),
                pltpu.SemaphoreType.DMA((3,)),
                pltpu.SemaphoreType.DMA((len(places),)),
            ]
            + [pltpu.VMEM((sizes[at], HEAD_DIM), jnp.bfloat16) for at in places],
            compiler_params=params(58),
            cost_estimate=SMALL,
            name="lay_out",
        )(z, query[0], key_stale[0], value_stale[0])
        for at, message in zip(places, laid):
            messages[at] = message
    left0, left1 = messages[SLOTS:]

    stream_mine = lax.dynamic_slice_in_dim(stream[0], guide * half, half, 0)
    stream_sent = lax.dynamic_slice_in_dim(stream[0], (1 - guide) * half, half, 0)

    fresh_shape = jax.ShapeDtypeStruct((heads * BLOCK, HEAD_DIM), jnp.bfloat16)
    fresh = pl.pallas_call(
        fresh_kernel,
        out_shape=fresh_shape,
        in_specs=[VMEM] * 3,
        out_specs=VMEM,
        compiler_params=params(32),
        cost_estimate=SMALL,
        name="fresh",
    )(query[0], key_fresh[0], value_fresh[0])

    x, core = tensor // 2, tensor % 2
    chips = (x + jnp.arange(4, dtype=jnp.int32)) % 4
    near_places = (2 * chips + core).astype(jnp.int32)
    far_places = (2 * chips + 1 - core).astype(jnp.int32)
    blocks_shape = jax.ShapeDtypeStruct((4, width, width), jnp.bfloat16)
    weight_own, weight_sent = pl.pallas_call(
        pick_kernel,
        out_shape=[blocks_shape, blocks_shape],
        in_specs=[SMEM, SMEM, ANY],
        out_specs=[ANY, ANY],
        scratch_shapes=[
            pltpu.VMEM((8, width, width), jnp.bfloat16),
            pltpu.SemaphoreType.DMA((8,)),
            pltpu.SemaphoreType.DMA((8,)),
        ],
        compiler_params=params(48),
        cost_estimate=SMALL,
        name="pick",
    )(near_places, after(far_places, messages[ORDER[0]]), out_weight)

    def joined(pair, begin, count):
        return jnp.concatenate([arrived[slot][begin * rows : (begin + count) * rows] for slot in pair], axis=0)

    def work_on(queries, names, pair, own=None):
        work = []
        for slot, part in queries:
            places = []
            for name in names[part]:
                for i, other in enumerate(pair):
                    if not (name in (own, str((own, part))) and other == slot):
                        places.append((name, (4 * i + 2 * part if name in WHOLE else 2 * i) * rows))
            work.append((slot, part, QUERIES.index((slot, part)) * rows, tuple(places)))
        return tuple(work)

    arrived = {slot: to_slot(messages[slot], slot) for slot in PAIRS[0]}
    stream_other = other_guide(stream_sent)
    here, there, fresh, stream_other, weight_sent, *rest = lax.optimization_barrier(
        (*arrived.values(), fresh, stream_other, weight_sent, *(messages[slot] for slot in PAIRS[1]))
    )
    arrived = dict(zip(PAIRS[0], (here, there)))
    for slot, message in zip(PAIRS[1], rest):
        arrived[slot] = to_slot(message, slot)
    early = joined(PAIRS[0], 0, 4)
    early_y, early_core = other_y(early), other_core(early)
    early_y, early_core, a, b = lax.optimization_barrier((early_y, early_core, *(arrived[slot] for slot in PAIRS[1])))
    arrived.update(zip(PAIRS[1], (a, b)))
    arrays = {"early": early, "early_y": early_y, "early_core": early_core}
    own = joined(PAIRS[1], 0, 2)
    over = other_y(own)
    left0, left1 = to_slot(after(left0, a), PAIRS[1][0]), to_slot(after(left1, b), PAIRS[1][1])
    arrays["early_y_core"] = other_core(early_y)

    def named(part, *names):
        return [str((name, part)) for name in names]

    def both_parts(*names):
        return {part: named(part, *names) for part in range(2)}

    state = stage(work_on(QUERIES, [WHOLE[:3]] * 2, PAIRS[0], "early"), arrived, arrays, None)
    over, left0, left1, arrays["early_y_core"], *state = lax.optimization_barrier(
        (over, left0, left1, arrays["early_y_core"], *state)
    )
    last_own = jnp.concatenate([left0, left1], axis=0)
    core, last_core = other_core(own), other_core(last_own)
    over_core, last_over = other_core(over), other_y(last_own)
    state = stage(work_on(QUERIES, [WHOLE[3:]] * 2, PAIRS[0]), arrived, arrays, state)
    core, last_core, over_core, *state = lax.optimization_barrier((core, last_core, over_core, *state))
    parts = both_parts("own", "core")
    arrays.update(zip(parts[0] + parts[1], (own, core, last_own, last_core)))
    state = stage(work_on(QUERIES, parts, PAIRS[1], "own"), arrived, arrays, state)
    parts = both_parts("y", "y_core")
    arrays.update(zip(parts[0], (over, over_core)))
    came = {}
    outs = stage(work_on(QUERIES[:SLOTS], parts, PAIRS[1]), arrived, arrays, state, True)
    for (slot, _), out in zip(QUERIES, outs):
        came[slot] = from_slot(out, slot)
    last_over = after(last_over, outs[0])
    arrays.update(zip(parts[1], (last_over, other_core(last_over))))
    (out,) = stage(work_on(QUERIES[SLOTS:], parts, PAIRS[1]), arrived, arrays, state, True)
    came[SLOTS] = from_slot(out, 0)
    came = [came[slot] for slot in range(SLOTS + 1)]
    weight_other = other_core(weight_sent)

    att_shape = jax.ShapeDtypeStruct((heads, half, HEAD_DIM), jnp.bfloat16)
    keep, send = pl.pallas_call(
        combine_kernel,
        out_shape=[att_shape, att_shape],
        in_specs=[SMEM, SMEM] + [VMEM] * 6,
        out_specs=[VMEM] * 2,
        compiler_params=params(32),
        cost_estimate=SMALL,
        name="combine",
    )(z, guide_at, *came, fresh)
    other = other_guide(send)

    share = jax.ShapeDtypeStruct((half, width), jnp.float32)
    sent = jax.ShapeDtypeStruct((half, width), jnp.bfloat16)
    shares = pl.pallas_call(
        project_kernel,
        out_shape=[share, sent, sent, sent],
        in_specs=[SMEM] + [VMEM] * 6,
        out_specs=[VMEM] * 4,
        compiler_params=params(32),
        cost_estimate=SMALL,
        name="project",
    )(guide_at, keep, other, other_core(keep), other_core(other), weight_own, weight_other)
    term = shares[0]
    for s in range(1, 4):
        term = term + shift_x(shares[s], s).astype(jnp.float32)

    gate = lax.dynamic_index_in_dim(gate_table, step_index[0], 0, keepdims=False)
    near, far = stream_mine.astype(jnp.float32), stream_other.astype(jnp.float32)
    cond = jnp.where(guide == 0, near, far)
    uncond = jnp.where(guide == 0, far, near)
    guided = (uncond + guide_scale * (cond - uncond) + gate[None, :] * term).astype(jnp.bfloat16)
    own_cols = width // 2
    stays = lax.dynamic_slice_in_dim(guided, guide * own_cols, own_cols, 1)
    goes = lax.dynamic_slice_in_dim(guided, (1 - guide) * own_cols, own_cols, 1)
    got = other_guide(goes)
    return jnp.where(
        guide == 0, jnp.concatenate([stays, got], axis=0), jnp.concatenate([got, stays], axis=0)
    )


def solution(mesh):
    in_specs = (
        P("guide", "patch", "tensor"),
        P("guide", "patch", "tensor"),
        P("guide", "patch", "tensor"),
        P("guide", "patch", "tensor"),
        P("guide", "patch", "tensor"),
        P("tensor", None),
        P("guide", "patch", "tensor"),
        P(None, "tensor"),
        P(),
    )
    out_specs = P("patch", ("tensor", "guide"))
    return jax.shard_map(
        on_device, mesh=mesh, in_specs=in_specs, out_specs=out_specs, check_vma=False
    )
```
